256 devices in a mesh: leaf: 256 (over z, x, y, core).
Axes of the slice: x: 4, y: 4, z: 8, core: 2. Of those that a mesh axis runs over, the one named last changes fastest.
Arguments:
- trial_vectors: bfloat16 [8192, 32, 128], P('leaf'), may hold values from -6 to 6
- leaf_basis: bfloat16 [8192, 32, 128], P('leaf'), may hold values from -0.5 to 0.5
- near_blocks: bfloat16 [8192, 8, 128, 128], P('leaf'), may hold values from -0.1875 to 0.1875
- near_src: int32 [8192, 8], P('leaf'), may hold values from 0 to 8191, as said below
- near_count: int32 [8192], P('leaf'), may hold values from 1 to 8
- couple_src: int32 [8192, 8], P('leaf'), may hold values from 0 to 8191, as said below
- couple_count: int32 [8192], P('leaf'), may hold values from 1 to 8
- couple_leaf: bfloat16 [8192, 8, 1024], P('leaf'), may hold values from -0.375 to 0.375
- transfer: bfloat16 [8192, 2, 1024], P('leaf'), may hold values from -0.875 to 0.875
- couple_upper: bfloat16 [8192, 3, 1024], P('leaf'), may hold values from -0.625 to 0.625
Outputs:
- applied: float32 [8192, 32, 128], P('leaf')
The draws below stay inside these ranges and needn't reach their ends.
Inputs may be any that keep to these rules, and one draw needn't show every extreme that they name: near_src[i, k] is a leaf at most 32 leaves from leaf i; slots from near_count[i] on are ignored. couple_src[i, k] is a leaf at most 32 leaves from leaf i; slots from couple_count[i] on are ignored.
All inputs are finite; a program needn't handle non-finite values.
Results may differ from the reference program's by a relative error of at most 0.003.
Values may be sent and summed in bfloat16 or wider, within the bound.
No kernel may reach another device: no remote copies, remote signals or barrier semaphores. Data moves between devices by JAX's collectives and lax.ppermute only.
A program may use at most 192 MiB of HBM per device.

```python
import jax
import jax.numpy as jnp
import numpy as np
from jax import lax

P_SIZE = 128
R = 32
NV = 32
KN = 8
KC = 8
LEAF_DEV = 32
LEAVES = 8192


def near_list(key, slots):
    leaf_ids = jnp.arange(LEAVES, dtype=jnp.int32)[:, None]
    offsets = jax.random.randint(key, (LEAVES, slots), -LEAF_DEV, LEAF_DEV + 1)
    chosen = jnp.clip(leaf_ids + offsets, 0, LEAVES - 1)
    chosen = chosen.at[0, 0].set(0).at[LEAVES - 1, 0].set(LEAVES - 1)
    return chosen.astype(jnp.int32)


def draw_near_src(key, part):
    key = jax.random.fold_in(key, 11)
    return near_list(key, KN)


def draw_couple_src(key, part):
    key = jax.random.fold_in(key, 13)
    return near_list(key, KC)


def draw_near_count(key, part):
    key = jax.random.fold_in(key, 17)
    first_key, second_key = jax.random.split(key)
    groups = LEAVES // LEAF_DEV
    heavy = jax.random.randint(first_key, (groups,), 1, KN + 1)
    spread = jnp.repeat(heavy, LEAF_DEV)
    raw_draw = jax.random.randint(second_key, (LEAVES,), 0, 65536)
    counts = 1 + raw_draw % spread
    counts = counts.at[0].set(KN).at[1].set(1)
    return counts.astype(jnp.int32)


def draw_couple_count(key, part):
    key = jax.random.fold_in(key, 19)
    counts = jax.random.randint(key, (LEAVES,), 1, KC + 1)
    counts = counts.at[0].set(KC).at[1].set(1)
    return counts.astype(jnp.int32)


def block_levels(own_key, shape, pieces, smallest, high):
    factor_of, own = 1.0, jax.random.fold_in(own_key, 6)
    for axis_at, parts in pieces:
        steps = jnp.exp(jax.random.uniform(jax.random.fold_in(own, axis_at), (parts,), jnp.float32, smallest / len(pieces), high / len(pieces)))
        factor_of = factor_of * jnp.repeat(steps, shape[axis_at] // parts).reshape([-1 if axis == axis_at else 1 for axis in range(len(shape))])
    return factor_of


def gaussian(own_key, shape, width, reach, shards=(), kind=jnp.bfloat16):
    drawn = jax.random.normal(own_key, shape, jnp.float32) * width
    if len(shards) > 0:
        drawn = block_levels(own_key, shape, shards, -0.22, 0.18) * drawn
    return jnp.clip(drawn, min=-reach, max=reach).astype(kind)


def setup_inputs(seed: int = 0) -> dict:
    splits = jax.random.split(jax.random.key(seed), 11)
    return {
        "trial_vectors": gaussian(splits[0], (LEAVES, NV, P_SIZE), 1.0, 6.0, ((0, 256),)),
        "leaf_basis": gaussian(splits[1], (LEAVES, R, P_SIZE), P_SIZE ** -0.5, 0.5, ((0, 256),)),
        "near_blocks": gaussian(splits[2], (LEAVES, KN, P_SIZE, P_SIZE), (KN * P_SIZE) ** -0.5, 0.1875, ((0, 256),)),
        "near_src": draw_near_src(jax.random.fold_in(splits[10], 71), 0),
        "near_count": draw_near_count(jax.random.fold_in(splits[10], 71), 0),
        "couple_src": draw_couple_src(jax.random.fold_in(splits[10], 71), 0),
        "couple_count": draw_couple_count(jax.random.fold_in(splits[10], 71), 0),
        "couple_leaf": gaussian(splits[7], (LEAVES, KC, R * R), (KC * R) ** -0.5, 0.375, ((0, 256),)),
        "transfer": gaussian(splits[8], (LEAVES, 2, R * R), (3 * R // 2) ** -0.5, 0.875, ((0, 256),)),
        "couple_upper": gaussian(splits[9], (LEAVES, 3, R * R), (3 * R) ** -0.5, 0.625, ((0, 256),)),
    }


highest = lax.Precision.HIGHEST


def mixed(form, left_op, right_op):
    return jnp.einsum(form, left_op, right_op, precision=highest)


def reference(trial_vectors, leaf_basis, near_blocks, near_src, near_count, couple_src, couple_count, couple_leaf, transfer, couple_upper):
    depth = LEAVES.bit_length() - 1
    basis_wide = leaf_basis.astype(jnp.float32)
    leaf_coef = mixed('lvp,lrp->lvr', trial_vectors.astype(jnp.float32), basis_wide)
    coefs = [leaf_coef]
    for l in range(1, depth + 1):
        nodes = LEAVES >> l
        inorder = np.arange(nodes) * 2 ** l + 2 ** (l - 1) - 1
        joined = transfer[inorder].astype(jnp.float32).reshape(nodes, 2, R, R)
        child_coef = coefs[-1].reshape(nodes, 2, NV, R)
        coefs.append(mixed('mcvr,mcrs->mvs', child_coef, joined))
    couple_zero = jnp.zeros((LEAVES, NV, R), jnp.float32)
    for k in range(KC):
        live = (k < couple_count).astype(jnp.float32)[:, None, None]
        picked = leaf_coef[couple_src[:, k]] * live
        matrices = couple_leaf[:, k].astype(jnp.float32).reshape(LEAVES, R, R)
        couple_zero = couple_zero + mixed('lvr,lrs->lvs', picked, matrices)
    couples = [couple_zero]
    for l in range(1, depth + 1):
        nodes = LEAVES >> l
        inorder = np.arange(nodes) * 2 ** l + 2 ** (l - 1) - 1
        node_index = np.arange(nodes)
        offsets = np.where((node_index % 2 == 0)[:, None], np.array([-2, 2, 3]), np.array([-3, -2, 2]))
        sources = node_index[:, None] + offsets
        valid = jnp.asarray(((sources >= 0) & (sources < nodes)).astype(np.float32))
        clipped = np.clip(sources, 0, nodes - 1)
        matrices = couple_upper[inorder].astype(jnp.float32).reshape(nodes, 3, R, R)
        picked = coefs[l][clipped] * valid[:, :, None, None]
        couples.append(mixed('mkvr,mkrs->mvs', picked, matrices))
    downward = couples[depth]
    for l in range(depth, 0, -1):
        nodes = LEAVES >> l
        inorder = np.arange(nodes) * 2 ** l + 2 ** (l - 1) - 1
        joined = transfer[inorder].astype(jnp.float32).reshape(nodes, 2, R, R)
        message = mixed('mvs,mcrs->mcvr', downward, joined).reshape(2 * nodes, NV, R)
        downward = couples[l - 1] + message
    rounded = lax.optimization_barrier(downward.astype(jnp.bfloat16)).astype(jnp.float32)
    result = mixed('lvr,lrp->lvp', rounded, basis_wide)
    for k in range(KN):
        live = (k < near_count).astype(jnp.float32)[:, None, None]
        picked = trial_vectors[near_src[:, k]].astype(jnp.float32) * live
        result = result + mixed('lvq,lqp->lvp', picked, near_blocks[:, k].astype(jnp.float32))
    return result
```

```python
import functools

import jax
import jax.numpy as jnp
import numpy as np
from jax import lax
from jax.experimental import pallas as pl
from jax.experimental.pallas import tpu as pltpu
from jax.sharding import PartitionSpec as P

F32, BF16 = jnp.float32, jnp.bfloat16
NT = (((1,), (1,)), ((), ()))
LANES = 128
R = 32
SPAN = 32
GROUP = 16
ROWS = 80
VMEM_LIMIT = 48 * 1024 * 1024


def rep_matrix(slots, stride, rows):
    made = np.zeros((slots * R, rows), np.float32)
    for slot in range(slots):
        for r in range(R):
            if slot < stride:
                made[slot * R + r, (r // 4) * stride + slot] = 1
    return made


REP_TRANSFER = rep_matrix(2, 2, 16)
REP_UPPER = rep_matrix(4, 4, 32)
REP_UPPER[96:] = 0
REP_LEAF = rep_matrix(8, 8, 64)


def lane_block(shape):
    return lax.broadcasted_iota(jnp.int32, shape, 1) >> 5


def spread(rep, rows):
    wide = jnp.dot(rep, rows, preferred_element_type=F32)
    at = lax.broadcasted_iota(jnp.int32, wide.shape, 0) & 3
    return jnp.where(lane_block(wide.shape) == at, wide, 0.0).astype(BF16)


def fold(x):
    x = x + pltpu.roll(x, 32, 1)
    return x + pltpu.roll(x, 64, 1)


def split(x):
    high = x.astype(BF16)
    return jnp.concatenate([high, (x - high.astype(F32)).astype(BF16)], axis=0)


def wide_dot(x, mats):
    y = jnp.dot(split(x), mats, preferred_element_type=F32)
    return y[:R] + y[R:]


def pack(x):
    high = x.astype(BF16).astype(F32)
    return jnp.where(lane_block(x.shape) == 0, high, x - high).astype(BF16)


def unpack(x):
    x = x.astype(F32)
    return fold(jnp.where(lane_block(x.shape) == 0, x + pltpu.roll(x, 96, 1), 0.0))


def join_up(left, right, mats):
    both = jnp.where(lane_block(left.shape) == 0, left, right)[:, : 2 * R]
    return fold(wide_dot(both, mats))


def pass_down(down, mats):
    wide = jnp.concatenate([mats, mats], axis=0)
    y = lax.dot_general(split(down), wide, NT, preferred_element_type=F32)
    y = y[:R] + y[R:]
    z = pltpu.roll(y, 32, 1)
    even = (lane_block(y.shape) & 1) == 0
    return jnp.where(even, y, z), jnp.where(even, z, y)


def couple(first, second, third, mats):
    at = lane_block(first.shape)
    return fold(wide_dot(jnp.where(at == 0, first, jnp.where(at == 1, second, third)), mats))


def upper_rows(upper_ref, node, room_ref):
    for i in range(8):
        room_ref[pl.ds(4 * i, 3), :] = upper_ref[node, :, LANES * i : LANES * (i + 1)].astype(F32)
    return room_ref[...].astype(BF16)


def kernel_params():
    return pltpu.CompilerParams(vmem_limit_bytes=VMEM_LIMIT)


def local_up_kernel(
    trial, basis, transfer, upper, rep_transfer, send, own, to_right, to_left, base_upper, tree, room
):
    room[...] = jnp.zeros_like(room)
    for n in range(SPAN):
        b = basis[n]
        tree[n] = lax.dot_general(
            trial[n], jnp.concatenate([b, b, b, b], axis=0), NT, preferred_element_type=F32
        )
    base = [0]
    for l in range(1, 6):
        base.append(base[-1] + (SPAN >> (l - 1)))
        for j in range(SPAN >> l):
            mats = spread(rep_transfer[...], transfer[j * 2**l + 2 ** (l - 1) - 1])
            child = base[l - 1] + 2 * j
            tree[base[l] + j] = join_up(tree[child], tree[child + 1], mats)
    head = jnp.concatenate(
        [pack(tree[62]), transfer[SPAN - 1], upper_rows(upper, SPAN - 1, room)], axis=0
    )
    for g in range(GROUP):
        send[g] = head
    base_upper[...] = upper_rows(upper, SPAN // 2 - 1, room)
    for n in range(62):
        own[n] = pack(tree[n])
    for out, ends in ((to_right, True), (to_left, False)):
        for n in range(SPAN):
            out[n] = trial[n]
            out[SPAN + n] = own[n]
        cursor = 2 * SPAN
        for l in range(1, 5):
            nodes = SPAN >> l
            keep = min(nodes, 3)
            for k in range(keep):
                out[cursor + k] = own[base[l] + (nodes - keep if ends else 0) + k]
            cursor += keep


def local_up(trial, basis, transfer, upper):
    block = (R, LANES)
    return pl.pallas_call(
        local_up_kernel,
        out_shape=[
            jax.ShapeDtypeStruct((GROUP, ROWS, LANES), BF16),
            jax.ShapeDtypeStruct((62, *block), BF16),
            jax.ShapeDtypeStruct((75, *block), BF16),
            jax.ShapeDtypeStruct((75, *block), BF16),
            jax.ShapeDtypeStruct(block, BF16),
        ],
        scratch_shapes=[pltpu.VMEM((63, *block), F32), pltpu.VMEM(block, F32)],
        compiler_params=kernel_params(),
        name="local_up",
    )(trial, basis, transfer, upper, jnp.asarray(REP_TRANSFER, BF16))


def group_up_kernel(got, rep_transfer, send, inside, to_right, to_left, tree):
    for e in range(GROUP):
        tree[e] = unpack(got[e, :R])
    base = [0]
    for g in range(1, 5):
        base.append(base[-1] + (GROUP >> (g - 1)))
        for j in range(GROUP >> g):
            owner = (2 * j + 1) * 2 ** (g - 1) - 1
            mats = spread(rep_transfer[...], got[owner, R : R + 16])
            child = base[g - 1] + 2 * j
            tree[base[g] + j] = join_up(tree[child], tree[child + 1], mats)
    for n in range(31):
        inside[n] = pack(tree[n])
    head = jnp.concatenate([inside[30], got[GROUP - 1, R:]], axis=0)
    for g in range(GROUP):
        send[g] = head
    cursor = 0
    for g in range(4):
        nodes = GROUP >> g
        keep = min(nodes, 3)
        for k in range(keep):
            to_right[cursor + k] = inside[base[g] + nodes - keep + k]
            to_left[cursor + k] = inside[base[g] + k]
        cursor += keep


def group_up(got):
    block = (R, LANES)
    return pl.pallas_call(
        group_up_kernel,
        out_shape=[
            jax.ShapeDtypeStruct((GROUP, ROWS, LANES), BF16),
            jax.ShapeDtypeStruct((31, *block), BF16),
            jax.ShapeDtypeStruct((11, *block), BF16),
            jax.ShapeDtypeStruct((11, *block), BF16),
        ],
        scratch_shapes=[pltpu.VMEM((31, *block), F32)],
        compiler_params=kernel_params(),
        name="group_up",
    )(got, jnp.asarray(REP_TRANSFER, BF16))


def source_row(src, count, row, slot, first):
    near = src[row, slot] - first
    near = jnp.minimum(jnp.maximum(near, 0), 3 * SPAN - 1)
    return jnp.where(slot < count[row], near, 3 * SPAN)


STEP = 4


def near_kernel(src, count, trial, left, right, blocks, out, held, sems):
    step = pl.program_id(0)
    first = (lax.axis_index("leaf") - 1) * SPAN

    @pl.when(step == 0)
    def _():
        copies = [
            pltpu.make_async_copy(ref.at[pl.ds(0, SPAN)], held.at[pl.ds(k * SPAN, SPAN)], sems.at[k])
            for k, ref in enumerate((left, trial, right))
        ]
        for copy in copies:
            copy.start()
        held[3 * SPAN] = jnp.zeros((R, LANES), BF16)
        for copy in copies:
            copy.wait()

    for n in range(STEP):
        row = step * STEP + n
        picked = [held[source_row(src, count, row, k, first)] for k in range(8)]
        out[n] = jnp.dot(
            jnp.concatenate(picked, axis=1),
            blocks[n].reshape(8 * LANES, LANES),
            preferred_element_type=F32,
        )


def near_field(src, count, trial, left, right, blocks):
    smem = pl.BlockSpec(memory_space=pltpu.SMEM)
    hbm = pl.BlockSpec(memory_space=pl.ANY)
    return pl.pallas_call(
        near_kernel,
        grid=(SPAN // STEP,),
        in_specs=[smem, smem, hbm, hbm, hbm, pl.BlockSpec((STEP, 8, LANES, LANES), lambda i: (i, 0, 0, 0))],
        out_specs=pl.BlockSpec((STEP, R, LANES), lambda i: (i, 0, 0)),
        out_shape=jax.ShapeDtypeStruct((SPAN, R, LANES), F32),
        scratch_shapes=[
            pltpu.VMEM((3 * SPAN + 1, R, LANES), BF16),
            pltpu.SemaphoreType.DMA((3,)),
        ],
        compiler_params=kernel_params(),
        cost_estimate=pl.CostEstimate(flops=2 * 2**28, bytes_accessed=10 * 2**20, transcendentals=0),
        name="near_field",
    )(src, count, trial, left, right, blocks)


def couple_kernel(
    src, count, own, left, right, flat, upper, rep_leaf, rep_upper, out, held, room
):
    first = (lax.axis_index("leaf") - 1) * SPAN
    room[...] = jnp.zeros_like(room)
    for n in range(SPAN):
        held[n] = split(unpack(left[SPAN + n]))
        held[SPAN + n] = split(unpack(own[n]))
        held[2 * SPAN + n] = split(unpack(right[SPAN + n]))
    held[3 * SPAN] = jnp.zeros((2 * R, LANES), BF16)
    at = lane_block((2 * R, LANES))
    picks = [jnp.where(at == k, 1.0, 0.0).astype(BF16) for k in range(4)]

    def leaf(n, carry):
        mats = spread(rep_leaf[...], flat[n])
        halves = []
        for h in range(2):
            terms = [
                held[source_row(src, count, n, 4 * h + k, first)] * picks[k] for k in range(4)
            ]
            halves.append((terms[0] + terms[1]) + (terms[2] + terms[3]))
        y = jnp.dot(jnp.concatenate(halves, axis=1), mats, preferred_element_type=F32)
        out[n] = fold(y[:R] + y[R:])
        return carry

    lax.fori_loop(0, SPAN, leaf, 0, unroll=4)
    base, cursor = SPAN, 2 * SPAN
    for l in range(1, 5):
        nodes = SPAN >> l
        keep = min(nodes, 3)

        def coef(j):
            if j < 0:
                return unpack(left[cursor + keep + j])
            if j >= nodes:
                return unpack(right[cursor + j - nodes])
            return unpack(own[base + j])

        for j in range(nodes):
            offsets = (-2, 2, 3) if j % 2 == 0 else (-3, -2, 2)
            mats = spread(rep_upper[...], upper_rows(upper, j * 2**l + 2 ** (l - 1) - 1, room))
            out[base + j] = couple(*[coef(j + k) for k in offsets], mats)
        base, cursor = base + nodes, cursor + keep


def local_couples(src, count, own, left, right, flat, upper):
    smem = pl.BlockSpec(memory_space=pltpu.SMEM)
    vmem = pl.BlockSpec(memory_space=pltpu.VMEM)
    return pl.pallas_call(
        couple_kernel,
        in_specs=[smem, smem] + [vmem] * 7,
        out_shape=jax.ShapeDtypeStruct((62, R, LANES), F32),
        scratch_shapes=[
            pltpu.VMEM((3 * SPAN + 1, 2 * R, LANES), BF16),
            pltpu.VMEM((R, LANES), F32),
        ],
        compiler_params=kernel_params(),
        cost_estimate=pl.CostEstimate(flops=2**28, bytes_accessed=4 * 2**20, transcendentals=0),
        name="local_couples",
    )(src, count, own, left, right, flat, upper, jnp.asarray(REP_LEAF, BF16), jnp.asarray(REP_UPPER, BF16))


def down_kernel(
    groups, got, inside, left, right, base_upper, transfer, basis, couples, near, rep_transfer, rep_upper,
    out, tree, side,
):
    device = lax.axis_index("leaf")
    place = lax.rem(device, GROUP)
    group = device // GROUP
    zero = jnp.zeros((R, LANES), F32)
    for e in range(GROUP):
        tree[e] = unpack(groups[e, :R])
    for j in range(8):
        mats = spread(rep_transfer[...], groups[2 * j, R : R + 16])
        tree[16 + j] = join_up(tree[2 * j], tree[2 * j + 1], mats)
    for j in range(4):
        mats = spread(rep_transfer[...], groups[4 * j + 1, R : R + 16])
        tree[24 + j] = join_up(tree[16 + 2 * j], tree[17 + 2 * j], mats)
    tree[28] = zero
    start, cursor, base = [], 0, 0
    at = 0
    for g in range(4):
        nodes = GROUP >> g
        keep = min(nodes, 3)
        start.append(at + keep)
        for k in range(keep):
            side[at + k] = unpack(left[cursor + k])
            side[at + keep + nodes + k] = unpack(right[cursor + k])
        for j in range(nodes):
            side[at + keep + j] = unpack(inside[base + j])
        at, cursor, base = at + nodes + 2 * keep, cursor + keep, base + nodes

    top = []
    for g in range(7):
        if g == 0:
            rows = base_upper[...]
        elif g < 5:
            rows = got[((place >> g) * 2 + 1) * 2 ** (g - 1) - 1, 48:]
        elif g == 5:
            rows = groups[(group >> 1) * 2, 48:]
        else:
            rows = groups[(group >> 2) * 4 + 1, 48:]
        mats = spread(rep_upper[...], rows)
        if g < 4:
            j = place >> g
            odd = j & 1
            terms = [side[start[g] + j + k] for k in (-2 - odd, 2 - 4 * odd, 3 - odd)]
        else:
            nodes, j = GROUP >> (g - 4), group >> (g - 4)
            odd = j & 1
            begin = (0, 16, 24)[g - 4]
            terms = []
            for k in (-2 - odd, 2 - 4 * odd, 3 - odd):
                ok = jnp.logical_and(j + k >= 0, j + k < nodes)
                terms.append(tree[jnp.where(ok, begin + j + k, 28)])
        top.append(couple(*terms, mats))

    down = top[6]
    for g in range(6, 0, -1):
        if g < 5:
            rows = got[((place >> g) * 2 + 1) * 2 ** (g - 1) - 1, 32:48]
        elif g == 5:
            rows = groups[(group >> 1) * 2, 32:48]
        else:
            rows = groups[(group >> 2) * 4 + 1, 32:48]
        lower, upper = pass_down(down, spread(rep_transfer[...], rows))
        odd = (device >> (g - 1)) & 1
        down = top[g - 1] + jnp.where(odd == 0, lower, upper)

    downs = [down]
    base = 62
    for l in range(5, 0, -1):
        nodes = SPAN >> l
        base -= 2 * nodes
        lower_downs = []
        for j in range(nodes):
            mats = spread(rep_transfer[...], transfer[j * 2**l + 2 ** (l - 1) - 1])
            lower, upper = pass_down(downs[j], mats)
            lower_downs.append(couples[base + 2 * j] + lower)
            lower_downs.append(couples[base + 2 * j + 1] + upper)
        downs = lower_downs
    for n in range(SPAN):
        rounded = downs[n][:, :R].astype(BF16)
        out[n] = near[n] + jnp.dot(rounded, basis[n], preferred_element_type=F32)


def down_all(groups, got, inside, left, right, base_upper, transfer, basis, couples, near):
    return pl.pallas_call(
        down_kernel,
        out_shape=jax.ShapeDtypeStruct((SPAN, R, LANES), F32),
        scratch_shapes=[pltpu.VMEM((29, R, LANES), F32), pltpu.VMEM((52, R, LANES), F32)],
        compiler_params=kernel_params(),
        name="down_all",
    )(
        groups, got, inside, left, right, base_upper, transfer, basis, couples, near,
        jnp.asarray(REP_TRANSFER, BF16), jnp.asarray(REP_UPPER, BF16),
    )


def passed_along(x, by, devices):
    pairs = [(i, i + by) for i in range(devices) if 0 <= i + by < devices]
    return lax.ppermute(x, "leaf", pairs)


def on_device(
    devices,
    trial_vectors,
    leaf_basis,
    near_blocks,
    near_src,
    near_count,
    couple_src,
    couple_count,
    couple_leaf,
    transfer,
    couple_upper,
):
    transfer_rows = transfer.reshape(SPAN, 2, 8, LANES).transpose(0, 2, 1, 3).reshape(SPAN, 16, LANES)
    leaf_rows = couple_leaf.reshape(SPAN, 8, 8, LANES).transpose(0, 2, 1, 3).reshape(SPAN, 64, LANES)

    in_row = [list(range(g * GROUP, (g + 1) * GROUP)) for g in range(GROUP)]
    across = [list(range(g, devices, GROUP)) for g in range(GROUP)]
    exchange = functools.partial(lax.all_to_all, axis_name="leaf", split_axis=0, concat_axis=0, tiled=True)

    send, own, to_right, to_left, base_upper = local_up(
        trial_vectors, leaf_basis, transfer_rows, couple_upper
    )
    got = exchange(send, axis_index_groups=in_row)
    left = passed_along(to_right, 1, devices)
    right = passed_along(to_left, -1, devices)
    group_send, inside, group_right, group_left = group_up(got)
    groups = exchange(group_send, axis_index_groups=across)
    from_left = passed_along(group_right, GROUP, devices)
    from_right = passed_along(group_left, -GROUP, devices)
    near = near_field(near_src, near_count, trial_vectors, left, right, near_blocks)
    couples = local_couples(couple_src, couple_count, own, left, right, leaf_rows, couple_upper)
    return down_all(
        groups, got, inside, from_left, from_right, base_upper, transfer_rows, leaf_basis, couples, near
    )


def solution(mesh):
    placed = (
        P("leaf", None, None),
        P("leaf", None, None),
        P("leaf", None, None, None),
        P("leaf", None),
        P("leaf"),
        P("leaf", None),
        P("leaf"),
        P("leaf", None, None),
        P("leaf", None, None),
        P("leaf", None, None),
    )
    return jax.shard_map(
        functools.partial(on_device, mesh.shape["leaf"]),
        mesh=mesh,
        in_specs=placed,
        out_specs=P("leaf", None, None),
        check_vma=False,
    )
```

```python
import functools

import jax
import jax.numpy as jnp
from jax import lax
from jax.experimental import pallas as pl
from jax.experimental.pallas import tpu as pltpu
from jax.sharding import PartitionSpec as P

F32, BF16 = jnp.float32, jnp.bfloat16
NT = (((1,), (1,)), ((), ()))
LANES = 128
R = 32
SPAN = 32
GROUP = 32
GROUPS = 8
ROWS = 64
EDGE = 96
BLOCK = (R, LANES)
VMEM_LIMIT = 60 * 1024 * 1024
HALO = SPAN * R + 43 * 16


def iota(shape, dim):
    return lax.broadcasted_iota(jnp.int32, shape, dim)


def block_of(x):
    return iota(x.shape, 1) >> 5


def one_hot(made):
    return jnp.where(made, 1.0, 0.0).astype(BF16)


def rep_rows(slots, rows, column):
    shape = (slots * R, rows)
    m, j = iota(shape, 0), iota(shape, 1)
    return one_hot(j == column(m >> 5, (m & 31) >> 2))


def rep_transfer():
    return rep_rows(2, 16, lambda c, i: i * 2 + c)


def rep_upper():
    return rep_rows(3, 32, lambda k, i: k * 8 + i)


def rep_leaf():
    return rep_rows(8, 64, lambda k, i: i * 8 + k)


def doubled(mats):
    pieces = [mats[R * (k // 2) : R * (k // 2 + 1)] for k in range(2 * mats.shape[0] // R)]
    return jnp.concatenate(pieces, axis=0)


def fold_matrix():
    shape = (LANES, LANES)
    return one_hot((iota(shape, 0) & 31) == (iota(shape, 1) & 31))


def spread(rep, rows):
    wide = jnp.dot(rep, rows, preferred_element_type=F32)
    return jnp.where(block_of(wide) == (iota(wide.shape, 0) & 3), wide, 0.0).astype(BF16)


def settle(mats, folds):
    return jnp.dot(mats, folds, preferred_element_type=F32).astype(BF16)


def fold(x):
    x = x + pltpu.roll(x, 32, 1)
    return x + pltpu.roll(x, 64, 1)


def split(x):
    high = x.astype(BF16)
    return jnp.concatenate([high, (x - high.astype(F32)).astype(BF16)], axis=1)


def gather_matrix():
    shape = (8 * LANES, LANES)
    row, lane = iota(shape, 0), iota(shape, 1)
    return one_hot(jnp.logical_and(row >> 8 == lane >> 5, (row & 31) == (lane & 31)))


def pack(x):
    high = x.astype(BF16).astype(F32)
    return jnp.where((block_of(x) & 1) == 0, high, x - high).astype(BF16)


def halve(x):
    low, high = x[:16].astype(F32), x[16:].astype(F32)
    return jnp.where(block_of(low) < 2, low, high).astype(BF16)


def unhalve(x):
    x = x.astype(F32)
    turned = pltpu.roll(x, 64, 1)
    low = block_of(x) < 2
    return jnp.concatenate([jnp.where(low, x, turned), jnp.where(low, turned, x)], axis=0)


def side_by_side(left, right):
    left, right = left.astype(F32), right.astype(F32)
    return jnp.where(block_of(left) < 2, left, right).astype(BF16)


def join_up(left, right, mats):
    return fold(jnp.dot(side_by_side(left, right), doubled(mats), preferred_element_type=F32))


def couple(terms, mats):
    both = jnp.concatenate([side_by_side(terms[0], terms[1]), terms[2][:, : 2 * R]], axis=1)
    return jnp.dot(both, doubled(mats), preferred_element_type=F32)


def times_transposed(x, mats):
    return lax.dot_general(pack(x)[:, : 2 * R], mats[:, : 2 * R], NT, preferred_element_type=F32)


def four_times(x):
    return jnp.concatenate([x, x, x, x], axis=0)


def kernel_params():
    return pltpu.CompilerParams(vmem_limit_bytes=VMEM_LIMIT)


HBM = pl.BlockSpec(memory_space=pltpu.HBM)
VMEM = pl.BlockSpec(memory_space=pltpu.VMEM)
SMEM = pl.BlockSpec(memory_space=pltpu.SMEM)


def fetch(pairs, sems, first=0):
    copies = [pltpu.make_async_copy(a, b, sems.at[first + k]) for k, (a, b) in enumerate(pairs)]
    for copy in copies:
        copy.start()
    return copies


def lay_out_upper(upper, room):
    for slot in range(3):
        for i in range(8):
            room[pl.ds((slot * 8 + i) * SPAN, SPAN), :] = upper[
                slot, :, LANES * i : LANES * (i + 1)
            ].astype(F32)


def upper_rows(room, node):
    rows = room[pl.ds(node, 24, stride=SPAN), :]
    return jnp.concatenate([rows, jnp.zeros((8, LANES), F32)], axis=0).astype(BF16)


def level_base(l):
    return sum(SPAN >> k for k in range(l))


def local_up_kernel(
    trial_hbm, basis_hbm, transfer_hbm, upper_hbm, send, own, to_right, to_left, base_upper,
    trial, basis, transfer, upper, room, head, edges, sems,
):
    copies = fetch(
        ((trial_hbm, trial), (basis_hbm, basis), (transfer_hbm, transfer), (upper_hbm, upper)), sems
    )
    whole = pl.ds(0, SPAN * R)
    rep = rep_transfer()
    for copy in copies[:3]:
        copy.wait()
    outs = fetch(((trial, to_right.at[whole]), (trial, to_left.at[whole])), sems, 4)
    for n in range(SPAN):
        own[n] = pack(
            lax.dot_general(
                trial[R * n : R * (n + 1)], four_times(basis[n]), NT, preferred_element_type=F32
            )
        )
    for l in range(1, 6):
        for j in range(SPAN >> l):
            mats = spread(rep, transfer[j * 2**l + 2 ** (l - 1) - 1])
            child = level_base(l - 1) + 2 * j
            own[level_base(l) + j] = pack(join_up(own[child], own[child + 1], mats))
    copies[3].wait()
    lay_out_upper(upper, room)
    head[:16] = halve(own[62])
    head[16:32] = transfer[SPAN - 1]
    head[32:] = upper_rows(room, SPAN - 1)
    outs += fetch([(head, send.at[g]) for g in range(GROUP)], sems, 6)
    base_upper[...] = upper_rows(room, SPAN // 2 - 1)
    for n in range(SPAN):
        edges[0, 16 * n : 16 * n + 16] = halve(own[n])
        edges[1, 16 * n : 16 * n + 16] = edges[0, 16 * n : 16 * n + 16]
    cursor = SPAN
    for l in range(1, 5):
        nodes = SPAN >> l
        keep = min(nodes, 3)
        for k in range(keep):
            at = level_base(l) + k
            edges[0, 16 * cursor : 16 * cursor + 16] = halve(own[at + nodes - keep])
            edges[1, 16 * cursor : 16 * cursor + 16] = halve(own[at])
            cursor += 1
    rest = pl.ds(SPAN * R, 16 * 43)
    outs += fetch(
        ((edges.at[0], to_right.at[rest]), (edges.at[1], to_left.at[rest])), sems, 6 + GROUP
    )
    for copy in outs:
        copy.wait()


def local_up(trial, basis, transfer, upper):
    return pl.pallas_call(
        local_up_kernel,
        in_specs=[HBM] * 4,
        out_specs=[HBM, VMEM, HBM, HBM, VMEM],
        out_shape=[
            jax.ShapeDtypeStruct((GROUP, ROWS, LANES), BF16),
            jax.ShapeDtypeStruct((63, *BLOCK), BF16),
            jax.ShapeDtypeStruct((HALO, LANES), BF16),
            jax.ShapeDtypeStruct((HALO, LANES), BF16),
            jax.ShapeDtypeStruct(BLOCK, BF16),
        ],
        scratch_shapes=[
            pltpu.VMEM((SPAN * R, LANES), BF16),
            pltpu.VMEM((SPAN, *BLOCK), BF16),
            pltpu.VMEM((SPAN, 16, LANES), BF16),
            pltpu.VMEM((3, SPAN, 1024), BF16),
            pltpu.VMEM((24 * SPAN, LANES), F32),
            pltpu.VMEM((ROWS, LANES), BF16),
            pltpu.VMEM((2, 16 * 43, LANES), BF16),
            pltpu.SemaphoreType.DMA((8 + GROUP,)),
        ],
        compiler_params=kernel_params(),
        name="local_up",
    )(trial, basis, transfer, upper)


def prepare_kernel(
    flat_hbm, transfer_hbm, upper_hbm, after, leaf_hbm, transfer_out, upper_out, token,
    flat, transfer, upper, room, leaf_out, sems,
):
    copies = fetch(((flat_hbm, flat), (transfer_hbm, transfer), (upper_hbm, upper)), sems)
    folds = fold_matrix()
    rep8, rep2, rep3 = rep_leaf(), rep_transfer(), rep_upper()
    for copy in copies:
        copy.wait()
    lay_out_upper(upper, room)

    def step(n, carry):
        leaf_out[n] = spread(rep8, flat[n])
        transfer_out[n] = settle(spread(rep2, transfer[n]), folds)
        upper_out[n] = settle(spread(rep3, upper_rows(room, n)), folds)
        return carry

    stores = []
    for k in range(4):
        lax.fori_loop(8 * k, 8 * (k + 1), step, 0, unroll=4)
        part = pl.ds(8 * k, 8)
        stores += fetch(((leaf_out.at[part], leaf_hbm.at[part]),), sems, 3 + k)
    token[...] = jnp.zeros_like(token)
    for copy in stores:
        copy.wait()


def prepare(flat, transfer, upper, after):
    return pl.pallas_call(
        prepare_kernel,
        in_specs=[HBM] * 4,
        out_specs=[HBM, VMEM, VMEM, VMEM],
        out_shape=[
            jax.ShapeDtypeStruct((SPAN, 256, LANES), BF16),
            jax.ShapeDtypeStruct((SPAN, 64, LANES), BF16),
            jax.ShapeDtypeStruct((SPAN, 96, LANES), BF16),
            jax.ShapeDtypeStruct((8, LANES), F32),
        ],
        scratch_shapes=[
            pltpu.VMEM((SPAN, 64, LANES), BF16),
            pltpu.VMEM((SPAN, 16, LANES), BF16),
            pltpu.VMEM((3, SPAN, 1024), BF16),
            pltpu.VMEM((24 * SPAN, LANES), F32),
            pltpu.VMEM((SPAN, 256, LANES), BF16),
            pltpu.SemaphoreType.DMA((7,)),
        ],
        compiler_params=kernel_params(),
        cost_estimate=pl.CostEstimate(flops=2**28, bytes_accessed=5 * 2**20, transcendentals=0),
        name="prepare",
    )(flat, transfer, upper, after)


def edge_level(place):
    return sum(jnp.where(place >= 2**g, 1, 0) for g in range(1, 5))


def group_up_kernel(got, after, left, right_halo, send, inside, token):
    rep = rep_transfer()
    for e in range(GROUP):
        inside[e] = unhalve(got[e, :16]).astype(BF16)
    for g in range(1, 6):
        for j in range(GROUP >> g):
            owner = (2 * j + 1) * 2 ** (g - 1) - 1
            mats = spread(rep, got[owner, 16:32])
            child = level_base(g - 1) + 2 * j
            inside[level_base(g) + j] = pack(join_up(inside[child], inside[child + 1], mats))
    device = lax.axis_index("leaf")
    place = lax.rem(device, GROUP)
    group = device // GROUP
    right = [level_base(g) + (GROUP >> g) - 2 for g in range(5)]
    right.append(63 - lax.shift_right_logical(32, edge_level(place)))
    left = [level_base(g) + 1 for g in range(5)]
    left.append(64 - lax.shift_right_logical(64, edge_level(GROUP - 1 - place)))
    head = jnp.concatenate([halve(inside[62]), got[GROUP - 1, 16:]], axis=0)
    to_left = jnp.concatenate([halve(inside[k]) for k in left], axis=0)
    for g in range(GROUPS):
        send[g, :ROWS] = head
        send[g, ROWS:] = to_left
    after_this = jnp.minimum(group + 1, GROUPS - 1)
    token[...] = jnp.zeros_like(token)
    send[after_this, ROWS:] = jnp.concatenate([halve(inside[k]) for k in right], axis=0)


def group_up(got, after, left, right):
    return pl.pallas_call(
        group_up_kernel,
        in_specs=[VMEM, HBM, HBM, HBM],
        out_shape=[
            jax.ShapeDtypeStruct((GROUPS, ROWS + EDGE, LANES), BF16),
            jax.ShapeDtypeStruct((63, *BLOCK), BF16),
            jax.ShapeDtypeStruct((8, LANES), F32),
        ],
        compiler_params=kernel_params(),
        name="group_up",
    )(got, after, left, right)


def source_row(src, count, row, slot, first):
    near = src[slot, row] - first
    near = jnp.minimum(jnp.maximum(near, 0), 3 * SPAN - 1)
    return jnp.where(slot < count[row], near, 3 * SPAN)


PIECES = 8


def middle_kernel(
    src, count, near_src, near_count, trial_hbm, own_hbm, left_hbm, right_hbm, leaf_hbm, transfer_hbm,
    upper_hbm, blocks_hbm, after, part_out, pass_out, near_out,
    own, left, right, leaf_mats, transfer, upper, blocks, trials, held, downs, coupled, sems,
):
    first = (lax.axis_index("leaf") - 1) * SPAN
    rest = pl.ds(SPAN * R, 16 * 43)
    whole = pl.ds(0, SPAN * R)
    copies = fetch(
        (
            (left_hbm.at[rest], left),
            (own_hbm, own),
            (right_hbm.at[rest], right),
            (transfer_hbm, transfer),
            (upper_hbm, upper),
            (leaf_hbm, leaf_mats),
            (left_hbm.at[whole], trials.at[pl.ds(0, SPAN * R)]),
            (trial_hbm, trials.at[pl.ds(SPAN * R, SPAN * R)]),
            (right_hbm.at[whole], trials.at[pl.ds(2 * SPAN * R, SPAN * R)]),
        ),
        sems,
    )
    size = SPAN // PIECES
    pieces = fetch(
        [
            (blocks_hbm.at[pl.ds(size * k, size)], blocks.at[pl.ds(size * k, size)])
            for k in range(PIECES)
        ],
        sems,
        len(copies),
    )
    held[3 * SPAN] = jnp.zeros(BLOCK, BF16)
    trials[3 * SPAN * R :] = jnp.zeros(BLOCK, BF16)
    shape = BLOCK
    eye = jnp.where(iota(shape, 0) == (iota(shape, 1) & 31), 1.0, 0.0)
    zero = jnp.zeros(shape, F32)
    downs[62] = jnp.concatenate([zero, eye], axis=0)
    for copy in copies[:5]:
        copy.wait()

    def edge(ref, k):
        return unhalve(ref[16 * k : 16 * k + 16]).astype(BF16)

    for n in range(SPAN):
        held[n] = edge(left, n)
        held[SPAN + n] = own[n]
        held[2 * SPAN + n] = edge(right, n)
    cursor = {}
    at = SPAN
    for l in range(1, 5):
        cursor[l] = at
        at += min(SPAN >> l, 3)
    for l in range(5, 0, -1):
        nodes = SPAN >> l
        for j in range(nodes):
            q = j * 2**l + 2 ** (l - 1) - 1
            mats = transfer[q]
            wide = jnp.concatenate([four_times(mats[:R]), four_times(mats[R:])], axis=0)
            y = times_transposed(downs[level_base(l) + j], wide)
            for c in range(2):
                part = y[:, LANES * c : LANES * (c + 1)]
                child, k = 2 * j + c, l - 1
                if k > 0:
                    n = SPAN >> k
                    keep = min(n, 3)

                    def coef(i):
                        if i < 0:
                            return edge(left, cursor[k] + keep + i)
                        if i >= n:
                            return edge(right, cursor[k] + i - n)
                        return own[level_base(k) + i]

                    offsets = (-2, 2, 3) if child % 2 == 0 else (-3, -2, 2)
                    m = upper[child * 2**k + 2 ** (k - 1) - 1]
                    got = couple([coef(child + i) for i in offsets], m)
                    part = part + jnp.concatenate([got, zero], axis=0)
                downs[level_base(k) + child] = part
    copies[5].wait()
    low = jnp.where((iota(BLOCK, 1) >> 6) == 0, 1.0, 0.0).astype(BF16)
    high = jnp.where((iota(BLOCK, 1) >> 6) == 1, 1.0, 0.0).astype(BF16)

    def leaf(n, carry):
        picked = [held[source_row(src, count, n, k, first)] for k in range(8)]
        row = jnp.concatenate(
            [picked[2 * h] * low + picked[2 * h + 1] * high for h in range(4)], axis=1
        )
        coupled[n] = jnp.dot(row, doubled(leaf_mats[n]), preferred_element_type=F32)
        return carry

    lax.fori_loop(0, SPAN, leaf, 0, unroll=8)
    at = block_of(zero)
    gather = gather_matrix()
    for m in range(8):
        x = [downs[4 * m + k] for k in range(4)]
        both = [
            jnp.where(at == 0, a, jnp.where(at == 1, b, jnp.where(at == 2, c, d)))
            for a, b, c, d in ([v[:R] for v in x], [v[R:] for v in x])
        ]
        wide = [split(coupled[4 * m + k]) for k in range(4)]
        part_out[m] = both[0] + jnp.dot(
            jnp.concatenate(wide, axis=1), gather, preferred_element_type=F32
        )
        high_part = both[1].astype(BF16)
        low_part = (both[1] - high_part.astype(F32)).astype(BF16)
        pass_out[m] = jnp.concatenate(
            [high_part, high_part, low_part, jnp.zeros(shape, BF16)], axis=0
        )
    for copy in copies[6:]:
        copy.wait()

    def near(n, carry):
        picked = []
        for k in range(8):
            row = pl.multiple_of(source_row(near_src, near_count, n, k, first) * R, R)
            picked.append(trials[pl.ds(row, R), :])
        near_out[n] = jnp.dot(
            jnp.concatenate(picked, axis=1),
            blocks[n].reshape(8 * LANES, LANES),
            preferred_element_type=F32,
        )
        return carry

    for k in range(PIECES):
        pieces[k].wait()
        lax.fori_loop(size * k, size * (k + 1), near, 0, unroll=size)


def middle(src, count, near_src, near_count, trial, own, left, right, leaf_mats, transfer, upper, blocks, after):
    return pl.pallas_call(
        middle_kernel,
        in_specs=[SMEM] * 4 + [HBM] * 9,
        out_shape=[
            jax.ShapeDtypeStruct((8, *BLOCK), F32),
            jax.ShapeDtypeStruct((8, LANES, LANES), BF16),
            jax.ShapeDtypeStruct((SPAN, *BLOCK), F32),
        ],
        scratch_shapes=[
            pltpu.VMEM((63, *BLOCK), BF16),
            pltpu.VMEM((16 * 43, LANES), BF16),
            pltpu.VMEM((16 * 43, LANES), BF16),
            pltpu.VMEM((SPAN, 256, LANES), BF16),
            pltpu.VMEM((SPAN, 64, LANES), BF16),
            pltpu.VMEM((SPAN, 96, LANES), BF16),
            pltpu.VMEM((SPAN, 8, LANES, LANES), BF16),
            pltpu.VMEM(((3 * SPAN + 1) * R, LANES), BF16),
            pltpu.VMEM((3 * SPAN + 1, *BLOCK), BF16),
            pltpu.VMEM((63, 2 * R, LANES), F32),
            pltpu.VMEM((SPAN, *BLOCK), F32),
            pltpu.SemaphoreType.DMA((9 + PIECES,)),
        ],
        compiler_params=kernel_params(),
        cost_estimate=pl.CostEstimate(flops=2**29, bytes_accessed=14 * 2**20, transcendentals=0),
        name="middle",
    )(src, count, near_src, near_count, trial, own, left, right, leaf_mats, transfer, upper, blocks, after)


def down_kernel(
    groups, got_hbm, inside_hbm, base_upper, basis_hbm, parts_hbm, passes_hbm, near_hbm, out_hbm,
    tree, side, path, basis, parts, passes, near, out, sems,
):
    device = lax.axis_index("leaf")
    place = lax.rem(device, GROUP)
    group = device // GROUP
    start, at = [], 0
    for g in range(5):
        start.append(at + 2)
        at += (GROUP >> g) + 4
    pairs = [
        (inside_hbm.at[pl.ds(level_base(g), GROUP >> g)], side.at[pl.ds(start[g], GROUP >> g)])
        for g in range(5)
    ]
    for g in range(1, 6):
        owner = ((place >> g) * 2 + 1) * 2 ** (g - 1) - 1
        pairs.append((got_hbm.at[owner, pl.ds(16, 48)], path.at[g]))
    early = fetch(pairs, sems)
    late = fetch(
        ((parts_hbm, parts), (passes_hbm, passes), (basis_hbm, basis), (near_hbm, near)), sems, 10
    )
    folds, rep2, rep3 = fold_matrix(), rep_transfer(), rep_upper()
    for e in range(GROUPS):
        tree[e] = unhalve(groups[e, :16]).astype(BF16)
    for j in range(4):
        mats = spread(rep2, groups[2 * j, 16:32])
        tree[8 + j] = pack(join_up(tree[2 * j], tree[2 * j + 1], mats))
    tree[12] = jnp.zeros(BLOCK, BF16)
    path[6] = groups[(group >> 1) * 2, 16:64]
    before, behind = jnp.maximum(group - 1, 0), jnp.minimum(group + 1, GROUPS - 1)
    has_before = jnp.where(group > 0, 1.0, 0.0)
    has_behind = jnp.where(group < GROUPS - 1, 1.0, 0.0)
    edges = []
    for k in range(6):
        rows = slice(ROWS + 16 * k, ROWS + 16 * (k + 1))
        edges.append(
            (
                (unhalve(groups[before, rows]) * has_before).astype(BF16),
                (unhalve(groups[behind, rows]) * has_behind).astype(BF16),
            )
        )
    for g in range(5):
        nodes = GROUP >> g
        side[start[g] - 2], side[start[g] - 1] = edges[g][0], edges[5][0]
        side[start[g] + nodes], side[start[g] + nodes + 1] = edges[5][1], edges[g][1]
    for copy in early:
        copy.wait()

    top = []
    for g in range(7):
        rows = base_upper[...] if g == 0 else path[g, 16:]
        if g < 5:
            j = place >> g
        else:
            j = group >> (g - 5)
        odd = j & 1
        terms = []
        for k in (-2 - odd, 2 - 4 * odd, 3 - odd):
            if g < 5:
                terms.append(side[start[g] + j + k])
            else:
                ok = jnp.logical_and(j + k >= 0, j + k < (GROUPS >> (g - 5)))
                terms.append(tree[jnp.where(ok, (0, 8)[g - 5] + j + k, 12)])
        top.append(fold(couple(terms, spread(rep3, rows))))

    down = top[6]
    for g in range(6, 0, -1):
        mats = settle(spread(rep2, path[g, :16]), folds)
        odd = jnp.broadcast_to((device >> (g - 1)) & 1, BLOCK)
        mats = jnp.where(odd == 1, mats[R:].astype(F32), mats[:R].astype(F32)).astype(BF16)
        down = top[g - 1] + times_transposed(down, four_times(mats))

    packed = pack(down).astype(F32)
    packed = jnp.where(block_of(down) < 3, packed, 0.0).astype(BF16)
    for copy in late:
        copy.wait()
    at = block_of(down)
    stores = []
    for m in range(8):
        x = parts[m] + jnp.dot(packed, passes[m], preferred_element_type=F32)
        x = x.astype(BF16).astype(F32)
        rows = jnp.concatenate([jnp.where(at == k, x, 0.0) for k in range(4)], axis=0)
        far = jnp.dot(
            rows.astype(BF16), basis[4 * m : 4 * m + 4].reshape(LANES, LANES), preferred_element_type=F32
        )
        for k in range(4):
            out[4 * m + k] = near[4 * m + k] + far[R * k : R * (k + 1)]
        stores += fetch(((out.at[pl.ds(4 * m, 4)], out_hbm.at[pl.ds(4 * m, 4)]),), sems, 14 + m)
    for copy in stores:
        copy.wait()


def down_all(groups, got, inside, base_upper, basis, parts, passes, near):
    return pl.pallas_call(
        down_kernel,
        in_specs=[VMEM, HBM, HBM, VMEM] + [HBM] * 4,
        out_specs=HBM,
        out_shape=jax.ShapeDtypeStruct((SPAN, *BLOCK), F32),
        scratch_shapes=[
            pltpu.VMEM((13, *BLOCK), BF16),
            pltpu.VMEM((82, *BLOCK), BF16),
            pltpu.VMEM((7, 48, LANES), BF16),
            pltpu.VMEM((SPAN, *BLOCK), BF16),
            pltpu.VMEM((8, *BLOCK), F32),
            pltpu.VMEM((8, LANES, LANES), BF16),
            pltpu.VMEM((SPAN, *BLOCK), F32),
            pltpu.VMEM((SPAN, *BLOCK), F32),
            pltpu.SemaphoreType.DMA((22,)),
        ],
        compiler_params=kernel_params(),
        name="down_all",
    )(groups, got, inside, base_upper, basis, parts, passes, near)


def passed_along(x, by, devices):
    pairs = [(i, i + by) for i in range(devices) if 0 <= i + by < devices]
    return lax.ppermute(x, "leaf", pairs)


def on_device(
    devices,
    trial_vectors,
    leaf_basis,
    near_blocks,
    near_src,
    near_count,
    couple_src,
    couple_count,
    couple_leaf,
    transfer,
    couple_upper,
):
    transfer_rows = transfer.reshape(SPAN, 2, 8, LANES).transpose(0, 2, 1, 3).reshape(SPAN, 16, LANES)
    leaf_rows = couple_leaf.reshape(SPAN, 8, 8, LANES).transpose(0, 2, 1, 3).reshape(SPAN, 64, LANES)
    upper_slots = couple_upper.transpose(1, 0, 2)

    in_row = [list(range(g * GROUP, (g + 1) * GROUP)) for g in range(GROUPS)]
    across = [list(range(g, devices, GROUP)) for g in range(GROUP)]
    exchange = functools.partial(lax.all_to_all, axis_name="leaf", split_axis=0, concat_axis=0, tiled=True)

    trial_rows = trial_vectors.reshape(SPAN * R, LANES)
    send, own, to_right, to_left, base_upper = local_up(
        trial_rows, leaf_basis, transfer_rows, upper_slots
    )
    got = exchange(send, axis_index_groups=in_row)
    left = passed_along(to_right, 1, devices)
    right = passed_along(to_left, -1, devices)
    leaf_mats, transfer_mats, upper_mats, prepared = prepare(leaf_rows, transfer_rows, upper_slots, base_upper)
    group_send, inside, token = group_up(got, prepared, left, right)
    groups = exchange(group_send, axis_index_groups=across)
    parts, passes, near = middle(
        couple_src.T, couple_count, near_src.T, near_count, trial_rows, own, left, right,
        leaf_mats, transfer_mats, upper_mats, near_blocks, token,
    )
    return down_all(groups, got, inside, base_upper, leaf_basis, parts, passes, near)


def solution(mesh):
    placed = (
        P("leaf", None, None),
        P("leaf", None, None),
        P("leaf", None, None, None),
        P("leaf", None),
        P("leaf"),
        P("leaf", None),
        P("leaf"),
        P("leaf", None, None),
        P("leaf", None, None),
        P("leaf", None, None),
    )
    return jax.shard_map(
        functools.partial(on_device, mesh.shape["leaf"]),
        mesh=mesh,
        in_specs=placed,
        out_specs=P("leaf", None, None),
        check_vma=False,
    )
```

```python
import functools

import jax
import jax.numpy as jnp
from jax import lax
from jax.experimental import pallas as pl
from jax.experimental.pallas import tpu as pltpu
from jax.sharding import PartitionSpec as P

F32, BF16 = jnp.float32, jnp.bfloat16
NT = (((1,), (1,)), ((), ()))
LANES = 128
R = 32
SPAN = 32
GROUP = 32
GROUPS = 8
ROWS = 64
EDGE = 96
BLOCK = (R, LANES)
VMEM_LIMIT = 60 * 1024 * 1024
HALO = SPAN * R + 43 * 16


def iota(shape, dim):
    return lax.broadcasted_iota(jnp.int32, shape, dim)


def block_of(x):
    return iota(x.shape, 1) >> 5


def one_hot(made):
    return jnp.where(made, 1.0, 0.0).astype(BF16)


def rep_rows(slots, rows, column):
    shape = (slots * R, rows)
    m, j = iota(shape, 0), iota(shape, 1)
    return one_hot(j == column(m >> 5, (m & 31) >> 2))


def rep_transfer():
    return rep_rows(2, 16, lambda c, i: i * 2 + c)


def rep_upper():
    return rep_rows(3, 32, lambda k, i: k * 8 + i)


def rep_leaf():
    return rep_rows(8, 64, lambda k, i: i * 8 + k)


def doubled(mats):
    pieces = [mats[R * (k // 2) : R * (k // 2 + 1)] for k in range(2 * mats.shape[0] // R)]
    return jnp.concatenate(pieces, axis=0)


def fold_matrix():
    shape = (LANES, LANES)
    return one_hot((iota(shape, 0) & 31) == (iota(shape, 1) & 31))


def spread(rep, rows):
    wide = jnp.dot(rep, rows, preferred_element_type=F32)
    return jnp.where(block_of(wide) == (iota(wide.shape, 0) & 3), wide, 0.0).astype(BF16)


def settle(mats, folds):
    return jnp.dot(mats, folds, preferred_element_type=F32).astype(BF16)


def fold(x):
    x = x + pltpu.roll(x, 32, 1)
    return x + pltpu.roll(x, 64, 1)


def split(x):
    high = x.astype(BF16)
    return jnp.concatenate([high, (x - high.astype(F32)).astype(BF16)], axis=1)


def gather_matrix():
    shape = (8 * LANES, LANES)
    row, lane = iota(shape, 0), iota(shape, 1)
    return one_hot(jnp.logical_and(row >> 8 == lane >> 5, (row & 31) == (lane & 31)))


def pack(x):
    high = x.astype(BF16).astype(F32)
    return jnp.where((block_of(x) & 1) == 0, high, x - high).astype(BF16)


def halve(x):
    low, high = x[:16].astype(F32), x[16:].astype(F32)
    return jnp.where(block_of(low) < 2, low, high).astype(BF16)


def unhalve(x):
    x = x.astype(F32)
    turned = pltpu.roll(x, 64, 1)
    low = block_of(x) < 2
    return jnp.concatenate([jnp.where(low, x, turned), jnp.where(low, turned, x)], axis=0)


def side_by_side(left, right):
    left, right = left.astype(F32), right.astype(F32)
    return jnp.where(block_of(left) < 2, left, right).astype(BF16)


def join_up(left, right, mats):
    return fold(jnp.dot(side_by_side(left, right), doubled(mats), preferred_element_type=F32))


def couple(terms, mats):
    both = jnp.concatenate([side_by_side(terms[0], terms[1]), terms[2][:, : 2 * R]], axis=1)
    return jnp.dot(both, doubled(mats), preferred_element_type=F32)


def times_transposed(x, mats):
    return lax.dot_general(pack(x)[:, : 2 * R], mats[:, : 2 * R], NT, preferred_element_type=F32)


def four_times(x):
    return jnp.concatenate([x, x, x, x], axis=0)


def kernel_params(limit=VMEM_LIMIT):
    return pltpu.CompilerParams(vmem_limit_bytes=limit)


HBM = pl.BlockSpec(memory_space=pltpu.HBM)
VMEM = pl.BlockSpec(memory_space=pltpu.VMEM)
SMEM = pl.BlockSpec(memory_space=pltpu.SMEM)


def fetch(pairs, sems, first=0):
    copies = [pltpu.make_async_copy(a, b, sems.at[first + k]) for k, (a, b) in enumerate(pairs)]
    for copy in copies:
        copy.start()
    return copies


def lay_out_upper(upper, room):
    nodes = upper.shape[1]
    for slot in range(3):
        for i in range(8):
            room[pl.ds((slot * 8 + i) * nodes, nodes), :] = upper[
                slot, :, LANES * i : LANES * (i + 1)
            ].astype(F32)


def upper_rows(room, node, nodes=SPAN):
    rows = room[pl.ds(node, 24, stride=nodes), :]
    return jnp.concatenate([rows, jnp.zeros((8, LANES), F32)], axis=0).astype(BF16)


def level_base(l):
    return sum(SPAN >> k for k in range(l))


def local_up_kernel(
    trial_hbm, basis_hbm, transfer_hbm, upper_hbm, send, own_hbm,
    trial, basis, transfer, upper, room, own, head, sems,
):
    last = pl.ds(SPAN - 8, 8)
    copies = fetch(
        (
            (trial_hbm, trial),
            (basis_hbm, basis),
            (transfer_hbm, transfer),
            (upper_hbm.at[:, last, :], upper),
        ),
        sems,
    )
    rep = rep_transfer()
    for copy in copies[:2]:
        copy.wait()
    for n in range(SPAN):
        own[n] = pack(
            lax.dot_general(
                trial[R * n : R * (n + 1)], four_times(basis[n]), NT, preferred_element_type=F32
            )
        )
    leaves, nodes = pl.ds(0, SPAN), pl.ds(SPAN, SPAN - 1)
    outs = fetch([(own.at[leaves], own_hbm.at[leaves])], sems, 4)
    for copy in copies[2:]:
        copy.wait()
    lay_out_upper(upper, room)
    head[16:32] = transfer[SPAN - 1]
    head[32:] = upper_rows(room, 7, 8)
    for l in range(1, 6):
        for j in range(SPAN >> l):
            mats = spread(rep, transfer[j * 2**l + 2 ** (l - 1) - 1])
            child = level_base(l - 1) + 2 * j
            own[level_base(l) + j] = pack(join_up(own[child], own[child + 1], mats))
    head[:16] = halve(own[62])
    outs += fetch(
        [(head, send.at[g]) for g in range(GROUP)] + [(own.at[nodes], own_hbm.at[nodes])], sems, 5
    )
    for copy in outs:
        copy.wait()


def local_up(trial, basis, transfer, upper):
    return pl.pallas_call(
        local_up_kernel,
        in_specs=[HBM] * 4,
        out_specs=[HBM, HBM],
        out_shape=[
            jax.ShapeDtypeStruct((GROUP, ROWS, LANES), BF16),
            jax.ShapeDtypeStruct((63, *BLOCK), BF16),
        ],
        scratch_shapes=[
            pltpu.VMEM((SPAN * R, LANES), BF16),
            pltpu.VMEM((SPAN, *BLOCK), BF16),
            pltpu.VMEM((SPAN, 16, LANES), BF16),
            pltpu.VMEM((3, 8, 1024), BF16),
            pltpu.VMEM((24 * 8, LANES), F32),
            pltpu.VMEM((63, *BLOCK), BF16),
            pltpu.VMEM((ROWS, LANES), BF16),
            pltpu.SemaphoreType.DMA((6 + GROUP,)),
        ],
        compiler_params=kernel_params(),
        name="local_up",
    )(trial, basis, transfer, upper)


def prepare_kernel(
    trial_hbm, own_hbm, transfer_hbm, upper_hbm, to_chip, to_next, transfer_out, upper_out, base_upper,
    trial, own, transfer, upper, room, edges, sems,
):
    copies = fetch(
        ((trial_hbm, trial), (own_hbm, own), (transfer_hbm, transfer), (upper_hbm, upper)), sems
    )
    odd = lax.axis_index("leaf") & 1
    whole, rest = pl.ds(0, SPAN * R), pl.ds(SPAN * R, 16 * 43)
    copies[0].wait()
    outs = fetch(((trial, to_chip.at[whole]), (trial, to_next.at[whole])), sems, 4)
    copies[1].wait()
    for n in range(SPAN):
        half = halve(own[n])
        edges[0, 16 * n : 16 * n + 16] = half
        edges[1, 16 * n : 16 * n + 16] = half
    cursor = SPAN
    for l in range(1, 5):
        nodes = SPAN >> l
        keep = min(nodes, 3)
        for k in range(keep):
            at = level_base(l) + k
            edges[0, 16 * cursor : 16 * cursor + 16] = halve(own[at + nodes - keep])
            edges[1, 16 * cursor : 16 * cursor + 16] = halve(own[at])
            cursor += 1
    outs += fetch(
        ((edges.at[odd], to_chip.at[rest]), (edges.at[1 - odd], to_next.at[rest])), sems, 6
    )
    folds = fold_matrix()
    rep2, rep3 = rep_transfer(), rep_upper()
    for copy in copies[2:]:
        copy.wait()
    lay_out_upper(upper, room)

    def step(n, carry):
        transfer_out[n] = settle(spread(rep2, transfer[n]), folds)
        upper_out[n] = settle(spread(rep3, upper_rows(room, n)), folds)
        return carry

    lax.fori_loop(0, SPAN, step, 0, unroll=8)
    base_upper[...] = upper_rows(room, SPAN // 2 - 1)
    for copy in outs:
        copy.wait()


def prepare(trial, own, transfer, upper):
    return pl.pallas_call(
        prepare_kernel,
        in_specs=[HBM] * 4,
        out_specs=[HBM, HBM, VMEM, VMEM, VMEM],
        out_shape=[
            jax.ShapeDtypeStruct((HALO, LANES), BF16),
            jax.ShapeDtypeStruct((HALO, LANES), BF16),
            jax.ShapeDtypeStruct((SPAN, 64, LANES), BF16),
            jax.ShapeDtypeStruct((SPAN, 96, LANES), BF16),
            jax.ShapeDtypeStruct(BLOCK, BF16),
        ],
        scratch_shapes=[
            pltpu.VMEM((SPAN * R, LANES), BF16),
            pltpu.VMEM((63, *BLOCK), BF16),
            pltpu.VMEM((SPAN, 16, LANES), BF16),
            pltpu.VMEM((3, SPAN, 1024), BF16),
            pltpu.VMEM((24 * SPAN, LANES), F32),
            pltpu.VMEM((2, 16 * 43, LANES), BF16),
            pltpu.SemaphoreType.DMA((8,)),
        ],
        compiler_params=kernel_params(),
        cost_estimate=pl.CostEstimate(flops=2**28, bytes_accessed=5 * 2**20, transcendentals=0),
        name="prepare",
    )(trial, own, transfer, upper)


def source_offsets(j):
    odd = j & 1
    return (-2 - odd, 2 - 4 * odd, 3 - odd)


def edge_level(place):
    return sum(jnp.where(place >= 2**g, 1, 0) for g in range(1, 5))


def group_up_kernel(got, send, mine, inside):
    rep = rep_transfer()
    for e in range(GROUP):
        inside[e] = unhalve(got[e, :16]).astype(BF16)
    for g in range(1, 6):
        for j in range(GROUP >> g):
            owner = (2 * j + 1) * 2 ** (g - 1) - 1
            mats = spread(rep, got[owner, 16:32])
            child = level_base(g - 1) + 2 * j
            inside[level_base(g) + j] = pack(join_up(inside[child], inside[child + 1], mats))
    device = lax.axis_index("leaf")
    place = lax.rem(device, GROUP)
    group = device // GROUP
    right = [level_base(g) + (GROUP >> g) - 2 for g in range(5)]
    right.append(63 - lax.shift_right_logical(32, edge_level(place)))
    left = [level_base(g) + 1 for g in range(5)]
    left.append(64 - lax.shift_right_logical(64, edge_level(GROUP - 1 - place)))
    head = jnp.concatenate([halve(inside[62]), got[GROUP - 1, 16:]], axis=0)
    to_left = jnp.concatenate([halve(inside[k]) for k in left], axis=0)
    for g in range(GROUPS):
        send[g, :ROWS] = head
        send[g, ROWS:] = to_left
    after_this = jnp.minimum(group + 1, GROUPS - 1)
    inside[63] = jnp.zeros(BLOCK, BF16)
    for g in range(5):
        j, nodes = place >> g, GROUP >> g
        for k, offset in enumerate(source_offsets(j)):
            at = j + offset
            ok = jnp.logical_and(at >= 0, at < nodes)
            mine[144 * g + R * k : 144 * g + R * (k + 1)] = inside[jnp.where(ok, level_base(g) + at, 63)]
        mine[144 * g + 96 : 144 * (g + 1)] = got[((place >> (g + 1)) * 2 + 1) * 2**g - 1, 16:]
    send[after_this, ROWS:] = jnp.concatenate([halve(inside[k]) for k in right], axis=0)


def group_up(got):
    return pl.pallas_call(
        group_up_kernel,
        out_shape=[
            jax.ShapeDtypeStruct((GROUPS, ROWS + EDGE, LANES), BF16),
            jax.ShapeDtypeStruct((5 * 144, LANES), BF16),
        ],
        scratch_shapes=[pltpu.VMEM((64, *BLOCK), BF16)],
        compiler_params=kernel_params(16 * 1024 * 1024),
        cost_estimate=pl.CostEstimate(flops=2**31, bytes_accessed=2**25, transcendentals=0),
        name="group_up",
    )(got)


def source_row(src, count, row, slot, first):
    near = src[slot, row] - first
    near = jnp.minimum(jnp.maximum(near, 0), 3 * SPAN - 1)
    return jnp.where(slot < count[row], near, 3 * SPAN)


PIECES = 8


def middle_kernel(
    src, count, near_src, near_count, trial_hbm, own_hbm, chip_hbm, next_hbm, leaf_hbm, transfer_hbm,
    upper_hbm, blocks_hbm, after, part_out, pass_out, near_out,
    own, sides, leaf_rows, transfer, upper, blocks, trials, held, downs, coupled, sems,
):
    first = (lax.axis_index("leaf") - 1) * SPAN
    rest = pl.ds(SPAN * R, 16 * 43)
    whole = pl.ds(0, SPAN * R)
    odd = lax.axis_index("leaf") & 1

    def trial_place(third):
        return trials.at[pl.ds(pl.multiple_of(third * (SPAN * R), SPAN * R), SPAN * R)]

    copies = fetch(
        (
            (chip_hbm.at[rest], sides.at[1 - odd]),
            (own_hbm, own),
            (next_hbm.at[rest], sides.at[odd]),
            (transfer_hbm, transfer),
            (upper_hbm, upper),
            (leaf_hbm, leaf_rows),
            (chip_hbm.at[whole], trial_place(2 - 2 * odd)),
            (trial_hbm, trial_place(1)),
            (next_hbm.at[whole], trial_place(2 * odd)),
        ),
        sems,
    )
    size = SPAN // PIECES
    pieces = fetch(
        [
            (blocks_hbm.at[pl.ds(size * k, size)], blocks.at[pl.ds(size * k, size)])
            for k in range(PIECES)
        ],
        sems,
        len(copies),
    )
    held[3 * SPAN] = jnp.zeros(BLOCK, BF16)
    trials[3 * SPAN * R :] = jnp.zeros(BLOCK, BF16)
    shape = BLOCK
    eye = jnp.where(iota(shape, 0) == (iota(shape, 1) & 31), 1.0, 0.0)
    zero = jnp.zeros(shape, F32)
    downs[62] = jnp.concatenate([zero, eye], axis=0)
    for copy in copies[:5]:
        copy.wait()

    def edge(side, k):
        return unhalve(sides[side, 16 * k : 16 * k + 16]).astype(BF16)

    for n in range(SPAN):
        held[n] = edge(0, n)
        held[SPAN + n] = own[n]
        held[2 * SPAN + n] = edge(1, n)
    cursor = {}
    at = SPAN
    for l in range(1, 5):
        cursor[l] = at
        at += min(SPAN >> l, 3)
    for l in range(5, 0, -1):
        nodes = SPAN >> l
        for j in range(nodes):
            q = j * 2**l + 2 ** (l - 1) - 1
            mats = transfer[q]
            wide = jnp.concatenate([four_times(mats[:R]), four_times(mats[R:])], axis=0)
            y = times_transposed(downs[level_base(l) + j], wide)
            for c in range(2):
                part = y[:, LANES * c : LANES * (c + 1)]
                child, k = 2 * j + c, l - 1
                if k > 0:
                    n = SPAN >> k
                    keep = min(n, 3)

                    def coef(i):
                        if i < 0:
                            return edge(0, cursor[k] + keep + i)
                        if i >= n:
                            return edge(1, cursor[k] + i - n)
                        return own[level_base(k) + i]

                    offsets = (-2, 2, 3) if child % 2 == 0 else (-3, -2, 2)
                    m = upper[child * 2**k + 2 ** (k - 1) - 1]
                    got = couple([coef(child + i) for i in offsets], m)
                    part = part + jnp.concatenate([got, zero], axis=0)
                downs[level_base(k) + child] = part
    copies[5].wait()
    low = jnp.where((iota(BLOCK, 1) >> 6) == 0, 1.0, 0.0).astype(BF16)
    high = jnp.where((iota(BLOCK, 1) >> 6) == 1, 1.0, 0.0).astype(BF16)

    rep8 = rep_leaf()

    def leaf(n, carry):
        mats = spread(rep8, leaf_rows[n])
        picked = [held[source_row(src, count, n, k, first)] for k in range(8)]
        row = jnp.concatenate(
            [picked[2 * h] * low + picked[2 * h + 1] * high for h in range(4)], axis=1
        )
        coupled[n] = jnp.dot(row, doubled(mats), preferred_element_type=F32)
        return carry

    lax.fori_loop(0, SPAN, leaf, 0, unroll=8)
    at = block_of(zero)
    gather = gather_matrix()
    for m in range(8):
        x = [downs[4 * m + k] for k in range(4)]
        both = [
            jnp.where(at == 0, a, jnp.where(at == 1, b, jnp.where(at == 2, c, d)))
            for a, b, c, d in ([v[:R] for v in x], [v[R:] for v in x])
        ]
        wide = [split(coupled[4 * m + k]) for k in range(4)]
        part_out[m] = both[0] + jnp.dot(
            jnp.concatenate(wide, axis=1), gather, preferred_element_type=F32
        )
        high_part = both[1].astype(BF16)
        low_part = (both[1] - high_part.astype(F32)).astype(BF16)
        pass_out[m] = jnp.concatenate(
            [high_part, high_part, low_part, jnp.zeros(shape, BF16)], axis=0
        )
    for copy in copies[6:]:
        copy.wait()

    def near(n, carry):
        picked = []
        for k in range(8):
            row = pl.multiple_of(source_row(near_src, near_count, n, k, first) * R, R)
            picked.append(trials[pl.ds(row, R), :])
        near_out[n] = jnp.dot(
            jnp.concatenate(picked, axis=1),
            blocks[n].reshape(8 * LANES, LANES),
            preferred_element_type=F32,
        )
        return carry

    for k in range(PIECES):
        pieces[k].wait()
        lax.fori_loop(size * k, size * (k + 1), near, 0, unroll=size)


def middle(src, count, near_src, near_count, trial, own, chip_halo, next_halo, leaf_rows, transfer, upper, blocks, after):
    return pl.pallas_call(
        middle_kernel,
        in_specs=[SMEM] * 4 + [HBM] * 9,
        out_shape=[
            jax.ShapeDtypeStruct((8, *BLOCK), F32),
            jax.ShapeDtypeStruct((8, LANES, LANES), BF16),
            jax.ShapeDtypeStruct((SPAN, *BLOCK), F32),
        ],
        scratch_shapes=[
            pltpu.VMEM((63, *BLOCK), BF16),
            pltpu.VMEM((2, 16 * 43, LANES), BF16),
            pltpu.VMEM((SPAN, 64, LANES), BF16),
            pltpu.VMEM((SPAN, 64, LANES), BF16),
            pltpu.VMEM((SPAN, 96, LANES), BF16),
            pltpu.VMEM((SPAN, 8, LANES, LANES), BF16),
            pltpu.VMEM(((3 * SPAN + 1) * R, LANES), BF16),
            pltpu.VMEM((3 * SPAN + 1, *BLOCK), BF16),
            pltpu.VMEM((63, 2 * R, LANES), F32),
            pltpu.VMEM((SPAN, *BLOCK), F32),
            pltpu.SemaphoreType.DMA((9 + PIECES,)),
        ],
        compiler_params=kernel_params(),
        cost_estimate=pl.CostEstimate(flops=2**36, bytes_accessed=2**29, transcendentals=0),
        name="middle",
    )(src, count, near_src, near_count, trial, own, chip_halo, next_halo, leaf_rows, transfer, upper, blocks, after)


def down_kernel(
    groups, mine, base_upper, basis_hbm, parts_hbm, passes_hbm, near_hbm, out_hbm,
    tree, side, basis, parts, passes, near, out, sems,
):
    device = lax.axis_index("leaf")
    place = lax.rem(device, GROUP)
    group = device // GROUP
    late = fetch(
        ((parts_hbm, parts), (passes_hbm, passes), (basis_hbm, basis), (near_hbm, near)), sems
    )
    folds, rep2, rep3 = fold_matrix(), rep_transfer(), rep_upper()
    for e in range(GROUPS):
        tree[e] = unhalve(groups[e, :16]).astype(BF16)
    for j in range(4):
        mats = spread(rep2, groups[2 * j, 16:32])
        tree[8 + j] = pack(join_up(tree[2 * j], tree[2 * j + 1], mats))
    tree[12] = jnp.zeros(BLOCK, BF16)
    top_path = groups[(group >> 1) * 2, 16:64]
    before, behind = jnp.maximum(group - 1, 0), jnp.minimum(group + 1, GROUPS - 1)
    has_before = jnp.where(group > 0, 1.0, 0.0)
    has_behind = jnp.where(group < GROUPS - 1, 1.0, 0.0)
    edges = []
    for k in range(6):
        rows = slice(ROWS + 16 * k, ROWS + 16 * (k + 1))
        edges.append(
            (
                (unhalve(groups[before, rows]) * has_before).astype(BF16),
                (unhalve(groups[behind, rows]) * has_behind).astype(BF16),
            )
        )
    for g in range(5):
        side[g, 0] = jnp.zeros(BLOCK, BF16)
        side[g, 1], side[g, 2] = edges[g][0], edges[5][0]
        side[g, 3], side[g, 4] = edges[5][1], edges[g][1]

    top = []
    for g in range(7):
        rows = base_upper[...] if g == 0 else mine[144 * g - 32 : 144 * g] if g < 6 else top_path[16:]
        sources = []
        if g < 5:
            j, nodes = place >> g, GROUP >> g
            for k, offset in enumerate(source_offsets(j)):
                at = j + offset
                pick = jnp.where(at < 0, at + 3, jnp.where(at < nodes, 0, at - nodes + 3))
                sources.append(mine[144 * g + R * k : 144 * g + R * (k + 1)] + side[g, pick])
        else:
            j, nodes = group >> (g - 5), GROUPS >> (g - 5)
            for offset in source_offsets(j):
                at = j + offset
                ok = jnp.logical_and(at >= 0, at < nodes)
                sources.append(tree[jnp.where(ok, (0, 8)[g - 5] + at, 12)])
        top.append(fold(couple(sources, spread(rep3, rows))))

    down = top[6]
    for g in range(6, 0, -1):
        rows = mine[144 * g - 48 : 144 * g - 32] if g < 6 else top_path[:16]
        mats = settle(spread(rep2, rows), folds)
        odd = jnp.broadcast_to((device >> (g - 1)) & 1, BLOCK)
        mats = jnp.where(odd == 1, mats[R:].astype(F32), mats[:R].astype(F32)).astype(BF16)
        down = top[g - 1] + times_transposed(down, four_times(mats))

    packed = pack(down).astype(F32)
    packed = jnp.where(block_of(down) < 3, packed, 0.0).astype(BF16)
    for copy in late:
        copy.wait()
    at = block_of(down)
    stores = []
    for m in range(8):
        x = parts[m] + jnp.dot(packed, passes[m], preferred_element_type=F32)
        x = x.astype(BF16).astype(F32)
        rows = jnp.concatenate([jnp.where(at == k, x, 0.0) for k in range(4)], axis=0)
        far = jnp.dot(
            rows.astype(BF16), basis[4 * m : 4 * m + 4].reshape(LANES, LANES), preferred_element_type=F32
        )
        for k in range(4):
            out[4 * m + k] = near[4 * m + k] + far[R * k : R * (k + 1)]
        stores += fetch(((out.at[pl.ds(4 * m, 4)], out_hbm.at[pl.ds(4 * m, 4)]),), sems, 4 + m)
    for copy in stores:
        copy.wait()


def down_all(groups, mine, base_upper, basis, parts, passes, near):
    return pl.pallas_call(
        down_kernel,
        in_specs=[VMEM] * 3 + [HBM] * 4,
        out_specs=HBM,
        out_shape=jax.ShapeDtypeStruct((SPAN, *BLOCK), F32),
        scratch_shapes=[
            pltpu.VMEM((13, *BLOCK), BF16),
            pltpu.VMEM((5, 5, *BLOCK), BF16),
            pltpu.VMEM((SPAN, *BLOCK), BF16),
            pltpu.VMEM((8, *BLOCK), F32),
            pltpu.VMEM((8, LANES, LANES), BF16),
            pltpu.VMEM((SPAN, *BLOCK), F32),
            pltpu.VMEM((SPAN, *BLOCK), F32),
            pltpu.SemaphoreType.DMA((12,)),
        ],
        compiler_params=kernel_params(),
        name="down_all",
    )(groups, mine, base_upper, basis, parts, passes, near)


def swapped(x, first, devices):
    lower = range(first, devices - 1, 2)
    return lax.ppermute(x, "leaf", [(i, i + 1) for i in lower] + [(i + 1, i) for i in lower])


def on_device(
    devices,
    trial_vectors,
    leaf_basis,
    near_blocks,
    near_src,
    near_count,
    couple_src,
    couple_count,
    couple_leaf,
    transfer,
    couple_upper,
):
    transfer_rows = transfer.reshape(SPAN, 2, 8, LANES).transpose(0, 2, 1, 3).reshape(SPAN, 16, LANES)
    leaf_rows = couple_leaf.reshape(SPAN, 8, 8, LANES).transpose(0, 2, 1, 3).reshape(SPAN, 64, LANES)
    upper_slots = couple_upper.transpose(1, 0, 2)

    in_row = [list(range(g * GROUP, (g + 1) * GROUP)) for g in range(GROUPS)]
    across = [list(range(g, devices, GROUP)) for g in range(GROUP)]
    exchange = functools.partial(lax.all_to_all, axis_name="leaf", split_axis=0, concat_axis=0, tiled=True)

    trial_rows = trial_vectors.reshape(SPAN * R, LANES)
    send, own = local_up(trial_rows, leaf_basis, transfer_rows, upper_slots)
    got = exchange(send, axis_index_groups=in_row)
    to_chip, to_next, transfer_mats, upper_mats, base_upper = prepare(
        trial_rows, own, transfer_rows, upper_slots
    )
    chip_halo = swapped(to_chip, 0, devices)
    next_halo = swapped(to_next, 1, devices)
    group_send, mine = group_up(got)
    groups = exchange(group_send, axis_index_groups=across)
    parts, passes, near = middle(
        couple_src.T, couple_count, near_src.T, near_count, trial_rows, own, chip_halo, next_halo,
        leaf_rows, transfer_mats, upper_mats, near_blocks, mine,
    )
    return down_all(groups, mine, base_upper, leaf_basis, parts, passes, near)


def solution(mesh):
    placed = (
        P("leaf", None, None),
        P("leaf", None, None),
        P("leaf", None, None, None),
        P("leaf", None),
        P("leaf"),
        P("leaf", None),
        P("leaf"),
        P("leaf", None, None),
        P("leaf", None, None),
        P("leaf", None, None),
    )
    return jax.shard_map(
        functools.partial(on_device, mesh.shape["leaf"]),
        mesh=mesh,
        in_specs=placed,
        out_specs=P("leaf", None, None),
        check_vma=False,
    )
```

```python
import functools

import jax
import jax.numpy as jnp
from jax import lax
from jax.experimental import pallas as pl
from jax.experimental.pallas import tpu as pltpu
from jax.sharding import PartitionSpec as P

F32, BF16 = jnp.float32, jnp.bfloat16
NT = (((1,), (1,)), ((), ()))
LANES = 128
R = 32
SPAN = 32
GROUP = 32
GROUPS = 8
ROWS = 64
EDGE = 96
BLOCK = (R, LANES)
VMEM_LIMIT = 60 * 1024 * 1024
HALO = SPAN * R + 43 * 16


def iota(shape, dim):
    return lax.broadcasted_iota(jnp.int32, shape, dim)


def block_of(x):
    return iota(x.shape, 1) >> 5


def one_hot(made):
    return jnp.where(made, 1.0, 0.0).astype(BF16)


def rep_rows(slots, rows, column):
    shape = (slots * R, rows)
    m, j = iota(shape, 0), iota(shape, 1)
    return one_hot(j == column(m >> 5, (m & 31) >> 2))


def rep_transfer():
    return rep_rows(2, 16, lambda c, i: i * 2 + c)


def rep_upper():
    return rep_rows(3, 32, lambda k, i: k * 8 + i)


def rep_four_transfers():
    shape = (4 * 64, 64)
    m, j = iota(shape, 0), iota(shape, 1)
    return one_hot(j == (m >> 6) * 16 + ((m & 31) >> 2) * 2 + ((m >> 5) & 1))


def rep_four_uppers():
    shape = (3 * 128, 128)
    m, j = iota(shape, 0), iota(shape, 1)
    return one_hot(j == ((m >> 5) & 3) * 32 + (m >> 7) * 8 + ((m & 31) >> 2))


def rep_leaf():
    return rep_rows(8, 64, lambda k, i: i * 8 + k)


def doubled(mats):
    pieces = [mats[R * (k // 2) : R * (k // 2 + 1)] for k in range(2 * mats.shape[0] // R)]
    return jnp.concatenate(pieces, axis=0)


def fold_matrix():
    shape = (LANES, LANES)
    return one_hot((iota(shape, 0) & 31) == (iota(shape, 1) & 31))


def spread(rep, rows):
    wide = jnp.dot(rep, rows, preferred_element_type=F32)
    return jnp.where(block_of(wide) == (iota(wide.shape, 0) & 3), wide, 0.0).astype(BF16)


def settle(mats, folds):
    return jnp.dot(mats, folds, preferred_element_type=F32).astype(BF16)


def fold(x):
    x = x + pltpu.roll(x, 32, 1)
    return x + pltpu.roll(x, 64, 1)


def split(x):
    high = x.astype(BF16)
    return jnp.concatenate([high, (x - high.astype(F32)).astype(BF16)], axis=1)


def gather_matrix():
    shape = (8 * LANES, LANES)
    row, lane = iota(shape, 0), iota(shape, 1)
    return one_hot(jnp.logical_and(row >> 8 == lane >> 5, (row & 31) == (lane & 31)))


def pack(x):
    high = x.astype(BF16).astype(F32)
    return jnp.where((block_of(x) & 1) == 0, high, x - high).astype(BF16)


def halve(x):
    low, high = x[:16].astype(F32), x[16:].astype(F32)
    return jnp.where(block_of(low) < 2, low, high).astype(BF16)


def unhalve(x):
    x = x.astype(F32)
    turned = pltpu.roll(x, 64, 1)
    low = block_of(x) < 2
    return jnp.concatenate([jnp.where(low, x, turned), jnp.where(low, turned, x)], axis=0)


def side_by_side(left, right):
    left, right = left.astype(F32), right.astype(F32)
    return jnp.where(block_of(left) < 2, left, right).astype(BF16)


def join_up(left, right, mats):
    return fold(jnp.dot(side_by_side(left, right), doubled(mats), preferred_element_type=F32))


def couple(terms, mats):
    both = jnp.concatenate([side_by_side(terms[0], terms[1]), terms[2][:, : 2 * R]], axis=1)
    return jnp.dot(both, doubled(mats), preferred_element_type=F32)


def times_transposed(x, mats):
    return lax.dot_general(pack(x)[:, : 2 * R], mats[:, : 2 * R], NT, preferred_element_type=F32)


def four_times(x):
    return jnp.concatenate([x, x, x, x], axis=0)


def kernel_params(limit=VMEM_LIMIT):
    return pltpu.CompilerParams(vmem_limit_bytes=limit)


HBM = pl.BlockSpec(memory_space=pltpu.HBM)
VMEM = pl.BlockSpec(memory_space=pltpu.VMEM)
SMEM = pl.BlockSpec(memory_space=pltpu.SMEM)


def fetch(pairs, sems, first=0):
    copies = [pltpu.make_async_copy(a, b, sems.at[first + k]) for k, (a, b) in enumerate(pairs)]
    for copy in copies:
        copy.start()
    return copies


def lay_out_upper(upper, room):
    nodes = upper.shape[1]
    for slot in range(3):
        for i in range(8):
            room[pl.ds((slot * 8 + i) * nodes, nodes), :] = upper[
                slot, :, LANES * i : LANES * (i + 1)
            ].astype(F32)


def upper_rows(room, node, nodes=SPAN):
    rows = room[pl.ds(node, 24, stride=nodes), :]
    return jnp.concatenate([rows, jnp.zeros((8, LANES), F32)], axis=0).astype(BF16)


def level_base(l):
    return sum(SPAN >> k for k in range(l))


def local_up_kernel(
    trial_hbm, basis_hbm, transfer_hbm, upper_hbm, send, own_hbm, mats_hbm,
    trial, basis, transfer, upper, room, own, head, mats, sems,
):
    last = pl.ds(SPAN - 8, 8)
    copies = fetch(
        (
            (trial_hbm, trial),
            (basis_hbm, basis),
            (transfer_hbm, transfer),
            (upper_hbm.at[:, last, :], upper),
        ),
        sems,
    )
    rep = rep_four_transfers()
    for copy in copies[:2]:
        copy.wait()
    for n in range(SPAN):
        own[n] = pack(
            lax.dot_general(
                trial[R * n : R * (n + 1)], four_times(basis[n]), NT, preferred_element_type=F32
            )
        )
    leaves, nodes = pl.ds(0, SPAN), pl.ds(SPAN, SPAN - 1)
    outs = fetch([(own.at[leaves], own_hbm.at[leaves])], sems, 4)
    for copy in copies[2:]:
        copy.wait()
    for k in range(0, SPAN, 4):
        four = spread(rep, transfer[k : k + 4].reshape(64, LANES))
        mats[k : k + 4] = four.reshape(4, 64, LANES)
    outs += fetch([(mats, mats_hbm)], sems, 6 + GROUP)
    lay_out_upper(upper, room)
    head[16:32] = transfer[SPAN - 1]
    head[32:] = upper_rows(room, 7, 8)
    for l in range(1, 6):
        for j in range(SPAN >> l):
            q, child = j * 2**l + 2 ** (l - 1) - 1, level_base(l - 1) + 2 * j
            own[level_base(l) + j] = pack(join_up(own[child], own[child + 1], mats[q]))
    head[:16] = halve(own[62])
    outs += fetch(
        [(head, send.at[g]) for g in range(GROUP)] + [(own.at[nodes], own_hbm.at[nodes])], sems, 5
    )
    for copy in outs:
        copy.wait()


def local_up(trial, basis, transfer, upper):
    return pl.pallas_call(
        local_up_kernel,
        in_specs=[HBM] * 4,
        out_specs=[HBM, HBM, HBM],
        out_shape=[
            jax.ShapeDtypeStruct((GROUP, ROWS, LANES), BF16),
            jax.ShapeDtypeStruct((63, *BLOCK), BF16),
            jax.ShapeDtypeStruct((SPAN, 64, LANES), BF16),
        ],
        scratch_shapes=[
            pltpu.VMEM((SPAN * R, LANES), BF16),
            pltpu.VMEM((SPAN, *BLOCK), BF16),
            pltpu.VMEM((SPAN, 16, LANES), BF16),
            pltpu.VMEM((3, 8, 1024), BF16),
            pltpu.VMEM((24 * 8, LANES), F32),
            pltpu.VMEM((63, *BLOCK), BF16),
            pltpu.VMEM((ROWS, LANES), BF16),
            pltpu.VMEM((SPAN, 64, LANES), BF16),
            pltpu.SemaphoreType.DMA((7 + GROUP,)),
        ],
        compiler_params=kernel_params(),
        name="local_up",
    )(trial, basis, transfer, upper)


def prepare_kernel(
    trial_hbm, own_hbm, mats_hbm, upper_hbm, to_chip, to_next, transfer_out, upper_out, base_upper,
    trial, own, mats, upper, room, uppers, edges, sems,
):
    copies = fetch(
        ((trial_hbm, trial), (own_hbm, own), (mats_hbm, mats), (upper_hbm, upper)), sems
    )
    odd = lax.axis_index("leaf") & 1
    whole, rest = pl.ds(0, SPAN * R), pl.ds(SPAN * R, 16 * 43)
    copies[0].wait()
    outs = fetch(((trial, to_chip.at[whole]), (trial, to_next.at[whole])), sems, 4)
    copies[1].wait()
    for n in range(SPAN):
        half = halve(own[n])
        edges[0, 16 * n : 16 * n + 16] = half
        edges[1, 16 * n : 16 * n + 16] = half
    cursor = SPAN
    for l in range(1, 5):
        nodes = SPAN >> l
        keep = min(nodes, 3)
        for k in range(keep):
            at = level_base(l) + k
            edges[0, 16 * cursor : 16 * cursor + 16] = halve(own[at + nodes - keep])
            edges[1, 16 * cursor : 16 * cursor + 16] = halve(own[at])
            cursor += 1
    outs += fetch(
        ((edges.at[odd], to_chip.at[rest]), (edges.at[1 - odd], to_next.at[rest])), sems, 6
    )
    folds = fold_matrix()
    rep3 = rep_four_uppers()
    for copy in copies[2:]:
        copy.wait()
    lay_out_upper(upper, room)

    for k in range(0, SPAN, 4):
        rows = jnp.concatenate([upper_rows(room, k + n) for n in range(4)], axis=0)
        four = spread(rep3, rows)
        for n in range(4):
            for slot in range(3):
                at = 128 * slot + R * n
                uppers[k + n, R * slot : R * (slot + 1)] = four[at : at + R]
    for k in range(0, SPAN, 4):
        four = settle(mats[k : k + 4].reshape(256, LANES), folds)
        transfer_out[k : k + 4] = four.reshape(4, 64, LANES)
        four = settle(uppers[k : k + 4].reshape(384, LANES), folds)
        upper_out[k : k + 4] = four.reshape(4, 96, LANES)
    base_upper[...] = upper_rows(room, SPAN // 2 - 1)
    for copy in outs:
        copy.wait()


def prepare(trial, own, mats, upper):
    return pl.pallas_call(
        prepare_kernel,
        in_specs=[HBM] * 4,
        out_specs=[HBM, HBM, VMEM, VMEM, VMEM],
        out_shape=[
            jax.ShapeDtypeStruct((HALO, LANES), BF16),
            jax.ShapeDtypeStruct((HALO, LANES), BF16),
            jax.ShapeDtypeStruct((SPAN, 64, LANES), BF16),
            jax.ShapeDtypeStruct((SPAN, 96, LANES), BF16),
            jax.ShapeDtypeStruct(BLOCK, BF16),
        ],
        scratch_shapes=[
            pltpu.VMEM((SPAN * R, LANES), BF16),
            pltpu.VMEM((63, *BLOCK), BF16),
            pltpu.VMEM((SPAN, 64, LANES), BF16),
            pltpu.VMEM((3, SPAN, 1024), BF16),
            pltpu.VMEM((24 * SPAN, LANES), F32),
            pltpu.VMEM((SPAN, 96, LANES), BF16),
            pltpu.VMEM((2, 16 * 43, LANES), BF16),
            pltpu.SemaphoreType.DMA((8,)),
        ],
        compiler_params=kernel_params(),
        cost_estimate=pl.CostEstimate(flops=2**28, bytes_accessed=5 * 2**20, transcendentals=0),
        name="prepare",
    )(trial, own, mats, upper)


def source_offsets(j):
    odd = j & 1
    return (-2 - odd, 2 - 4 * odd, 3 - odd)


def edge_level(place):
    return sum(jnp.where(place >= 2**g, 1, 0) for g in range(1, 5))


def group_up_kernel(got, send, mine, inside, mats):
    rep = rep_four_transfers()
    for k in range(0, GROUP, 4):
        rows = jnp.concatenate([got[k + n, 16:32] for n in range(4)], axis=0)
        mats[k : k + 4] = spread(rep, rows).reshape(4, 64, LANES)
    for e in range(GROUP):
        inside[e] = unhalve(got[e, :16]).astype(BF16)
    for g in range(1, 6):
        for j in range(GROUP >> g):
            owner = (2 * j + 1) * 2 ** (g - 1) - 1
            child = level_base(g - 1) + 2 * j
            inside[level_base(g) + j] = pack(join_up(inside[child], inside[child + 1], mats[owner]))
    device = lax.axis_index("leaf")
    place = lax.rem(device, GROUP)
    group = device // GROUP
    right = [level_base(g) + (GROUP >> g) - 2 for g in range(5)]
    right.append(63 - lax.shift_right_logical(32, edge_level(place)))
    left = [level_base(g) + 1 for g in range(5)]
    left.append(64 - lax.shift_right_logical(64, edge_level(GROUP - 1 - place)))
    head = jnp.concatenate([halve(inside[62]), got[GROUP - 1, 16:]], axis=0)
    to_left = jnp.concatenate([halve(inside[k]) for k in left], axis=0)
    for g in range(GROUPS):
        send[g, :ROWS] = head
        send[g, ROWS:] = to_left
    after_this = jnp.minimum(group + 1, GROUPS - 1)
    inside[63] = jnp.zeros(BLOCK, BF16)
    for g in range(5):
        j, nodes = place >> g, GROUP >> g
        for k, offset in enumerate(source_offsets(j)):
            at = j + offset
            ok = jnp.logical_and(at >= 0, at < nodes)
            mine[144 * g + R * k : 144 * g + R * (k + 1)] = inside[jnp.where(ok, level_base(g) + at, 63)]
        mine[144 * g + 96 : 144 * (g + 1)] = got[((place >> (g + 1)) * 2 + 1) * 2**g - 1, 16:]
    send[after_this, ROWS:] = jnp.concatenate([halve(inside[k]) for k in right], axis=0)


def group_up(got):
    return pl.pallas_call(
        group_up_kernel,
        out_shape=[
            jax.ShapeDtypeStruct((GROUPS, ROWS + EDGE, LANES), BF16),
            jax.ShapeDtypeStruct((5 * 144, LANES), BF16),
        ],
        scratch_shapes=[pltpu.VMEM((64, *BLOCK), BF16), pltpu.VMEM((GROUP, 64, LANES), BF16)],
        compiler_params=kernel_params(16 * 1024 * 1024),
        cost_estimate=pl.CostEstimate(flops=2**31, bytes_accessed=2**25, transcendentals=0),
        name="group_up",
    )(got)


def source_row(src, count, row, slot, first):
    near = src[slot, row] - first
    near = jnp.minimum(jnp.maximum(near, 0), 3 * SPAN - 1)
    return jnp.where(slot < count[row], near, 3 * SPAN)


PIECES = 8


def middle_kernel(
    src, count, near_src, near_count, trial_hbm, own_hbm, chip_hbm, next_hbm, leaf_hbm, transfer_hbm,
    upper_hbm, blocks_hbm, after, part_out, pass_out, near_out,
    own, sides, leaf_rows, transfer, upper, blocks, trials, held, downs, coupled, sems,
):
    first = (lax.axis_index("leaf") - 1) * SPAN
    rest = pl.ds(SPAN * R, 16 * 43)
    whole = pl.ds(0, SPAN * R)
    odd = lax.axis_index("leaf") & 1

    def trial_place(third):
        return trials.at[pl.ds(pl.multiple_of(third * (SPAN * R), SPAN * R), SPAN * R)]

    copies = fetch(
        (
            (chip_hbm.at[rest], sides.at[1 - odd]),
            (own_hbm, own),
            (next_hbm.at[rest], sides.at[odd]),
            (transfer_hbm, transfer),
            (upper_hbm, upper),
            (leaf_hbm, leaf_rows),
            (chip_hbm.at[whole], trial_place(2 - 2 * odd)),
            (trial_hbm, trial_place(1)),
            (next_hbm.at[whole], trial_place(2 * odd)),
        ),
        sems,
    )
    size = SPAN // PIECES
    pieces = fetch(
        [
            (blocks_hbm.at[pl.ds(size * k, size)], blocks.at[pl.ds(size * k, size)])
            for k in range(PIECES)
        ],
        sems,
        len(copies),
    )
    held[3 * SPAN] = jnp.zeros(BLOCK, BF16)
    trials[3 * SPAN * R :] = jnp.zeros(BLOCK, BF16)
    shape = BLOCK
    eye = jnp.where(iota(shape, 0) == (iota(shape, 1) & 31), 1.0, 0.0)
    zero = jnp.zeros(shape, F32)
    downs[62] = jnp.concatenate([zero, eye], axis=0)
    for copy in copies[:5]:
        copy.wait()

    def edge(side, k):
        return unhalve(sides[side, 16 * k : 16 * k + 16]).astype(BF16)

    for n in range(SPAN):
        held[n] = edge(0, n)
        held[SPAN + n] = own[n]
        held[2 * SPAN + n] = edge(1, n)
    cursor = {}
    at = SPAN
    for l in range(1, 5):
        cursor[l] = at
        at += min(SPAN >> l, 3)
    for l in range(5, 0, -1):
        nodes = SPAN >> l
        for j in range(nodes):
            q = j * 2**l + 2 ** (l - 1) - 1
            mats = transfer[q]
            wide = jnp.concatenate([four_times(mats[:R]), four_times(mats[R:])], axis=0)
            y = times_transposed(downs[level_base(l) + j], wide)
            for c in range(2):
                part = y[:, LANES * c : LANES * (c + 1)]
                child, k = 2 * j + c, l - 1
                if k > 0:
                    n = SPAN >> k
                    keep = min(n, 3)

                    def coef(i):
                        if i < 0:
                            return edge(0, cursor[k] + keep + i)
                        if i >= n:
                            return edge(1, cursor[k] + i - n)
                        return own[level_base(k) + i]

                    offsets = (-2, 2, 3) if child % 2 == 0 else (-3, -2, 2)
                    m = upper[child * 2**k + 2 ** (k - 1) - 1]
                    got = couple([coef(child + i) for i in offsets], m)
                    part = part + jnp.concatenate([got, zero], axis=0)
                downs[level_base(k) + child] = part
    copies[5].wait()
    low = jnp.where((iota(BLOCK, 1) >> 6) == 0, 1.0, 0.0).astype(BF16)
    high = jnp.where((iota(BLOCK, 1) >> 6) == 1, 1.0, 0.0).astype(BF16)

    rep8 = rep_leaf()

    def leaf(n, carry):
        mats = spread(rep8, leaf_rows[n])
        picked = [held[source_row(src, count, n, k, first)] for k in range(8)]
        row = jnp.concatenate(
            [picked[2 * h] * low + picked[2 * h + 1] * high for h in range(4)], axis=1
        )
        coupled[n] = jnp.dot(row, doubled(mats), preferred_element_type=F32)
        return carry

    lax.fori_loop(0, SPAN, leaf, 0, unroll=8)
    at = block_of(zero)
    gather = gather_matrix()
    for m in range(8):
        x = [downs[4 * m + k] for k in range(4)]
        both = [
            jnp.where(at == 0, a, jnp.where(at == 1, b, jnp.where(at == 2, c, d)))
            for a, b, c, d in ([v[:R] for v in x], [v[R:] for v in x])
        ]
        wide = [split(coupled[4 * m + k]) for k in range(4)]
        part_out[m] = both[0] + jnp.dot(
            jnp.concatenate(wide, axis=1), gather, preferred_element_type=F32
        )
        high_part = both[1].astype(BF16)
        low_part = (both[1] - high_part.astype(F32)).astype(BF16)
        pass_out[m] = jnp.concatenate(
            [high_part, high_part, low_part, jnp.zeros(shape, BF16)], axis=0
        )
    for copy in copies[6:]:
        copy.wait()

    def near(n, carry):
        picked = []
        for k in range(8):
            row = pl.multiple_of(source_row(near_src, near_count, n, k, first) * R, R)
            picked.append(trials[pl.ds(row, R), :])
        near_out[n] = jnp.dot(
            jnp.concatenate(picked, axis=1),
            blocks[n].reshape(8 * LANES, LANES),
            preferred_element_type=F32,
        )
        return carry

    for k in range(PIECES):
        pieces[k].wait()
        lax.fori_loop(size * k, size * (k + 1), near, 0, unroll=size)


def middle(src, count, near_src, near_count, trial, own, chip_halo, next_halo, leaf_rows, transfer, upper, blocks, after):
    return pl.pallas_call(
        middle_kernel,
        in_specs=[SMEM] * 4 + [HBM] * 9,
        out_shape=[
            jax.ShapeDtypeStruct((8, *BLOCK), F32),
            jax.ShapeDtypeStruct((8, LANES, LANES), BF16),
            jax.ShapeDtypeStruct((SPAN, *BLOCK), F32),
        ],
        scratch_shapes=[
            pltpu.VMEM((63, *BLOCK), BF16),
            pltpu.VMEM((2, 16 * 43, LANES), BF16),
            pltpu.VMEM((SPAN, 64, LANES), BF16),
            pltpu.VMEM((SPAN, 64, LANES), BF16),
            pltpu.VMEM((SPAN, 96, LANES), BF16),
            pltpu.VMEM((SPAN, 8, LANES, LANES), BF16),
            pltpu.VMEM(((3 * SPAN + 1) * R, LANES), BF16),
            pltpu.VMEM((3 * SPAN + 1, *BLOCK), BF16),
            pltpu.VMEM((63, 2 * R, LANES), F32),
            pltpu.VMEM((SPAN, *BLOCK), F32),
            pltpu.SemaphoreType.DMA((9 + PIECES,)),
        ],
        compiler_params=kernel_params(),
        cost_estimate=pl.CostEstimate(flops=2**36, bytes_accessed=2**29, transcendentals=0),
        name="middle",
    )(src, count, near_src, near_count, trial, own, chip_halo, next_halo, leaf_rows, transfer, upper, blocks, after)


def down_kernel(
    groups_hbm, mine_hbm, base_hbm, basis_hbm, parts_hbm, passes_hbm, near_hbm, out_hbm,
    groups, mine, base_upper, tree, side, basis, parts, passes, near, out, sems,
):
    device = lax.axis_index("leaf")
    place = lax.rem(device, GROUP)
    group = device // GROUP
    early = fetch(((groups_hbm, groups), (mine_hbm, mine), (base_hbm, base_upper)), sems)
    late = fetch(
        ((parts_hbm, parts), (passes_hbm, passes), (basis_hbm, basis), (near_hbm, near)), sems, 3
    )
    folds, rep2, rep3 = fold_matrix(), rep_transfer(), rep_upper()
    for copy in early:
        copy.wait()
    for e in range(GROUPS):
        tree[e] = unhalve(groups[e, :16]).astype(BF16)
    for j in range(4):
        mats = spread(rep2, groups[2 * j, 16:32])
        tree[8 + j] = pack(join_up(tree[2 * j], tree[2 * j + 1], mats))
    tree[12] = jnp.zeros(BLOCK, BF16)
    top_path = groups[(group >> 1) * 2, 16:64]
    before, behind = jnp.maximum(group - 1, 0), jnp.minimum(group + 1, GROUPS - 1)
    has_before = jnp.where(group > 0, 1.0, 0.0)
    has_behind = jnp.where(group < GROUPS - 1, 1.0, 0.0)
    edges = []
    for k in range(6):
        rows = slice(ROWS + 16 * k, ROWS + 16 * (k + 1))
        edges.append(
            (
                (unhalve(groups[before, rows]) * has_before).astype(BF16),
                (unhalve(groups[behind, rows]) * has_behind).astype(BF16),
            )
        )
    for g in range(5):
        side[g, 0] = jnp.zeros(BLOCK, BF16)
        side[g, 1], side[g, 2] = edges[g][0], edges[5][0]
        side[g, 3], side[g, 4] = edges[5][1], edges[g][1]

    top = []
    for g in range(7):
        rows = base_upper[...] if g == 0 else mine[144 * g - 32 : 144 * g] if g < 6 else top_path[16:]
        sources = []
        if g < 5:
            j, nodes = place >> g, GROUP >> g
            for k, offset in enumerate(source_offsets(j)):
                at = j + offset
                pick = jnp.where(at < 0, at + 3, jnp.where(at < nodes, 0, at - nodes + 3))
                sources.append(mine[144 * g + R * k : 144 * g + R * (k + 1)] + side[g, pick])
        else:
            j, nodes = group >> (g - 5), GROUPS >> (g - 5)
            for offset in source_offsets(j):
                at = j + offset
                ok = jnp.logical_and(at >= 0, at < nodes)
                sources.append(tree[jnp.where(ok, (0, 8)[g - 5] + at, 12)])
        top.append(fold(couple(sources, spread(rep3, rows))))

    down = top[6]
    for g in range(6, 0, -1):
        rows = mine[144 * g - 48 : 144 * g - 32] if g < 6 else top_path[:16]
        mats = settle(spread(rep2, rows), folds)
        odd = jnp.broadcast_to((device >> (g - 1)) & 1, BLOCK)
        mats = jnp.where(odd == 1, mats[R:].astype(F32), mats[:R].astype(F32)).astype(BF16)
        down = top[g - 1] + times_transposed(down, four_times(mats))

    packed = pack(down).astype(F32)
    packed = jnp.where(block_of(down) < 3, packed, 0.0).astype(BF16)
    for copy in late:
        copy.wait()
    at = block_of(down)
    stores = []
    for m in range(8):
        x = parts[m] + jnp.dot(packed, passes[m], preferred_element_type=F32)
        x = x.astype(BF16).astype(F32)
        rows = jnp.concatenate([jnp.where(at == k, x, 0.0) for k in range(4)], axis=0)
        far = jnp.dot(
            rows.astype(BF16), basis[4 * m : 4 * m + 4].reshape(LANES, LANES), preferred_element_type=F32
        )
        for k in range(4):
            out[4 * m + k] = near[4 * m + k] + far[R * k : R * (k + 1)]
        stores += fetch(((out.at[pl.ds(4 * m, 4)], out_hbm.at[pl.ds(4 * m, 4)]),), sems, 7 + m)
    for copy in stores:
        copy.wait()


def down_all(groups, mine, base_upper, basis, parts, passes, near):
    return pl.pallas_call(
        down_kernel,
        in_specs=[HBM] * 7,
        out_specs=HBM,
        out_shape=jax.ShapeDtypeStruct((SPAN, *BLOCK), F32),
        scratch_shapes=[
            pltpu.VMEM((GROUPS, ROWS + EDGE, LANES), BF16),
            pltpu.VMEM((5 * 144, LANES), BF16),
            pltpu.VMEM(BLOCK, BF16),
            pltpu.VMEM((13, *BLOCK), BF16),
            pltpu.VMEM((5, 5, *BLOCK), BF16),
            pltpu.VMEM((SPAN, *BLOCK), BF16),
            pltpu.VMEM((8, *BLOCK), F32),
            pltpu.VMEM((8, LANES, LANES), BF16),
            pltpu.VMEM((SPAN, *BLOCK), F32),
            pltpu.VMEM((SPAN, *BLOCK), F32),
            pltpu.SemaphoreType.DMA((15,)),
        ],
        compiler_params=kernel_params(),
        name="down_all",
    )(groups, mine, base_upper, basis, parts, passes, near)


def swapped(x, first, devices):
    lower = range(first, devices - 1, 2)
    return lax.ppermute(x, "leaf", [(i, i + 1) for i in lower] + [(i + 1, i) for i in lower])


def on_device(
    devices,
    trial_vectors,
    leaf_basis,
    near_blocks,
    near_src,
    near_count,
    couple_src,
    couple_count,
    couple_leaf,
    transfer,
    couple_upper,
):
    transfer_rows = transfer.reshape(SPAN, 2, 8, LANES).transpose(0, 2, 1, 3).reshape(SPAN, 16, LANES)
    leaf_rows = couple_leaf.reshape(SPAN, 8, 8, LANES).transpose(0, 2, 1, 3).reshape(SPAN, 64, LANES)
    upper_slots = couple_upper.transpose(1, 0, 2)

    in_row = [list(range(g * GROUP, (g + 1) * GROUP)) for g in range(GROUPS)]
    across = [list(range(g, devices, GROUP)) for g in range(GROUP)]
    exchange = functools.partial(lax.all_to_all, axis_name="leaf", split_axis=0, concat_axis=0, tiled=True)

    trial_rows = trial_vectors.reshape(SPAN * R, LANES)
    send, own, spread_mats = local_up(trial_rows, leaf_basis, transfer_rows, upper_slots)
    got = exchange(send, axis_index_groups=in_row)
    to_chip, to_next, transfer_mats, upper_mats, base_upper = prepare(
        trial_rows, own, spread_mats, upper_slots
    )
    chip_halo = swapped(to_chip, 0, devices)
    next_halo = swapped(to_next, 1, devices)
    group_send, mine = group_up(got)
    groups = exchange(group_send, axis_index_groups=across)
    parts, passes, near = middle(
        couple_src.T, couple_count, near_src.T, near_count, trial_rows, own, chip_halo, next_halo,
        leaf_rows, transfer_mats, upper_mats, near_blocks, mine,
    )
    return down_all(groups, mine, base_upper, leaf_basis, parts, passes, near)


def solution(mesh):
    placed = (
        P("leaf", None, None),
        P("leaf", None, None),
        P("leaf", None, None, None),
        P("leaf", None),
        P("leaf"),
        P("leaf", None),
        P("leaf"),
        P("leaf", None, None),
        P("leaf", None, None),
        P("leaf", None, None),
    )
    return jax.shard_map(
        functools.partial(on_device, mesh.shape["leaf"]),
        mesh=mesh,
        in_specs=placed,
        out_specs=P("leaf", None, None),
        check_vma=False,
    )
```

```python
import functools

import jax
import jax.numpy as jnp
from jax import lax
from jax.experimental import pallas as pl
from jax.experimental.pallas import tpu as pltpu
from jax.sharding import PartitionSpec as P

F32, BF16 = jnp.float32, jnp.bfloat16
NT = (((1,), (1,)), ((), ()))
LANES = 128
R = 32
SPAN = 32
GROUP = 32
GROUPS = 8
ROWS = 64
EDGE = 96
BLOCK = (R, LANES)
VMEM_LIMIT = 60 * 1024 * 1024
HALO = SPAN * R + 43 * 16


def iota(shape, dim):
    return lax.broadcasted_iota(jnp.int32, shape, dim)


def block_of(x):
    return iota(x.shape, 1) >> 5


def one_hot(made):
    return jnp.where(made, 1.0, 0.0).astype(BF16)


def rep_rows(slots, rows, column):
    shape = (slots * R, rows)
    m, j = iota(shape, 0), iota(shape, 1)
    return one_hot(j == column(m >> 5, (m & 31) >> 2))


def rep_transfer():
    return rep_rows(2, 16, lambda c, i: i * 2 + c)


def rep_upper():
    return rep_rows(3, 32, lambda k, i: k * 8 + i)


def rep_four_transfers():
    shape = (4 * 64, 64)
    m, j = iota(shape, 0), iota(shape, 1)
    return one_hot(j == (m >> 6) * 16 + ((m & 31) >> 2) * 2 + ((m >> 5) & 1))


def rep_four_uppers():
    shape = (3 * 128, 128)
    m, j = iota(shape, 0), iota(shape, 1)
    return one_hot(j == ((m >> 5) & 3) * 32 + (m >> 7) * 8 + ((m & 31) >> 2))


def rep_leaf():
    return rep_rows(8, 64, lambda k, i: i * 8 + k)


def doubled(mats):
    pieces = [mats[R * (k // 2) : R * (k // 2 + 1)] for k in range(2 * mats.shape[0] // R)]
    return jnp.concatenate(pieces, axis=0)


def fold_matrix():
    shape = (LANES, LANES)
    return one_hot((iota(shape, 0) & 31) == (iota(shape, 1) & 31))


def spread(rep, rows):
    wide = jnp.dot(rep, rows, preferred_element_type=F32)
    return jnp.where(block_of(wide) == (iota(wide.shape, 0) & 3), wide, 0.0).astype(BF16)


def settle(mats, folds):
    return jnp.dot(mats, folds, preferred_element_type=F32).astype(BF16)


def fold(x):
    x = x + pltpu.roll(x, 32, 1)
    return x + pltpu.roll(x, 64, 1)


def split(x):
    high = x.astype(BF16)
    return jnp.concatenate([high, (x - high.astype(F32)).astype(BF16)], axis=1)


def gather_matrix():
    shape = (8 * LANES, LANES)
    row, lane = iota(shape, 0), iota(shape, 1)
    return one_hot(jnp.logical_and(row >> 8 == lane >> 5, (row & 31) == (lane & 31)))


def pack(x):
    high = x.astype(BF16).astype(F32)
    return jnp.where((block_of(x) & 1) == 0, high, x - high).astype(BF16)


def halve(x):
    low, high = x[:16].astype(F32), x[16:].astype(F32)
    return jnp.where(block_of(low) < 2, low, high).astype(BF16)


def unhalve(x):
    x = x.astype(F32)
    turned = pltpu.roll(x, 64, 1)
    low = block_of(x) < 2
    return jnp.concatenate([jnp.where(low, x, turned), jnp.where(low, turned, x)], axis=0)


def side_by_side(left, right):
    left, right = left.astype(F32), right.astype(F32)
    return jnp.where(block_of(left) < 2, left, right).astype(BF16)


def join_up(left, right, mats):
    return fold(jnp.dot(side_by_side(left, right), doubled(mats), preferred_element_type=F32))


def couple(terms, mats):
    both = jnp.concatenate([side_by_side(terms[0], terms[1]), terms[2][:, : 2 * R]], axis=1)
    return jnp.dot(both, doubled(mats), preferred_element_type=F32)


def times_transposed(x, mats):
    return lax.dot_general(pack(x)[:, : 2 * R], mats[:, : 2 * R], NT, preferred_element_type=F32)


def four_times(x):
    return jnp.concatenate([x, x, x, x], axis=0)


def kernel_params(limit=VMEM_LIMIT):
    return pltpu.CompilerParams(vmem_limit_bytes=limit)


HBM = pl.BlockSpec(memory_space=pltpu.HBM)
VMEM = pl.BlockSpec(memory_space=pltpu.VMEM)
SMEM = pl.BlockSpec(memory_space=pltpu.SMEM)


def fetch(pairs, sems, first=0):
    copies = [pltpu.make_async_copy(a, b, sems.at[first + k]) for k, (a, b) in enumerate(pairs)]
    for copy in copies:
        copy.start()
    return copies


def lay_out_upper(upper, room):
    nodes = upper.shape[1]
    for slot in range(3):
        for i in range(8):
            room[pl.ds((slot * 8 + i) * nodes, nodes), :] = upper[
                slot, :, LANES * i : LANES * (i + 1)
            ].astype(F32)


def upper_rows(room, node, nodes=SPAN):
    rows = room[pl.ds(node, 24, stride=nodes), :]
    return jnp.concatenate([rows, jnp.zeros((8, LANES), F32)], axis=0).astype(BF16)


def level_base(l):
    return sum(SPAN >> k for k in range(l))


def local_up_kernel(
    trial_hbm, basis_hbm, transfer_hbm, upper_hbm, send, own_hbm, mats_hbm,
    trial, basis, transfer, upper, room, own, head, mats, sems,
):
    last = pl.ds(SPAN - 8, 8)
    copies = fetch(
        (
            (trial_hbm, trial),
            (basis_hbm, basis),
            (transfer_hbm, transfer),
            (upper_hbm.at[:, last, :], upper),
        ),
        sems,
    )
    rep = rep_four_transfers()
    for copy in copies[:2]:
        copy.wait()
    for n in range(SPAN):
        own[n] = pack(
            lax.dot_general(
                trial[R * n : R * (n + 1)], four_times(basis[n]), NT, preferred_element_type=F32
            )
        )
    leaves, nodes = pl.ds(0, SPAN), pl.ds(SPAN, SPAN - 1)
    outs = fetch([(own.at[leaves], own_hbm.at[leaves])], sems, 4)
    for copy in copies[2:]:
        copy.wait()
    for k in range(0, SPAN, 4):
        four = spread(rep, transfer[k : k + 4].reshape(64, LANES))
        mats[k : k + 4] = four.reshape(4, 64, LANES)
    outs += fetch([(mats, mats_hbm)], sems, 6 + GROUP)
    lay_out_upper(upper, room)
    head[16:32] = transfer[SPAN - 1]
    head[32:] = upper_rows(room, 7, 8)
    for l in range(1, 6):
        for j in range(SPAN >> l):
            q, child = j * 2**l + 2 ** (l - 1) - 1, level_base(l - 1) + 2 * j
            own[level_base(l) + j] = pack(join_up(own[child], own[child + 1], mats[q]))
    head[:16] = halve(own[62])
    outs += fetch(
        [(head, send.at[g]) for g in range(GROUP)] + [(own.at[nodes], own_hbm.at[nodes])], sems, 5
    )
    for copy in outs:
        copy.wait()


def local_up(trial, basis, transfer, upper):
    return pl.pallas_call(
        local_up_kernel,
        in_specs=[HBM] * 4,
        out_specs=[HBM, HBM, HBM],
        out_shape=[
            jax.ShapeDtypeStruct((GROUP, ROWS, LANES), BF16),
            jax.ShapeDtypeStruct((63, *BLOCK), BF16),
            jax.ShapeDtypeStruct((SPAN, 64, LANES), BF16),
        ],
        scratch_shapes=[
            pltpu.VMEM((SPAN * R, LANES), BF16),
            pltpu.VMEM((SPAN, *BLOCK), BF16),
            pltpu.VMEM((SPAN, 16, LANES), BF16),
            pltpu.VMEM((3, 8, 1024), BF16),
            pltpu.VMEM((24 * 8, LANES), F32),
            pltpu.VMEM((63, *BLOCK), BF16),
            pltpu.VMEM((ROWS, LANES), BF16),
            pltpu.VMEM((SPAN, 64, LANES), BF16),
            pltpu.SemaphoreType.DMA((7 + GROUP,)),
        ],
        compiler_params=kernel_params(),
        name="local_up",
    )(trial, basis, transfer, upper)


def prepare_kernel(
    trial_hbm, own_hbm, mats_hbm, upper_hbm, to_chip, to_next, transfer_out, upper_out, base_upper,
    trial, own, mats, upper, room, uppers, edges, sems,
):
    copies = fetch(
        ((trial_hbm, trial), (own_hbm, own), (mats_hbm, mats), (upper_hbm, upper)), sems
    )
    odd = lax.axis_index("leaf") & 1
    whole, rest = pl.ds(0, SPAN * R), pl.ds(SPAN * R, 16 * 43)
    copies[0].wait()
    outs = fetch(((trial, to_chip.at[whole]), (trial, to_next.at[whole])), sems, 4)
    copies[1].wait()
    for n in range(SPAN):
        half = halve(own[n])
        edges[0, 16 * n : 16 * n + 16] = half
        edges[1, 16 * n : 16 * n + 16] = half
    cursor = SPAN
    for l in range(1, 5):
        nodes = SPAN >> l
        keep = min(nodes, 3)
        for k in range(keep):
            at = level_base(l) + k
            edges[0, 16 * cursor : 16 * cursor + 16] = halve(own[at + nodes - keep])
            edges[1, 16 * cursor : 16 * cursor + 16] = halve(own[at])
            cursor += 1
    outs += fetch(
        ((edges.at[odd], to_chip.at[rest]), (edges.at[1 - odd], to_next.at[rest])), sems, 6
    )
    folds = fold_matrix()
    rep3 = rep_four_uppers()
    for copy in copies[2:]:
        copy.wait()
    lay_out_upper(upper, room)

    for k in range(0, SPAN, 4):
        rows = jnp.concatenate([upper_rows(room, k + n) for n in range(4)], axis=0)
        four = spread(rep3, rows)
        for n in range(4):
            for slot in range(3):
                at = 128 * slot + R * n
                uppers[k + n, R * slot : R * (slot + 1)] = four[at : at + R]
    for k in range(0, SPAN, 4):
        four = settle(mats[k : k + 4].reshape(256, LANES), folds)
        transfer_out[k : k + 4] = four.reshape(4, 64, LANES)
        four = settle(uppers[k : k + 4].reshape(384, LANES), folds)
        upper_out[k : k + 4] = four.reshape(4, 96, LANES)
    base_upper[...] = upper_rows(room, SPAN // 2 - 1)
    for copy in outs:
        copy.wait()


def prepare(trial, own, mats, upper):
    return pl.pallas_call(
        prepare_kernel,
        in_specs=[HBM] * 4,
        out_specs=[HBM, HBM, VMEM, VMEM, VMEM],
        out_shape=[
            jax.ShapeDtypeStruct((HALO, LANES), BF16),
            jax.ShapeDtypeStruct((HALO, LANES), BF16),
            jax.ShapeDtypeStruct((SPAN, 64, LANES), BF16),
            jax.ShapeDtypeStruct((SPAN, 96, LANES), BF16),
            jax.ShapeDtypeStruct(BLOCK, BF16),
        ],
        scratch_shapes=[
            pltpu.VMEM((SPAN * R, LANES), BF16),
            pltpu.VMEM((63, *BLOCK), BF16),
            pltpu.VMEM((SPAN, 64, LANES), BF16),
            pltpu.VMEM((3, SPAN, 1024), BF16),
            pltpu.VMEM((24 * SPAN, LANES), F32),
            pltpu.VMEM((SPAN, 96, LANES), BF16),
            pltpu.VMEM((2, 16 * 43, LANES), BF16),
            pltpu.SemaphoreType.DMA((8,)),
        ],
        compiler_params=kernel_params(),
        cost_estimate=pl.CostEstimate(flops=2**28, bytes_accessed=5 * 2**20, transcendentals=0),
        name="prepare",
    )(trial, own, mats, upper)


def source_offsets(j):
    odd = j & 1
    return (-2 - odd, 2 - 4 * odd, 3 - odd)


def edge_level(place):
    return sum(jnp.where(place >= 2**g, 1, 0) for g in range(1, 5))


def group_up_kernel(got, send, mine, inside, mats):
    rep = rep_four_transfers()
    for k in range(0, GROUP, 4):
        rows = jnp.concatenate([got[k + n, 16:32] for n in range(4)], axis=0)
        mats[k : k + 4] = spread(rep, rows).reshape(4, 64, LANES)
    for e in range(GROUP):
        inside[e] = unhalve(got[e, :16]).astype(BF16)
    for g in range(1, 6):
        for j in range(GROUP >> g):
            owner = (2 * j + 1) * 2 ** (g - 1) - 1
            child = level_base(g - 1) + 2 * j
            inside[level_base(g) + j] = pack(join_up(inside[child], inside[child + 1], mats[owner]))
    device = lax.axis_index("leaf")
    place = lax.rem(device, GROUP)
    group = device // GROUP
    right = [level_base(g) + (GROUP >> g) - 2 for g in range(5)]
    right.append(63 - lax.shift_right_logical(32, edge_level(place)))
    left = [level_base(g) + 1 for g in range(5)]
    left.append(64 - lax.shift_right_logical(64, edge_level(GROUP - 1 - place)))
    head = jnp.concatenate([halve(inside[62]), got[GROUP - 1, 16:]], axis=0)
    to_left = jnp.concatenate([halve(inside[k]) for k in left], axis=0)
    for g in range(GROUPS):
        send[g, :ROWS] = head
        send[g, ROWS:] = to_left
    after_this = jnp.minimum(group + 1, GROUPS - 1)
    inside[63] = jnp.zeros(BLOCK, BF16)
    for g in range(5):
        j, nodes = place >> g, GROUP >> g
        for k, offset in enumerate(source_offsets(j)):
            at = j + offset
            ok = jnp.logical_and(at >= 0, at < nodes)
            mine[144 * g + R * k : 144 * g + R * (k + 1)] = inside[jnp.where(ok, level_base(g) + at, 63)]
        mine[144 * g + 96 : 144 * (g + 1)] = got[((place >> (g + 1)) * 2 + 1) * 2**g - 1, 16:]
    send[after_this, ROWS:] = jnp.concatenate([halve(inside[k]) for k in right], axis=0)


def group_up(got):
    return pl.pallas_call(
        group_up_kernel,
        out_shape=[
            jax.ShapeDtypeStruct((GROUPS, ROWS + EDGE, LANES), BF16),
            jax.ShapeDtypeStruct((5 * 144, LANES), BF16),
        ],
        scratch_shapes=[pltpu.VMEM((64, *BLOCK), BF16), pltpu.VMEM((GROUP, 64, LANES), BF16)],
        compiler_params=kernel_params(16 * 1024 * 1024),
        cost_estimate=pl.CostEstimate(flops=2**31, bytes_accessed=2**25, transcendentals=0),
        name="group_up",
    )(got)


def source_row(src, count, row, slot, first):
    near = src[slot, row] - first
    near = jnp.minimum(jnp.maximum(near, 0), 3 * SPAN - 1)
    return jnp.where(slot < count[row], near, 3 * SPAN)


PIECES = 4


def middle_kernel(
    src, count, near_src, near_count, trial_hbm, own_hbm, chip_hbm, next_hbm, leaf_hbm, transfer_hbm,
    upper_hbm, blocks_hbm, after, part_out, pass_out, near_out,
    own, sides, leaf_rows, transfer, upper, blocks, trials, held, downs, coupled, sems,
):
    first = (lax.axis_index("leaf") - 1) * SPAN
    rest = pl.ds(SPAN * R, 16 * 43)
    whole = pl.ds(0, SPAN * R)
    odd = lax.axis_index("leaf") & 1

    def trial_place(third):
        return trials.at[pl.ds(pl.multiple_of(third * (SPAN * R), SPAN * R), SPAN * R)]

    copies = fetch(
        (
            (chip_hbm.at[rest], sides.at[1 - odd]),
            (own_hbm, own),
            (next_hbm.at[rest], sides.at[odd]),
            (transfer_hbm, transfer),
            (upper_hbm, upper),
            (leaf_hbm, leaf_rows),
            (chip_hbm.at[whole], trial_place(2 - 2 * odd)),
            (trial_hbm, trial_place(1)),
            (next_hbm.at[whole], trial_place(2 * odd)),
        ),
        sems,
    )
    size = SPAN // PIECES
    pieces = fetch(
        [
            (blocks_hbm.at[pl.ds(size * k, size)], blocks.at[pl.ds(size * k, size)])
            for k in range(PIECES)
        ],
        sems,
        len(copies),
    )
    held[3 * SPAN] = jnp.zeros(BLOCK, BF16)
    trials[3 * SPAN * R :] = jnp.zeros(BLOCK, BF16)
    shape = BLOCK
    eye = jnp.where(iota(shape, 0) == (iota(shape, 1) & 31), 1.0, 0.0)
    zero = jnp.zeros(shape, F32)
    downs[62] = jnp.concatenate([zero, eye], axis=0)
    for copy in copies[:5]:
        copy.wait()

    def edge(side, k):
        return unhalve(sides[side, 16 * k : 16 * k + 16]).astype(BF16)

    for n in range(SPAN):
        held[n] = edge(0, n)
        held[SPAN + n] = own[n]
        held[2 * SPAN + n] = edge(1, n)
    cursor = {}
    at = SPAN
    for l in range(1, 5):
        cursor[l] = at
        at += min(SPAN >> l, 3)
    for l in range(5, 0, -1):
        nodes = SPAN >> l
        for j in range(nodes):
            q = j * 2**l + 2 ** (l - 1) - 1
            mats = transfer[q]
            wide = jnp.concatenate([four_times(mats[:R]), four_times(mats[R:])], axis=0)
            y = times_transposed(downs[level_base(l) + j], wide)
            for c in range(2):
                part = y[:, LANES * c : LANES * (c + 1)]
                child, k = 2 * j + c, l - 1
                if k > 0:
                    n = SPAN >> k
                    keep = min(n, 3)

                    def coef(i):
                        if i < 0:
                            return edge(0, cursor[k] + keep + i)
                        if i >= n:
                            return edge(1, cursor[k] + i - n)
                        return own[level_base(k) + i]

                    offsets = (-2, 2, 3) if child % 2 == 0 else (-3, -2, 2)
                    m = upper[child * 2**k + 2 ** (k - 1) - 1]
                    got = couple([coef(child + i) for i in offsets], m)
                    part = part + jnp.concatenate([got, zero], axis=0)
                downs[level_base(k) + child] = part
    copies[5].wait()
    low = jnp.where((iota(BLOCK, 1) >> 6) == 0, 1.0, 0.0).astype(BF16)
    high = jnp.where((iota(BLOCK, 1) >> 6) == 1, 1.0, 0.0).astype(BF16)

    rep8 = rep_leaf()

    def leaf(n, carry):
        mats = spread(rep8, leaf_rows[n])
        picked = [held[source_row(src, count, n, k, first)] for k in range(8)]
        row = jnp.concatenate(
            [picked[2 * h] * low + picked[2 * h + 1] * high for h in range(4)], axis=1
        )
        coupled[n] = jnp.dot(row, doubled(mats), preferred_element_type=F32)
        return carry

    lax.fori_loop(0, SPAN, leaf, 0, unroll=16)
    at = block_of(zero)
    gather = gather_matrix()
    for m in range(8):
        x = [downs[4 * m + k] for k in range(4)]
        both = [
            jnp.where(at == 0, a, jnp.where(at == 1, b, jnp.where(at == 2, c, d)))
            for a, b, c, d in ([v[:R] for v in x], [v[R:] for v in x])
        ]
        wide = [split(coupled[4 * m + k]) for k in range(4)]
        part_out[m] = both[0] + jnp.dot(
            jnp.concatenate(wide, axis=1), gather, preferred_element_type=F32
        )
        high_part = both[1].astype(BF16)
        low_part = (both[1] - high_part.astype(F32)).astype(BF16)
        pass_out[m] = jnp.concatenate(
            [high_part, high_part, low_part, jnp.zeros(shape, BF16)], axis=0
        )
    for copy in copies[6:]:
        copy.wait()

    def near(n, carry):
        picked = []
        for k in range(8):
            row = pl.multiple_of(source_row(near_src, near_count, n, k, first) * R, R)
            picked.append(trials[pl.ds(row, R), :])
        near_out[n] = jnp.dot(
            jnp.concatenate(picked, axis=1),
            blocks[n].reshape(8 * LANES, LANES),
            preferred_element_type=F32,
        )
        return carry

    for k in range(PIECES):
        pieces[k].wait()
        lax.fori_loop(size * k, size * (k + 1), near, 0, unroll=size)


def middle(src, count, near_src, near_count, trial, own, chip_halo, next_halo, leaf_rows, transfer, upper, blocks, after):
    return pl.pallas_call(
        middle_kernel,
        in_specs=[SMEM] * 4 + [HBM] * 9,
        out_shape=[
            jax.ShapeDtypeStruct((8, *BLOCK), F32),
            jax.ShapeDtypeStruct((8, LANES, LANES), BF16),
            jax.ShapeDtypeStruct((SPAN, *BLOCK), F32),
        ],
        scratch_shapes=[
            pltpu.VMEM((63, *BLOCK), BF16),
            pltpu.VMEM((2, 16 * 43, LANES), BF16),
            pltpu.VMEM((SPAN, 64, LANES), BF16),
            pltpu.VMEM((SPAN, 64, LANES), BF16),
            pltpu.VMEM((SPAN, 96, LANES), BF16),
            pltpu.VMEM((SPAN, 8, LANES, LANES), BF16),
            pltpu.VMEM(((3 * SPAN + 1) * R, LANES), BF16),
            pltpu.VMEM((3 * SPAN + 1, *BLOCK), BF16),
            pltpu.VMEM((63, 2 * R, LANES), F32),
            pltpu.VMEM((SPAN, *BLOCK), F32),
            pltpu.SemaphoreType.DMA((9 + PIECES,)),
        ],
        compiler_params=kernel_params(),
        cost_estimate=pl.CostEstimate(flops=2**36, bytes_accessed=2**29, transcendentals=0),
        name="middle",
    )(src, count, near_src, near_count, trial, own, chip_halo, next_halo, leaf_rows, transfer, upper, blocks, after)


def down_kernel(
    groups_hbm, mine_hbm, base_hbm, basis_hbm, parts_hbm, passes_hbm, near_hbm, out_hbm,
    groups, mine, base_upper, tree, side, basis, parts, passes, near, out, sems,
):
    device = lax.axis_index("leaf")
    place = lax.rem(device, GROUP)
    group = device // GROUP
    early = fetch(((groups_hbm, groups), (mine_hbm, mine), (base_hbm, base_upper)), sems)
    late = fetch(
        ((parts_hbm, parts), (passes_hbm, passes), (basis_hbm, basis), (near_hbm, near)), sems, 3
    )
    folds, rep2, rep3 = fold_matrix(), rep_four_transfers(), rep_four_uppers()
    for copy in early:
        copy.wait()
    for e in range(GROUPS):
        tree[e] = unhalve(groups[e, :16]).astype(BF16)
    joins = spread(rep2, jnp.concatenate([groups[2 * j, 16:32] for j in range(4)], axis=0))
    for j in range(4):
        mats = joins[64 * j : 64 * (j + 1)]
        tree[8 + j] = pack(join_up(tree[2 * j], tree[2 * j + 1], mats))
    tree[12] = jnp.zeros(BLOCK, BF16)
    top_path = groups[(group >> 1) * 2, 16:64]
    before, behind = jnp.maximum(group - 1, 0), jnp.minimum(group + 1, GROUPS - 1)
    has_before = jnp.where(group > 0, 1.0, 0.0)
    has_behind = jnp.where(group < GROUPS - 1, 1.0, 0.0)
    edges = []
    for k in range(6):
        rows = slice(ROWS + 16 * k, ROWS + 16 * (k + 1))
        edges.append(
            (
                (unhalve(groups[before, rows]) * has_before).astype(BF16),
                (unhalve(groups[behind, rows]) * has_behind).astype(BF16),
            )
        )
    for g in range(5):
        side[g, 0] = jnp.zeros(BLOCK, BF16)
        side[g, 1], side[g, 2] = edges[g][0], edges[5][0]
        side[g, 3], side[g, 4] = edges[5][1], edges[g][1]

    def upper_flat(g):
        return base_upper[...] if g == 0 else mine[144 * g - 32 : 144 * g] if g < 6 else top_path[16:]

    def transfer_flat(g):
        return mine[144 * g - 48 : 144 * g - 32] if g < 6 else top_path[:16]

    uppers, passing = {}, {}
    for levels in ((6, 5, 4, 3), (2, 1, 0, 0)):
        four = spread(rep3, jnp.concatenate([upper_flat(g) for g in levels], axis=0))
        for k, g in enumerate(levels):
            uppers[g] = jnp.concatenate(
                [four[128 * slot + R * k : 128 * slot + R * (k + 1)] for slot in range(3)], axis=0
            )
    for levels in ((6, 5, 4, 3), (2, 1, 1, 1)):
        four = spread(rep2, jnp.concatenate([transfer_flat(g) for g in levels], axis=0))
        four = settle(four, folds)
        for k, g in enumerate(levels):
            passing[g] = four[64 * k : 64 * (k + 1)]
    top = []
    for g in range(7):
        sources = []
        if g < 5:
            j, nodes = place >> g, GROUP >> g
            for k, offset in enumerate(source_offsets(j)):
                at = j + offset
                pick = jnp.where(at < 0, at + 3, jnp.where(at < nodes, 0, at - nodes + 3))
                sources.append(mine[144 * g + R * k : 144 * g + R * (k + 1)] + side[g, pick])
        else:
            j, nodes = group >> (g - 5), GROUPS >> (g - 5)
            for offset in source_offsets(j):
                at = j + offset
                ok = jnp.logical_and(at >= 0, at < nodes)
                sources.append(tree[jnp.where(ok, (0, 8)[g - 5] + at, 12)])
        top.append(fold(couple(sources, uppers[g])))

    down = top[6]
    for g in range(6, 0, -1):
        mats = passing[g]
        odd = jnp.broadcast_to((device >> (g - 1)) & 1, BLOCK)
        mats = jnp.where(odd == 1, mats[R:].astype(F32), mats[:R].astype(F32)).astype(BF16)
        down = top[g - 1] + times_transposed(down, four_times(mats))

    packed = pack(down).astype(F32)
    packed = jnp.where(block_of(down) < 3, packed, 0.0).astype(BF16)
    for copy in late:
        copy.wait()
    at = block_of(down)
    stores = []
    for m in range(8):
        x = parts[m] + jnp.dot(packed, passes[m], preferred_element_type=F32)
        x = x.astype(BF16).astype(F32)
        rows = jnp.concatenate([jnp.where(at == k, x, 0.0) for k in range(4)], axis=0)
        far = jnp.dot(
            rows.astype(BF16), basis[4 * m : 4 * m + 4].reshape(LANES, LANES), preferred_element_type=F32
        )
        for k in range(4):
            out[4 * m + k] = near[4 * m + k] + far[R * k : R * (k + 1)]
        stores += fetch(((out.at[pl.ds(4 * m, 4)], out_hbm.at[pl.ds(4 * m, 4)]),), sems, 7 + m)
    for copy in stores:
        copy.wait()


def down_all(groups, mine, base_upper, basis, parts, passes, near):
    return pl.pallas_call(
        down_kernel,
        in_specs=[HBM] * 7,
        out_specs=HBM,
        out_shape=jax.ShapeDtypeStruct((SPAN, *BLOCK), F32),
        scratch_shapes=[
            pltpu.VMEM((GROUPS, ROWS + EDGE, LANES), BF16),
            pltpu.VMEM((5 * 144, LANES), BF16),
            pltpu.VMEM(BLOCK, BF16),
            pltpu.VMEM((13, *BLOCK), BF16),
            pltpu.VMEM((5, 5, *BLOCK), BF16),
            pltpu.VMEM((SPAN, *BLOCK), BF16),
            pltpu.VMEM((8, *BLOCK), F32),
            pltpu.VMEM((8, LANES, LANES), BF16),
            pltpu.VMEM((SPAN, *BLOCK), F32),
            pltpu.VMEM((SPAN, *BLOCK), F32),
            pltpu.SemaphoreType.DMA((15,)),
        ],
        compiler_params=kernel_params(),
        name="down_all",
    )(groups, mine, base_upper, basis, parts, passes, near)


def swapped(x, first, devices):
    lower = range(first, devices - 1, 2)
    return lax.ppermute(x, "leaf", [(i, i + 1) for i in lower] + [(i + 1, i) for i in lower])


def on_device(
    devices,
    trial_vectors,
    leaf_basis,
    near_blocks,
    near_src,
    near_count,
    couple_src,
    couple_count,
    couple_leaf,
    transfer,
    couple_upper,
):
    transfer_rows = transfer.reshape(SPAN, 2, 8, LANES).transpose(0, 2, 1, 3).reshape(SPAN, 16, LANES)
    leaf_rows = couple_leaf.reshape(SPAN, 8, 8, LANES).transpose(0, 2, 1, 3).reshape(SPAN, 64, LANES)
    upper_slots = couple_upper.transpose(1, 0, 2)

    in_row = [list(range(g * GROUP, (g + 1) * GROUP)) for g in range(GROUPS)]
    across = [list(range(g, devices, GROUP)) for g in range(GROUP)]
    exchange = functools.partial(lax.all_to_all, axis_name="leaf", split_axis=0, concat_axis=0, tiled=True)

    trial_rows = trial_vectors.reshape(SPAN * R, LANES)
    send, own, spread_mats = local_up(trial_rows, leaf_basis, transfer_rows, upper_slots)
    got = exchange(send, axis_index_groups=in_row)
    to_chip, to_next, transfer_mats, upper_mats, base_upper = prepare(
        trial_rows, own, spread_mats, upper_slots
    )
    chip_halo = swapped(to_chip, 0, devices)
    next_halo = swapped(to_next, 1, devices)
    group_send, mine = group_up(got)
    groups = exchange(group_send, axis_index_groups=across)
    parts, passes, near = middle(
        couple_src.T, couple_count, near_src.T, near_count, trial_rows, own, chip_halo, next_halo,
        leaf_rows, transfer_mats, upper_mats, near_blocks, mine,
    )
    return down_all(groups, mine, base_upper, leaf_basis, parts, passes, near)


def solution(mesh):
    placed = (
        P("leaf", None, None),
        P("leaf", None, None),
        P("leaf", None, None, None),
        P("leaf", None),
        P("leaf"),
        P("leaf", None),
        P("leaf"),
        P("leaf", None, None),
        P("leaf", None, None),
        P("leaf", None, None),
    )
    return jax.shard_map(
        functools.partial(on_device, mesh.shape["leaf"]),
        mesh=mesh,
        in_specs=placed,
        out_specs=P("leaf", None, None),
        check_vma=False,
    )
```

```python
import functools

import jax
import jax.numpy as jnp
from jax import lax
from jax.experimental import pallas as pl
from jax.experimental.pallas import tpu as pltpu
from jax.sharding import PartitionSpec as P

F32, BF16 = jnp.float32, jnp.bfloat16
NT = (((1,), (1,)), ((), ()))
LANES = 128
R = 32
SPAN = 32
GROUP = 32
GROUPS = 8
ROWS = 64
TOP = 48
EDGE = 96
BLOCK = (R, LANES)
VMEM_LIMIT = 60 * 1024 * 1024
HALO = SPAN * R + 43 * 16


def iota(shape, dim):
    return lax.broadcasted_iota(jnp.int32, shape, dim)


def block_of(x):
    return iota(x.shape, 1) >> 5


def one_hot(made):
    return jnp.where(made, 1.0, 0.0).astype(BF16)


def rep_rows(slots, rows, column):
    shape = (slots * R, rows)
    m, j = iota(shape, 0), iota(shape, 1)
    return one_hot(j == column(m >> 5, (m & 31) >> 2))


def rep_transfer():
    return rep_rows(2, 16, lambda c, i: i * 2 + c)


def rep_upper():
    return rep_rows(3, 32, lambda k, i: k * 8 + i)


def rep_four_transfers():
    shape = (4 * 64, 64)
    m, j = iota(shape, 0), iota(shape, 1)
    return one_hot(j == (m >> 6) * 16 + ((m & 31) >> 2) * 2 + ((m >> 5) & 1))


def rep_four_uppers():
    shape = (3 * 128, 128)
    m, j = iota(shape, 0), iota(shape, 1)
    return one_hot(j == ((m >> 5) & 3) * 32 + (m >> 7) * 8 + ((m & 31) >> 2))


def rep_leaf():
    return rep_rows(8, 64, lambda k, i: i * 8 + k)


def doubled(mats):
    pieces = [mats[R * (k // 2) : R * (k // 2 + 1)] for k in range(2 * mats.shape[0] // R)]
    return jnp.concatenate(pieces, axis=0)


def fold_matrix():
    shape = (LANES, LANES)
    return one_hot((iota(shape, 0) & 31) == (iota(shape, 1) & 31))


def spread(rep, rows):
    wide = jnp.dot(rep, rows, preferred_element_type=F32)
    return jnp.where(block_of(wide) == (iota(wide.shape, 0) & 3), wide, 0.0).astype(BF16)


def settle(mats, folds):
    return jnp.dot(mats, folds, preferred_element_type=F32).astype(BF16)


def fold(x):
    x = x + pltpu.roll(x, 32, 1)
    return x + pltpu.roll(x, 64, 1)


def split(x):
    high = x.astype(BF16)
    return jnp.concatenate([high, (x - high.astype(F32)).astype(BF16)], axis=1)


def gather_matrix():
    shape = (8 * LANES, LANES)
    row, lane = iota(shape, 0), iota(shape, 1)
    return one_hot(jnp.logical_and(row >> 8 == lane >> 5, (row & 31) == (lane & 31)))


def pack(x):
    high = x.astype(BF16).astype(F32)
    return jnp.where((block_of(x) & 1) == 0, high, x - high).astype(BF16)


def halve(x):
    low, high = x[:16].astype(F32), x[16:].astype(F32)
    return jnp.where(block_of(low) < 2, low, high).astype(BF16)


def unhalve(x):
    x = x.astype(F32)
    turned = pltpu.roll(x, 64, 1)
    low = block_of(x) < 2
    return jnp.concatenate([jnp.where(low, x, turned), jnp.where(low, turned, x)], axis=0)


def side_by_side(left, right):
    left, right = left.astype(F32), right.astype(F32)
    return jnp.where(block_of(left) < 2, left, right).astype(BF16)


def join_up(left, right, mats):
    return fold(jnp.dot(side_by_side(left, right), doubled(mats), preferred_element_type=F32))


def couple(terms, mats):
    both = jnp.concatenate([side_by_side(terms[0], terms[1]), terms[2][:, : 2 * R]], axis=1)
    return jnp.dot(both, doubled(mats), preferred_element_type=F32)


def times_transposed(x, mats):
    return lax.dot_general(pack(x)[:, : 2 * R], mats[:, : 2 * R], NT, preferred_element_type=F32)


def four_times(x):
    return jnp.concatenate([x, x, x, x], axis=0)


def kernel_params(limit=VMEM_LIMIT):
    return pltpu.CompilerParams(vmem_limit_bytes=limit)


HBM = pl.BlockSpec(memory_space=pltpu.HBM)
VMEM = pl.BlockSpec(memory_space=pltpu.VMEM)
SMEM = pl.BlockSpec(memory_space=pltpu.SMEM)


def fetch(pairs, sems, first=0):
    copies = [pltpu.make_async_copy(a, b, sems.at[first + k]) for k, (a, b) in enumerate(pairs)]
    for copy in copies:
        copy.start()
    return copies


def lay_out_upper(upper, room):
    nodes = upper.shape[1]
    for slot in range(3):
        for i in range(8):
            room[pl.ds((slot * 8 + i) * nodes, nodes), :] = upper[
                slot, :, LANES * i : LANES * (i + 1)
            ].astype(F32)


def upper_rows(room, node, nodes=SPAN):
    rows = room[pl.ds(node, 24, stride=nodes), :]
    return jnp.concatenate([rows, jnp.zeros((8, LANES), F32)], axis=0).astype(BF16)


def level_base(l):
    return sum(SPAN >> k for k in range(l))


def local_up_kernel(
    trial_hbm, basis_hbm, transfer_hbm, upper_hbm, send, own_hbm, mats_hbm,
    trial, basis, transfer, upper, room, own, head, mats, sems,
):
    last = pl.ds(SPAN - 8, 8)
    copies = fetch(
        (
            (trial_hbm, trial),
            (basis_hbm, basis),
            (transfer_hbm, transfer),
            (upper_hbm.at[:, last, :], upper),
        ),
        sems,
    )
    rep = rep_four_transfers()
    for copy in copies[:2]:
        copy.wait()
    for n in range(SPAN):
        own[n] = pack(
            lax.dot_general(
                trial[R * n : R * (n + 1)], four_times(basis[n]), NT, preferred_element_type=F32
            )
        )
    leaves, nodes = pl.ds(0, SPAN), pl.ds(SPAN, SPAN - 1)
    outs = fetch([(own.at[leaves], own_hbm.at[leaves])], sems, 4)
    for copy in copies[2:]:
        copy.wait()
    for k in range(0, SPAN, 4):
        four = spread(rep, transfer[k : k + 4].reshape(64, LANES))
        mats[k : k + 4] = four.reshape(4, 64, LANES)
    outs += fetch([(mats, mats_hbm)], sems, 6 + GROUP)
    lay_out_upper(upper, room)
    head[16:32] = transfer[SPAN - 1]
    head[32:] = upper_rows(room, 7, 8)
    for l in range(1, 6):
        for j in range(SPAN >> l):
            q, child = j * 2**l + 2 ** (l - 1) - 1, level_base(l - 1) + 2 * j
            own[level_base(l) + j] = pack(join_up(own[child], own[child + 1], mats[q]))
    head[:16] = halve(own[62])
    outs += fetch(
        [(head, send.at[g]) for g in range(GROUP)] + [(own.at[nodes], own_hbm.at[nodes])], sems, 5
    )
    for copy in outs:
        copy.wait()


def local_up(trial, basis, transfer, upper):
    return pl.pallas_call(
        local_up_kernel,
        in_specs=[HBM] * 4,
        out_specs=[HBM, HBM, HBM],
        out_shape=[
            jax.ShapeDtypeStruct((GROUP, ROWS, LANES), BF16),
            jax.ShapeDtypeStruct((63, *BLOCK), BF16),
            jax.ShapeDtypeStruct((SPAN, 64, LANES), BF16),
        ],
        scratch_shapes=[
            pltpu.VMEM((SPAN * R, LANES), BF16),
            pltpu.VMEM((SPAN, *BLOCK), BF16),
            pltpu.VMEM((SPAN, 16, LANES), BF16),
            pltpu.VMEM((3, 8, 1024), BF16),
            pltpu.VMEM((24 * 8, LANES), F32),
            pltpu.VMEM((63, *BLOCK), BF16),
            pltpu.VMEM((ROWS, LANES), BF16),
            pltpu.VMEM((SPAN, 64, LANES), BF16),
            pltpu.SemaphoreType.DMA((7 + GROUP,)),
        ],
        compiler_params=kernel_params(),
        name="local_up",
    )(trial, basis, transfer, upper)


def prepare_kernel(
    trial_hbm, own_hbm, mats_hbm, upper_hbm, to_chip, to_next, transfer_out, upper_out, base_upper,
    trial, own, mats, upper, room, uppers, edges, sems,
):
    copies = fetch(
        ((trial_hbm, trial), (own_hbm, own), (mats_hbm, mats), (upper_hbm, upper)), sems
    )
    odd = lax.axis_index("leaf") & 1
    whole, rest = pl.ds(0, SPAN * R), pl.ds(SPAN * R, 16 * 43)
    copies[0].wait()
    outs = fetch(((trial, to_chip.at[whole]), (trial, to_next.at[whole])), sems, 4)
    copies[1].wait()
    for n in range(SPAN):
        half = halve(own[n])
        edges[0, 16 * n : 16 * n + 16] = half
        edges[1, 16 * n : 16 * n + 16] = half
    cursor = SPAN
    for l in range(1, 5):
        nodes = SPAN >> l
        keep = min(nodes, 3)
        for k in range(keep):
            at = level_base(l) + k
            edges[0, 16 * cursor : 16 * cursor + 16] = halve(own[at + nodes - keep])
            edges[1, 16 * cursor : 16 * cursor + 16] = halve(own[at])
            cursor += 1
    outs += fetch(
        ((edges.at[odd], to_chip.at[rest]), (edges.at[1 - odd], to_next.at[rest])), sems, 6
    )
    folds = fold_matrix()
    rep3 = rep_four_uppers()
    for copy in copies[2:]:
        copy.wait()
    lay_out_upper(upper, room)

    for k in range(0, SPAN, 4):
        rows = jnp.concatenate([upper_rows(room, k + n) for n in range(4)], axis=0)
        four = spread(rep3, rows)
        for n in range(4):
            for slot in range(3):
                at = 128 * slot + R * n
                uppers[k + n, R * slot : R * (slot + 1)] = four[at : at + R]
    for k in range(0, SPAN, 4):
        four = settle(mats[k : k + 4].reshape(256, LANES), folds)
        transfer_out[k : k + 4] = four.reshape(4, 64, LANES)
        four = settle(uppers[k : k + 4].reshape(384, LANES), folds)
        upper_out[k : k + 4] = four.reshape(4, 96, LANES)
    base_upper[...] = upper_rows(room, SPAN // 2 - 1)
    for copy in outs:
        copy.wait()


def prepare(trial, own, mats, upper):
    return pl.pallas_call(
        prepare_kernel,
        in_specs=[HBM] * 4,
        out_specs=[HBM, HBM, VMEM, VMEM, VMEM],
        out_shape=[
            jax.ShapeDtypeStruct((HALO, LANES), BF16),
            jax.ShapeDtypeStruct((HALO, LANES), BF16),
            jax.ShapeDtypeStruct((SPAN, 64, LANES), BF16),
            jax.ShapeDtypeStruct((SPAN, 96, LANES), BF16),
            jax.ShapeDtypeStruct(BLOCK, BF16),
        ],
        scratch_shapes=[
            pltpu.VMEM((SPAN * R, LANES), BF16),
            pltpu.VMEM((63, *BLOCK), BF16),
            pltpu.VMEM((SPAN, 64, LANES), BF16),
            pltpu.VMEM((3, SPAN, 1024), BF16),
            pltpu.VMEM((24 * SPAN, LANES), F32),
            pltpu.VMEM((SPAN, 96, LANES), BF16),
            pltpu.VMEM((2, 16 * 43, LANES), BF16),
            pltpu.SemaphoreType.DMA((8,)),
        ],
        compiler_params=kernel_params(),
        cost_estimate=pl.CostEstimate(flops=2**28, bytes_accessed=5 * 2**20, transcendentals=0),
        name="prepare",
    )(trial, own, mats, upper)


def source_offsets(j):
    odd = j & 1
    return (-2 - odd, 2 - 4 * odd, 3 - odd)


def edge_level(place):
    return sum(jnp.where(place >= 2**g, 1, 0) for g in range(1, 5))


def group_up_kernel(got, send, mine, inside, mats):
    rep = rep_four_transfers()
    for k in range(0, GROUP, 4):
        rows = jnp.concatenate([got[k + n, 16:32] for n in range(4)], axis=0)
        mats[k : k + 4] = spread(rep, rows).reshape(4, 64, LANES)
    for e in range(GROUP):
        inside[e] = unhalve(got[e, :16]).astype(BF16)
    for g in range(1, 6):
        for j in range(GROUP >> g):
            owner = (2 * j + 1) * 2 ** (g - 1) - 1
            child = level_base(g - 1) + 2 * j
            inside[level_base(g) + j] = pack(join_up(inside[child], inside[child + 1], mats[owner]))
    device = lax.axis_index("leaf")
    place = lax.rem(device, GROUP)
    group = device // GROUP
    right = [level_base(g) + (GROUP >> g) - 2 for g in range(5)]
    right.append(63 - lax.shift_right_logical(32, edge_level(place)))
    left = [level_base(g) + 1 for g in range(5)]
    left.append(64 - lax.shift_right_logical(64, edge_level(GROUP - 1 - place)))
    flat = got[GROUP - 1, R:].astype(F32)
    flat = jnp.where(group < GROUPS // 2, flat[8:24], flat[:16]).astype(BF16)
    head = jnp.concatenate([halve(inside[62]), got[GROUP - 1, 16:R], flat], axis=0)
    to_left = jnp.concatenate([halve(inside[k]) for k in left], axis=0)
    for g in range(GROUPS):
        send[g, :TOP] = head
        send[g, TOP:] = to_left
    after_this = jnp.minimum(group + 1, GROUPS - 1)
    inside[63] = jnp.zeros(BLOCK, BF16)
    for g in range(5):
        j, nodes = place >> g, GROUP >> g
        for k, offset in enumerate(source_offsets(j)):
            at = j + offset
            ok = jnp.logical_and(at >= 0, at < nodes)
            mine[144 * g + R * k : 144 * g + R * (k + 1)] = inside[jnp.where(ok, level_base(g) + at, 63)]
        mine[144 * g + 96 : 144 * (g + 1)] = got[((place >> (g + 1)) * 2 + 1) * 2**g - 1, 16:]
    send[after_this, TOP:] = jnp.concatenate([halve(inside[k]) for k in right], axis=0)


def group_up(got):
    return pl.pallas_call(
        group_up_kernel,
        out_shape=[
            jax.ShapeDtypeStruct((GROUPS, TOP + EDGE, LANES), BF16),
            jax.ShapeDtypeStruct((5 * 144, LANES), BF16),
        ],
        scratch_shapes=[pltpu.VMEM((64, *BLOCK), BF16), pltpu.VMEM((GROUP, 64, LANES), BF16)],
        compiler_params=kernel_params(16 * 1024 * 1024),
        cost_estimate=pl.CostEstimate(flops=2**31, bytes_accessed=2**25, transcendentals=0),
        name="group_up",
    )(got)


def source_row(src, count, row, slot, first):
    near = src[slot, row] - first
    near = jnp.minimum(jnp.maximum(near, 0), 3 * SPAN - 1)
    return jnp.where(slot < count[row], near, 3 * SPAN)


PIECES = 4


def middle_kernel(
    src, count, near_src, near_count, trial_hbm, own_hbm, chip_hbm, next_hbm, leaf_hbm, transfer_hbm,
    upper_hbm, blocks_hbm, after, part_out, pass_out, near_out,
    own, sides, leaf_rows, transfer, upper, blocks, trials, held, downs, coupled, sems,
):
    first = (lax.axis_index("leaf") - 1) * SPAN
    rest = pl.ds(SPAN * R, 16 * 43)
    whole = pl.ds(0, SPAN * R)
    odd = lax.axis_index("leaf") & 1

    def trial_place(third):
        return trials.at[pl.ds(pl.multiple_of(third * (SPAN * R), SPAN * R), SPAN * R)]

    copies = fetch(
        (
            (chip_hbm.at[rest], sides.at[1 - odd]),
            (own_hbm, own),
            (next_hbm.at[rest], sides.at[odd]),
            (transfer_hbm, transfer),
            (upper_hbm, upper),
            (leaf_hbm, leaf_rows),
            (chip_hbm.at[whole], trial_place(2 - 2 * odd)),
            (trial_hbm, trial_place(1)),
            (next_hbm.at[whole], trial_place(2 * odd)),
        ),
        sems,
    )
    size = SPAN // PIECES
    pieces = fetch(
        [
            (blocks_hbm.at[pl.ds(size * k, size)], blocks.at[pl.ds(size * k, size)])
            for k in range(PIECES)
        ],
        sems,
        len(copies),
    )
    held[3 * SPAN] = jnp.zeros(BLOCK, BF16)
    trials[3 * SPAN * R :] = jnp.zeros(BLOCK, BF16)
    shape = BLOCK
    eye = jnp.where(iota(shape, 0) == (iota(shape, 1) & 31), 1.0, 0.0)
    zero = jnp.zeros(shape, F32)
    downs[62] = jnp.concatenate([zero, eye], axis=0)
    for copy in copies[:5]:
        copy.wait()

    def edge(side, k):
        return unhalve(sides[side, 16 * k : 16 * k + 16]).astype(BF16)

    for n in range(SPAN):
        held[n] = edge(0, n)
        held[SPAN + n] = own[n]
        held[2 * SPAN + n] = edge(1, n)
    cursor = {}
    at = SPAN
    for l in range(1, 5):
        cursor[l] = at
        at += min(SPAN >> l, 3)
    for l in range(5, 0, -1):
        nodes = SPAN >> l
        for j in range(nodes):
            q = j * 2**l + 2 ** (l - 1) - 1
            mats = transfer[q]
            wide = jnp.concatenate([four_times(mats[:R]), four_times(mats[R:])], axis=0)
            y = times_transposed(downs[level_base(l) + j], wide)
            for c in range(2):
                part = y[:, LANES * c : LANES * (c + 1)]
                child, k = 2 * j + c, l - 1
                if k > 0:
                    n = SPAN >> k
                    keep = min(n, 3)

                    def coef(i):
                        if i < 0:
                            return edge(0, cursor[k] + keep + i)
                        if i >= n:
                            return edge(1, cursor[k] + i - n)
                        return own[level_base(k) + i]

                    offsets = (-2, 2, 3) if child % 2 == 0 else (-3, -2, 2)
                    m = upper[child * 2**k + 2 ** (k - 1) - 1]
                    got = couple([coef(child + i) for i in offsets], m)
                    part = part + jnp.concatenate([got, zero], axis=0)
                downs[level_base(k) + child] = part
    copies[5].wait()
    low = jnp.where((iota(BLOCK, 1) >> 6) == 0, 1.0, 0.0).astype(BF16)
    high = jnp.where((iota(BLOCK, 1) >> 6) == 1, 1.0, 0.0).astype(BF16)

    rep8 = rep_leaf()

    def leaf(n, carry):
        mats = spread(rep8, leaf_rows[n])
        picked = [held[source_row(src, count, n, k, first)] for k in range(8)]
        row = jnp.concatenate(
            [picked[2 * h] * low + picked[2 * h + 1] * high for h in range(4)], axis=1
        )
        coupled[n] = jnp.dot(row, doubled(mats), preferred_element_type=F32)
        return carry

    lax.fori_loop(0, SPAN, leaf, 0, unroll=16)
    at = block_of(zero)
    gather = gather_matrix()
    for m in range(8):
        x = [downs[4 * m + k] for k in range(4)]
        both = [
            jnp.where(at == 0, a, jnp.where(at == 1, b, jnp.where(at == 2, c, d)))
            for a, b, c, d in ([v[:R] for v in x], [v[R:] for v in x])
        ]
        wide = [split(coupled[4 * m + k]) for k in range(4)]
        part_out[m] = both[0] + jnp.dot(
            jnp.concatenate(wide, axis=1), gather, preferred_element_type=F32
        )
        high_part = both[1].astype(BF16)
        low_part = (both[1] - high_part.astype(F32)).astype(BF16)
        pass_out[m] = jnp.concatenate(
            [high_part, high_part, low_part, jnp.zeros(shape, BF16)], axis=0
        )
    for copy in copies[6:]:
        copy.wait()

    def near(n, carry):
        picked = []
        for k in range(8):
            row = pl.multiple_of(source_row(near_src, near_count, n, k, first) * R, R)
            picked.append(trials[pl.ds(row, R), :])
        near_out[n] = jnp.dot(
            jnp.concatenate(picked, axis=1),
            blocks[n].reshape(8 * LANES, LANES),
            preferred_element_type=F32,
        )
        return carry

    for k in range(PIECES):
        pieces[k].wait()
        lax.fori_loop(size * k, size * (k + 1), near, 0, unroll=size)


def middle(src, count, near_src, near_count, trial, own, chip_halo, next_halo, leaf_rows, transfer, upper, blocks, after):
    return pl.pallas_call(
        middle_kernel,
        in_specs=[SMEM] * 4 + [HBM] * 9,
        out_shape=[
            jax.ShapeDtypeStruct((8, *BLOCK), F32),
            jax.ShapeDtypeStruct((8, LANES, LANES), BF16),
            jax.ShapeDtypeStruct((SPAN, *BLOCK), F32),
        ],
        scratch_shapes=[
            pltpu.VMEM((63, *BLOCK), BF16),
            pltpu.VMEM((2, 16 * 43, LANES), BF16),
            pltpu.VMEM((SPAN, 64, LANES), BF16),
            pltpu.VMEM((SPAN, 64, LANES), BF16),
            pltpu.VMEM((SPAN, 96, LANES), BF16),
            pltpu.VMEM((SPAN, 8, LANES, LANES), BF16),
            pltpu.VMEM(((3 * SPAN + 1) * R, LANES), BF16),
            pltpu.VMEM((3 * SPAN + 1, *BLOCK), BF16),
            pltpu.VMEM((63, 2 * R, LANES), F32),
            pltpu.VMEM((SPAN, *BLOCK), F32),
            pltpu.SemaphoreType.DMA((9 + PIECES,)),
        ],
        compiler_params=kernel_params(),
        cost_estimate=pl.CostEstimate(flops=2**36, bytes_accessed=2**29, transcendentals=0),
        name="middle",
    )(src, count, near_src, near_count, trial, own, chip_halo, next_halo, leaf_rows, transfer, upper, blocks, after)


def down_kernel(
    groups_hbm, mine_hbm, base_hbm, basis_hbm, parts_hbm, passes_hbm, near_hbm, out_hbm,
    groups, mine, base_upper, tree, side, basis, parts, passes, near, out, sems,
):
    device = lax.axis_index("leaf")
    place = lax.rem(device, GROUP)
    group = device // GROUP
    early = fetch(((groups_hbm, groups), (mine_hbm, mine), (base_hbm, base_upper)), sems)
    late = fetch(
        ((parts_hbm, parts), (passes_hbm, passes), (basis_hbm, basis), (near_hbm, near)), sems, 3
    )
    folds, rep2, rep3 = fold_matrix(), rep_four_transfers(), rep_four_uppers()
    for copy in early:
        copy.wait()
    for e in range(GROUPS):
        tree[e] = unhalve(groups[e, :16]).astype(BF16)
    joins = spread(rep2, jnp.concatenate([groups[2 * j, 16:32] for j in range(4)], axis=0))
    for j in range(4):
        mats = joins[64 * j : 64 * (j + 1)]
        tree[8 + j] = pack(join_up(tree[2 * j], tree[2 * j + 1], mats))
    tree[12] = jnp.zeros(BLOCK, BF16)
    owner = (group >> 1) * 2
    top_transfer, two_slots = groups[owner, 16:32], groups[owner, 32:TOP].astype(F32)
    none = jnp.zeros((8, LANES), F32)
    top_upper = jnp.where(
        group < GROUPS // 2,
        jnp.concatenate([none, two_slots, none], axis=0),
        jnp.concatenate([two_slots, none, none], axis=0),
    ).astype(BF16)
    before, behind = jnp.maximum(group - 1, 0), jnp.minimum(group + 1, GROUPS - 1)
    has_before = jnp.where(group > 0, 1.0, 0.0)
    has_behind = jnp.where(group < GROUPS - 1, 1.0, 0.0)
    edges = []
    for k in range(6):
        rows = slice(TOP + 16 * k, TOP + 16 * (k + 1))
        edges.append(
            (
                (unhalve(groups[before, rows]) * has_before).astype(BF16),
                (unhalve(groups[behind, rows]) * has_behind).astype(BF16),
            )
        )
    for g in range(5):
        side[g, 0] = jnp.zeros(BLOCK, BF16)
        side[g, 1], side[g, 2] = edges[g][0], edges[5][0]
        side[g, 3], side[g, 4] = edges[5][1], edges[g][1]

    def upper_flat(g):
        return base_upper[...] if g == 0 else mine[144 * g - 32 : 144 * g] if g < 6 else top_upper

    def transfer_flat(g):
        return mine[144 * g - 48 : 144 * g - 32] if g < 6 else top_transfer

    uppers, passing = {}, {}
    for levels in ((6, 5, 4, 3), (2, 1, 0, 0)):
        four = spread(rep3, jnp.concatenate([upper_flat(g) for g in levels], axis=0))
        for k, g in enumerate(levels):
            uppers[g] = jnp.concatenate(
                [four[128 * slot + R * k : 128 * slot + R * (k + 1)] for slot in range(3)], axis=0
            )
    for levels in ((6, 5, 4, 3), (2, 1, 1, 1)):
        four = spread(rep2, jnp.concatenate([transfer_flat(g) for g in levels], axis=0))
        four = settle(four, folds)
        for k, g in enumerate(levels):
            passing[g] = four[64 * k : 64 * (k + 1)]
    top = []
    for g in range(7):
        sources = []
        if g < 5:
            j, nodes = place >> g, GROUP >> g
            for k, offset in enumerate(source_offsets(j)):
                at = j + offset
                pick = jnp.where(at < 0, at + 3, jnp.where(at < nodes, 0, at - nodes + 3))
                sources.append(mine[144 * g + R * k : 144 * g + R * (k + 1)] + side[g, pick])
        else:
            j, nodes = group >> (g - 5), GROUPS >> (g - 5)
            for offset in source_offsets(j):
                at = j + offset
                ok = jnp.logical_and(at >= 0, at < nodes)
                sources.append(tree[jnp.where(ok, (0, 8)[g - 5] + at, 12)])
        top.append(fold(couple(sources, uppers[g])))

    down = top[6]
    for g in range(6, 0, -1):
        mats = passing[g]
        odd = jnp.broadcast_to((device >> (g - 1)) & 1, BLOCK)
        mats = jnp.where(odd == 1, mats[R:].astype(F32), mats[:R].astype(F32)).astype(BF16)
        down = top[g - 1] + times_transposed(down, four_times(mats))

    packed = pack(down).astype(F32)
    packed = jnp.where(block_of(down) < 3, packed, 0.0).astype(BF16)
    for copy in late:
        copy.wait()
    at = block_of(down)
    stores = []
    for m in range(8):
        x = parts[m] + jnp.dot(packed, passes[m], preferred_element_type=F32)
        x = x.astype(BF16).astype(F32)
        rows = jnp.concatenate([jnp.where(at == k, x, 0.0) for k in range(4)], axis=0)
        far = jnp.dot(
            rows.astype(BF16), basis[4 * m : 4 * m + 4].reshape(LANES, LANES), preferred_element_type=F32
        )
        for k in range(4):
            out[4 * m + k] = near[4 * m + k] + far[R * k : R * (k + 1)]
        stores += fetch(((out.at[pl.ds(4 * m, 4)], out_hbm.at[pl.ds(4 * m, 4)]),), sems, 7 + m)
    for copy in stores:
        copy.wait()


def down_all(groups, mine, base_upper, basis, parts, passes, near):
    return pl.pallas_call(
        down_kernel,
        in_specs=[HBM] * 7,
        out_specs=HBM,
        out_shape=jax.ShapeDtypeStruct((SPAN, *BLOCK), F32),
        scratch_shapes=[
            pltpu.VMEM((GROUPS, TOP + EDGE, LANES), BF16),
            pltpu.VMEM((5 * 144, LANES), BF16),
            pltpu.VMEM(BLOCK, BF16),
            pltpu.VMEM((13, *BLOCK), BF16),
            pltpu.VMEM((5, 5, *BLOCK), BF16),
            pltpu.VMEM((SPAN, *BLOCK), BF16),
            pltpu.VMEM((8, *BLOCK), F32),
            pltpu.VMEM((8, LANES, LANES), BF16),
            pltpu.VMEM((SPAN, *BLOCK), F32),
            pltpu.VMEM((SPAN, *BLOCK), F32),
            pltpu.SemaphoreType.DMA((15,)),
        ],
        compiler_params=kernel_params(),
        name="down_all",
    )(groups, mine, base_upper, basis, parts, passes, near)


def swapped(x, first, devices):
    lower = range(first, devices - 1, 2)
    return lax.ppermute(x, "leaf", [(i, i + 1) for i in lower] + [(i + 1, i) for i in lower])


def on_device(
    devices,
    trial_vectors,
    leaf_basis,
    near_blocks,
    near_src,
    near_count,
    couple_src,
    couple_count,
    couple_leaf,
    transfer,
    couple_upper,
):
    transfer_rows = transfer.reshape(SPAN, 2, 8, LANES).transpose(0, 2, 1, 3).reshape(SPAN, 16, LANES)
    leaf_rows = couple_leaf.reshape(SPAN, 8, 8, LANES).transpose(0, 2, 1, 3).reshape(SPAN, 64, LANES)
    upper_slots = couple_upper.transpose(1, 0, 2)

    in_row = [list(range(g * GROUP, (g + 1) * GROUP)) for g in range(GROUPS)]
    across = [list(range(g, devices, GROUP)) for g in range(GROUP)]
    exchange = functools.partial(lax.all_to_all, axis_name="leaf", split_axis=0, concat_axis=0, tiled=True)

    trial_rows = trial_vectors.reshape(SPAN * R, LANES)
    send, own, spread_mats = local_up(trial_rows, leaf_basis, transfer_rows, upper_slots)
    got = exchange(send, axis_index_groups=in_row)
    to_chip, to_next, transfer_mats, upper_mats, base_upper = prepare(
        trial_rows, own, spread_mats, upper_slots
    )
    chip_halo = swapped(to_chip, 0, devices)
    next_halo = swapped(to_next, 1, devices)
    group_send, mine = group_up(got)
    groups = exchange(group_send, axis_index_groups=across)
    parts, passes, near = middle(
        couple_src.T, couple_count, near_src.T, near_count, trial_rows, own, chip_halo, next_halo,
        leaf_rows, transfer_mats, upper_mats, near_blocks, mine,
    )
    return down_all(groups, mine, base_upper, leaf_basis, parts, passes, near)


def solution(mesh):
    placed = (
        P("leaf", None, None),
        P("leaf", None, None),
        P("leaf", None, None, None),
        P("leaf", None),
        P("leaf"),
        P("leaf", None),
        P("leaf"),
        P("leaf", None, None),
        P("leaf", None, None),
        P("leaf", None, None),
    )
    return jax.shard_map(
        functools.partial(on_device, mesh.shape["leaf"]),
        mesh=mesh,
        in_specs=placed,
        out_specs=P("leaf", None, None),
        check_vma=False,
    )
```

```python
import functools

import jax
import jax.numpy as jnp
from jax import lax
from jax.experimental import pallas as pl
from jax.experimental.pallas import tpu as pltpu
from jax.sharding import PartitionSpec as P

F32, BF16 = jnp.float32, jnp.bfloat16
NT = (((1,), (1,)), ((), ()))
LANES = 128
R = 32
SPAN = 32
GROUP = 32
GROUPS = 8
ROWS = 64
TOP = 48
EDGE = 96
BLOCK = (R, LANES)
VMEM_LIMIT = 60 * 1024 * 1024
HALO = SPAN * R + 43 * 16


def iota(shape, dim):
    return lax.broadcasted_iota(jnp.int32, shape, dim)


def block_of(x):
    return iota(x.shape, 1) >> 5


def one_hot(made):
    return jnp.where(made, 1.0, 0.0).astype(BF16)


def rep_rows(slots, rows, column):
    shape = (slots * R, rows)
    m, j = iota(shape, 0), iota(shape, 1)
    return one_hot(j == column(m >> 5, (m & 31) >> 2))


def rep_transfer():
    return rep_rows(2, 16, lambda c, i: i * 2 + c)


def rep_upper():
    return rep_rows(3, 32, lambda k, i: k * 8 + i)


def rep_four_transfers():
    shape = (4 * 64, 64)
    m, j = iota(shape, 0), iota(shape, 1)
    return one_hot(j == (m >> 6) * 16 + ((m & 31) >> 2) * 2 + ((m >> 5) & 1))


def rep_four_uppers():
    shape = (3 * 128, 128)
    m, j = iota(shape, 0), iota(shape, 1)
    return one_hot(j == ((m >> 5) & 3) * 32 + (m >> 7) * 8 + ((m & 31) >> 2))


def rep_leaf():
    return rep_rows(8, 64, lambda k, i: i * 8 + k)


def doubled(mats):
    pieces = [mats[R * (k // 2) : R * (k // 2 + 1)] for k in range(2 * mats.shape[0] // R)]
    return jnp.concatenate(pieces, axis=0)


def fold_matrix():
    shape = (LANES, LANES)
    return one_hot((iota(shape, 0) & 31) == (iota(shape, 1) & 31))


def spread(rep, rows):
    wide = jnp.dot(rep, rows, preferred_element_type=F32)
    return jnp.where(block_of(wide) == (iota(wide.shape, 0) & 3), wide, 0.0).astype(BF16)


def settle(mats, folds):
    return jnp.dot(mats, folds, preferred_element_type=F32).astype(BF16)


def fold(x):
    x = x + pltpu.roll(x, 32, 1)
    return x + pltpu.roll(x, 64, 1)


def split(x):
    high = x.astype(BF16)
    return jnp.concatenate([high, (x - high.astype(F32)).astype(BF16)], axis=1)


def gather_matrix():
    shape = (8 * LANES, LANES)
    row, lane = iota(shape, 0), iota(shape, 1)
    return one_hot(jnp.logical_and(row >> 8 == lane >> 5, (row & 31) == (lane & 31)))


def pack(x):
    high = x.astype(BF16).astype(F32)
    return jnp.where((block_of(x) & 1) == 0, high, x - high).astype(BF16)


def halve(x):
    low, high = x[:16].astype(F32), x[16:].astype(F32)
    return jnp.where(block_of(low) < 2, low, high).astype(BF16)


def unhalve(x):
    x = x.astype(F32)
    turned = pltpu.roll(x, 64, 1)
    low = block_of(x) < 2
    return jnp.concatenate([jnp.where(low, x, turned), jnp.where(low, turned, x)], axis=0)


def side_by_side(left, right):
    left, right = left.astype(F32), right.astype(F32)
    return jnp.where(block_of(left) < 2, left, right).astype(BF16)


def join_up(left, right, mats):
    return fold(jnp.dot(side_by_side(left, right), doubled(mats), preferred_element_type=F32))


def couple(terms, mats):
    both = jnp.concatenate([side_by_side(terms[0], terms[1]), terms[2][:, : 2 * R]], axis=1)
    return jnp.dot(both, doubled(mats), preferred_element_type=F32)


def times_transposed(x, mats):
    return lax.dot_general(pack(x)[:, : 2 * R], mats[:, : 2 * R], NT, preferred_element_type=F32)


def four_times(x):
    return jnp.concatenate([x, x, x, x], axis=0)


def kernel_params(limit=VMEM_LIMIT):
    return pltpu.CompilerParams(vmem_limit_bytes=limit)


HBM = pl.BlockSpec(memory_space=pltpu.HBM)
VMEM = pl.BlockSpec(memory_space=pltpu.VMEM)
SMEM = pl.BlockSpec(memory_space=pltpu.SMEM)


def fetch(pairs, sems, first=0):
    copies = [pltpu.make_async_copy(a, b, sems.at[first + k]) for k, (a, b) in enumerate(pairs)]
    for copy in copies:
        copy.start()
    return copies


def lay_out_upper(upper, room):
    nodes = upper.shape[1]
    for slot in range(3):
        for i in range(8):
            room[pl.ds((slot * 8 + i) * nodes, nodes), :] = upper[
                slot, :, LANES * i : LANES * (i + 1)
            ].astype(F32)


def upper_rows(room, node, nodes=SPAN):
    rows = room[pl.ds(node, 24, stride=nodes), :]
    return jnp.concatenate([rows, jnp.zeros((8, LANES), F32)], axis=0).astype(BF16)


def level_base(l):
    return sum(SPAN >> k for k in range(l))


def local_up_kernel(
    trial_hbm, basis_hbm, transfer_hbm, upper_hbm, send, own_hbm, mats_hbm,
    trial, basis, transfer, upper, room, own, head, mats, sems,
):
    last = pl.ds(SPAN - 8, 8)
    copies = fetch(
        (
            (trial_hbm, trial),
            (basis_hbm, basis),
            (transfer_hbm, transfer),
            (upper_hbm.at[:, last, :], upper),
        ),
        sems,
    )
    rep, folds = rep_four_transfers(), fold_matrix()
    for copy in copies[:2]:
        copy.wait()
    for n in range(SPAN):
        own[n] = pack(
            lax.dot_general(
                trial[R * n : R * (n + 1)], four_times(basis[n]), NT, preferred_element_type=F32
            )
        )
    leaves, nodes = pl.ds(0, SPAN), pl.ds(SPAN, SPAN - 1)
    outs = fetch([(own.at[leaves], own_hbm.at[leaves])], sems, 4)
    for copy in copies[2:]:
        copy.wait()
    for k in range(0, SPAN, 4):
        four = settle(spread(rep, transfer[k : k + 4].reshape(64, LANES)), folds)
        mats[k : k + 4] = four.reshape(4, 64, LANES)
    outs += fetch([(mats, mats_hbm)], sems, 6 + GROUP)
    lay_out_upper(upper, room)
    head[16:32] = transfer[SPAN - 1]
    head[32:] = upper_rows(room, 7, 8)
    for l in range(1, 6):
        for j in range(SPAN >> l):
            q, child = j * 2**l + 2 ** (l - 1) - 1, level_base(l - 1) + 2 * j
            both = side_by_side(own[child], own[child + 1])
            own[level_base(l) + j] = pack(
                jnp.dot(both, doubled(mats[q]), preferred_element_type=F32)
            )
    head[:16] = halve(own[62])
    outs += fetch(
        [(head, send.at[g]) for g in range(GROUP)] + [(own.at[nodes], own_hbm.at[nodes])], sems, 5
    )
    for copy in outs:
        copy.wait()


def local_up(trial, basis, transfer, upper):
    return pl.pallas_call(
        local_up_kernel,
        in_specs=[HBM] * 4,
        out_specs=[HBM, HBM, HBM],
        out_shape=[
            jax.ShapeDtypeStruct((GROUP, ROWS, LANES), BF16),
            jax.ShapeDtypeStruct((63, *BLOCK), BF16),
            jax.ShapeDtypeStruct((SPAN, 64, LANES), BF16),
        ],
        scratch_shapes=[
            pltpu.VMEM((SPAN * R, LANES), BF16),
            pltpu.VMEM((SPAN, *BLOCK), BF16),
            pltpu.VMEM((SPAN, 16, LANES), BF16),
            pltpu.VMEM((3, 8, 1024), BF16),
            pltpu.VMEM((24 * 8, LANES), F32),
            pltpu.VMEM((63, *BLOCK), BF16),
            pltpu.VMEM((ROWS, LANES), BF16),
            pltpu.VMEM((SPAN, 64, LANES), BF16),
            pltpu.SemaphoreType.DMA((7 + GROUP,)),
        ],
        compiler_params=kernel_params(),
        name="local_up",
    )(trial, basis, transfer, upper)


def prepare_kernel(
    trial_hbm, own_hbm, upper_hbm, to_chip, to_next, upper_out, base_upper,
    trial, own, upper, room, uppers, edges, sems,
):
    copies = fetch(
        ((trial_hbm, trial), (own_hbm, own), (upper_hbm, upper)), sems
    )
    odd = lax.axis_index("leaf") & 1
    whole, rest = pl.ds(0, SPAN * R), pl.ds(SPAN * R, 16 * 43)
    copies[0].wait()
    outs = fetch(((trial, to_chip.at[whole]), (trial, to_next.at[whole])), sems, 4)
    copies[1].wait()
    for n in range(SPAN):
        half = halve(own[n])
        edges[0, 16 * n : 16 * n + 16] = half
        edges[1, 16 * n : 16 * n + 16] = half
    cursor = SPAN
    for l in range(1, 5):
        nodes = SPAN >> l
        keep = min(nodes, 3)
        for k in range(keep):
            at = level_base(l) + k
            edges[0, 16 * cursor : 16 * cursor + 16] = halve(own[at + nodes - keep])
            edges[1, 16 * cursor : 16 * cursor + 16] = halve(own[at])
            cursor += 1
    outs += fetch(
        ((edges.at[odd], to_chip.at[rest]), (edges.at[1 - odd], to_next.at[rest])), sems, 6
    )
    folds = fold_matrix()
    rep3 = rep_four_uppers()
    for copy in copies[2:]:
        copy.wait()
    lay_out_upper(upper, room)

    for k in range(0, SPAN, 4):
        rows = jnp.concatenate([upper_rows(room, k + n) for n in range(4)], axis=0)
        four = spread(rep3, rows)
        for n in range(4):
            for slot in range(3):
                at = 128 * slot + R * n
                uppers[k + n, R * slot : R * (slot + 1)] = four[at : at + R]
    for k in range(0, SPAN, 4):
        four = settle(uppers[k : k + 4].reshape(384, LANES), folds)
        upper_out[k : k + 4] = four.reshape(4, 96, LANES)
    base_upper[...] = upper_rows(room, SPAN // 2 - 1)
    for copy in outs:
        copy.wait()


def prepare(trial, own, upper):
    return pl.pallas_call(
        prepare_kernel,
        in_specs=[HBM] * 3,
        out_specs=[HBM, HBM, VMEM, VMEM],
        out_shape=[
            jax.ShapeDtypeStruct((HALO, LANES), BF16),
            jax.ShapeDtypeStruct((HALO, LANES), BF16),
            jax.ShapeDtypeStruct((SPAN, 96, LANES), BF16),
            jax.ShapeDtypeStruct(BLOCK, BF16),
        ],
        scratch_shapes=[
            pltpu.VMEM((SPAN * R, LANES), BF16),
            pltpu.VMEM((63, *BLOCK), BF16),
            pltpu.VMEM((3, SPAN, 1024), BF16),
            pltpu.VMEM((24 * SPAN, LANES), F32),
            pltpu.VMEM((SPAN, 96, LANES), BF16),
            pltpu.VMEM((2, 16 * 43, LANES), BF16),
            pltpu.SemaphoreType.DMA((8,)),
        ],
        compiler_params=kernel_params(),
        cost_estimate=pl.CostEstimate(flops=2**28, bytes_accessed=5 * 2**20, transcendentals=0),
        name="prepare",
    )(trial, own, upper)


def source_offsets(j):
    odd = j & 1
    return (-2 - odd, 2 - 4 * odd, 3 - odd)


def edge_level(place):
    return sum(jnp.where(place >= 2**g, 1, 0) for g in range(1, 5))


def group_up_kernel(got, send, mine, inside, mats):
    rep, folds = rep_four_transfers(), fold_matrix()
    for k in range(0, GROUP, 4):
        rows = jnp.concatenate([got[k + n, 16:32] for n in range(4)], axis=0)
        mats[k : k + 4] = settle(spread(rep, rows), folds).reshape(4, 64, LANES)
    for e in range(GROUP):
        inside[e] = unhalve(got[e, :16]).astype(BF16)
    for g in range(1, 6):
        for j in range(GROUP >> g):
            owner = (2 * j + 1) * 2 ** (g - 1) - 1
            child = level_base(g - 1) + 2 * j
            both = side_by_side(inside[child], inside[child + 1])
            inside[level_base(g) + j] = pack(
                jnp.dot(both, doubled(mats[owner]), preferred_element_type=F32)
            )
    device = lax.axis_index("leaf")
    place = lax.rem(device, GROUP)
    group = device // GROUP
    right = [level_base(g) + (GROUP >> g) - 2 for g in range(5)]
    right.append(63 - lax.shift_right_logical(32, edge_level(place)))
    left = [level_base(g) + 1 for g in range(5)]
    left.append(64 - lax.shift_right_logical(64, edge_level(GROUP - 1 - place)))
    flat = got[GROUP - 1, R:].astype(F32)
    flat = jnp.where(group < GROUPS // 2, flat[8:24], flat[:16]).astype(BF16)
    head = jnp.concatenate([halve(inside[62]), got[GROUP - 1, 16:R], flat], axis=0)
    to_left = jnp.concatenate([halve(inside[k]) for k in left], axis=0)
    for g in range(GROUPS):
        send[g, :TOP] = head
        send[g, TOP:] = to_left
    after_this = jnp.minimum(group + 1, GROUPS - 1)
    inside[63] = jnp.zeros(BLOCK, BF16)
    for g in range(5):
        j, nodes = place >> g, GROUP >> g
        for k, offset in enumerate(source_offsets(j)):
            at = j + offset
            ok = jnp.logical_and(at >= 0, at < nodes)
            mine[144 * g + R * k : 144 * g + R * (k + 1)] = inside[jnp.where(ok, level_base(g) + at, 63)]
        mine[144 * g + 96 : 144 * (g + 1)] = got[((place >> (g + 1)) * 2 + 1) * 2**g - 1, 16:]
    send[after_this, TOP:] = jnp.concatenate([halve(inside[k]) for k in right], axis=0)


def group_up(got):
    return pl.pallas_call(
        group_up_kernel,
        out_shape=[
            jax.ShapeDtypeStruct((GROUPS, TOP + EDGE, LANES), BF16),
            jax.ShapeDtypeStruct((5 * 144, LANES), BF16),
        ],
        scratch_shapes=[pltpu.VMEM((64, *BLOCK), BF16), pltpu.VMEM((GROUP, 64, LANES), BF16)],
        compiler_params=kernel_params(16 * 1024 * 1024),
        cost_estimate=pl.CostEstimate(flops=2**31, bytes_accessed=2**25, transcendentals=0),
        name="group_up",
    )(got)


def source_row(src, count, row, slot, first):
    near = src[slot, row] - first
    near = jnp.minimum(jnp.maximum(near, 0), 3 * SPAN - 1)
    return jnp.where(slot < count[row], near, 3 * SPAN)


PIECES = 4


def middle_kernel(
    src, count, near_src, near_count, trial_hbm, own_hbm, chip_hbm, next_hbm, leaf_hbm, transfer_hbm,
    upper_hbm, blocks_hbm, after, part_out, pass_out, near_out,
    own, sides, leaf_rows, transfer, upper, blocks, trials, held, downs, coupled, sems,
):
    first = (lax.axis_index("leaf") - 1) * SPAN
    rest = pl.ds(SPAN * R, 16 * 43)
    whole = pl.ds(0, SPAN * R)
    odd = lax.axis_index("leaf") & 1

    def trial_place(third):
        return trials.at[pl.ds(pl.multiple_of(third * (SPAN * R), SPAN * R), SPAN * R)]

    copies = fetch(
        (
            (chip_hbm.at[rest], sides.at[1 - odd]),
            (own_hbm, own),
            (next_hbm.at[rest], sides.at[odd]),
            (transfer_hbm, transfer),
            (upper_hbm, upper),
            (leaf_hbm, leaf_rows),
            (chip_hbm.at[whole], trial_place(2 - 2 * odd)),
            (trial_hbm, trial_place(1)),
            (next_hbm.at[whole], trial_place(2 * odd)),
        ),
        sems,
    )
    size = SPAN // PIECES
    pieces = fetch(
        [
            (blocks_hbm.at[pl.ds(size * k, size)], blocks.at[pl.ds(size * k, size)])
            for k in range(PIECES)
        ],
        sems,
        len(copies),
    )
    held[3 * SPAN] = jnp.zeros(BLOCK, BF16)
    trials[3 * SPAN * R :] = jnp.zeros(BLOCK, BF16)
    shape = BLOCK
    eye = jnp.where(iota(shape, 0) == (iota(shape, 1) & 31), 1.0, 0.0)
    zero = jnp.zeros(shape, F32)
    downs[62] = jnp.concatenate([zero, eye], axis=0)
    for copy in copies[:5]:
        copy.wait()

    def edge(side, k):
        return unhalve(sides[side, 16 * k : 16 * k + 16]).astype(BF16)

    for n in range(SPAN):
        held[n] = edge(0, n)
        held[SPAN + n] = own[n]
        held[2 * SPAN + n] = edge(1, n)
    cursor = {}
    at = SPAN
    for l in range(1, 5):
        cursor[l] = at
        at += min(SPAN >> l, 3)
    for l in range(5, 0, -1):
        nodes = SPAN >> l
        for j in range(nodes):
            q = j * 2**l + 2 ** (l - 1) - 1
            mats = transfer[q]
            wide = jnp.concatenate([four_times(mats[:R]), four_times(mats[R:])], axis=0)
            y = times_transposed(downs[level_base(l) + j], wide)
            for c in range(2):
                part = y[:, LANES * c : LANES * (c + 1)]
                child, k = 2 * j + c, l - 1
                if k > 0:
                    n = SPAN >> k
                    keep = min(n, 3)

                    def coef(i):
                        if i < 0:
                            return edge(0, cursor[k] + keep + i)
                        if i >= n:
                            return edge(1, cursor[k] + i - n)
                        return own[level_base(k) + i]

                    offsets = (-2, 2, 3) if child % 2 == 0 else (-3, -2, 2)
                    m = upper[child * 2**k + 2 ** (k - 1) - 1]
                    got = couple([coef(child + i) for i in offsets], m)
                    part = part + jnp.concatenate([got, zero], axis=0)
                downs[level_base(k) + child] = part
    copies[5].wait()
    low = jnp.where((iota(BLOCK, 1) >> 6) == 0, 1.0, 0.0).astype(BF16)
    high = jnp.where((iota(BLOCK, 1) >> 6) == 1, 1.0, 0.0).astype(BF16)

    rep8 = rep_leaf()

    def leaf(n, carry):
        mats = spread(rep8, leaf_rows[n])
        picked = [held[source_row(src, count, n, k, first)] for k in range(8)]
        row = jnp.concatenate(
            [picked[2 * h] * low + picked[2 * h + 1] * high for h in range(4)], axis=1
        )
        coupled[n] = jnp.dot(row, doubled(mats), preferred_element_type=F32)
        return carry

    lax.fori_loop(0, SPAN, leaf, 0, unroll=16)
    at = block_of(zero)
    gather = gather_matrix()
    for m in range(8):
        x = [downs[4 * m + k] for k in range(4)]
        both = [
            jnp.where(at == 0, a, jnp.where(at == 1, b, jnp.where(at == 2, c, d)))
            for a, b, c, d in ([v[:R] for v in x], [v[R:] for v in x])
        ]
        wide = [split(coupled[4 * m + k]) for k in range(4)]
        part_out[m] = both[0] + jnp.dot(
            jnp.concatenate(wide, axis=1), gather, preferred_element_type=F32
        )
        high_part = both[1].astype(BF16)
        low_part = (both[1] - high_part.astype(F32)).astype(BF16)
        pass_out[m] = jnp.concatenate(
            [high_part, high_part, low_part, jnp.zeros(shape, BF16)], axis=0
        )
    for copy in copies[6:]:
        copy.wait()

    def near(n, carry):
        picked = []
        for k in range(8):
            row = pl.multiple_of(source_row(near_src, near_count, n, k, first) * R, R)
            picked.append(trials[pl.ds(row, R), :])
        near_out[n] = jnp.dot(
            jnp.concatenate(picked, axis=1),
            blocks[n].reshape(8 * LANES, LANES),
            preferred_element_type=F32,
        )
        return carry

    for k in range(PIECES):
        pieces[k].wait()
        lax.fori_loop(size * k, size * (k + 1), near, 0, unroll=size)


def middle(src, count, near_src, near_count, trial, own, chip_halo, next_halo, leaf_rows, transfer, upper, blocks, after):
    return pl.pallas_call(
        middle_kernel,
        in_specs=[SMEM] * 4 + [HBM] * 9,
        out_shape=[
            jax.ShapeDtypeStruct((8, *BLOCK), F32),
            jax.ShapeDtypeStruct((8, LANES, LANES), BF16),
            jax.ShapeDtypeStruct((SPAN, *BLOCK), F32),
        ],
        scratch_shapes=[
            pltpu.VMEM((63, *BLOCK), BF16),
            pltpu.VMEM((2, 16 * 43, LANES), BF16),
            pltpu.VMEM((SPAN, 64, LANES), BF16),
            pltpu.VMEM((SPAN, 64, LANES), BF16),
            pltpu.VMEM((SPAN, 96, LANES), BF16),
            pltpu.VMEM((SPAN, 8, LANES, LANES), BF16),
            pltpu.VMEM(((3 * SPAN + 1) * R, LANES), BF16),
            pltpu.VMEM((3 * SPAN + 1, *BLOCK), BF16),
            pltpu.VMEM((63, 2 * R, LANES), F32),
            pltpu.VMEM((SPAN, *BLOCK), F32),
            pltpu.SemaphoreType.DMA((9 + PIECES,)),
        ],
        compiler_params=kernel_params(),
        cost_estimate=pl.CostEstimate(flops=2**36, bytes_accessed=2**29, transcendentals=0),
        name="middle",
    )(src, count, near_src, near_count, trial, own, chip_halo, next_halo, leaf_rows, transfer, upper, blocks, after)


def down_kernel(
    groups_hbm, mine_hbm, base_hbm, basis_hbm, parts_hbm, passes_hbm, near_hbm, out_hbm,
    groups, mine, base_upper, tree, side, basis, parts, passes, near, out, sems,
):
    device = lax.axis_index("leaf")
    place = lax.rem(device, GROUP)
    group = device // GROUP
    early = fetch(((groups_hbm, groups), (mine_hbm, mine), (base_hbm, base_upper)), sems)
    late = fetch(
        ((parts_hbm, parts), (passes_hbm, passes), (basis_hbm, basis), (near_hbm, near)), sems, 3
    )
    folds, rep2, rep3 = fold_matrix(), rep_four_transfers(), rep_four_uppers()
    for copy in early:
        copy.wait()
    for e in range(GROUPS):
        tree[e] = unhalve(groups[e, :16]).astype(BF16)
    joins = spread(rep2, jnp.concatenate([groups[2 * j, 16:32] for j in range(4)], axis=0))
    for j in range(4):
        mats = joins[64 * j : 64 * (j + 1)]
        tree[8 + j] = pack(join_up(tree[2 * j], tree[2 * j + 1], mats))
    tree[12] = jnp.zeros(BLOCK, BF16)
    owner = (group >> 1) * 2
    top_transfer, two_slots = groups[owner, 16:32], groups[owner, 32:TOP].astype(F32)
    none = jnp.zeros((8, LANES), F32)
    top_upper = jnp.where(
        group < GROUPS // 2,
        jnp.concatenate([none, two_slots, none], axis=0),
        jnp.concatenate([two_slots, none, none], axis=0),
    ).astype(BF16)
    before, behind = jnp.maximum(group - 1, 0), jnp.minimum(group + 1, GROUPS - 1)
    has_before = jnp.where(group > 0, 1.0, 0.0)
    has_behind = jnp.where(group < GROUPS - 1, 1.0, 0.0)
    edges = []
    for k in range(6):
        rows = slice(TOP + 16 * k, TOP + 16 * (k + 1))
        edges.append(
            (
                (unhalve(groups[before, rows]) * has_before).astype(BF16),
                (unhalve(groups[behind, rows]) * has_behind).astype(BF16),
            )
        )
    for g in range(5):
        side[g, 0] = jnp.zeros(BLOCK, BF16)
        side[g, 1], side[g, 2] = edges[g][0], edges[5][0]
        side[g, 3], side[g, 4] = edges[5][1], edges[g][1]

    def upper_flat(g):
        return base_upper[...] if g == 0 else mine[144 * g - 32 : 144 * g] if g < 6 else top_upper

    def transfer_flat(g):
        return mine[144 * g - 48 : 144 * g - 32] if g < 6 else top_transfer

    uppers, passing = {}, {}
    for levels in ((6, 5, 4, 3), (2, 1, 0, 0)):
        four = spread(rep3, jnp.concatenate([upper_flat(g) for g in levels], axis=0))
        for k, g in enumerate(levels):
            uppers[g] = jnp.concatenate(
                [four[128 * slot + R * k : 128 * slot + R * (k + 1)] for slot in range(3)], axis=0
            )
    for levels in ((6, 5, 4, 3), (2, 1, 1, 1)):
        four = spread(rep2, jnp.concatenate([transfer_flat(g) for g in levels], axis=0))
        four = settle(four, folds)
        for k, g in enumerate(levels):
            passing[g] = four[64 * k : 64 * (k + 1)]
    top = []
    for g in range(7):
        sources = []
        if g < 5:
            j, nodes = place >> g, GROUP >> g
            for k, offset in enumerate(source_offsets(j)):
                at = j + offset
                pick = jnp.where(at < 0, at + 3, jnp.where(at < nodes, 0, at - nodes + 3))
                sources.append(mine[144 * g + R * k : 144 * g + R * (k + 1)] + side[g, pick])
        else:
            j, nodes = group >> (g - 5), GROUPS >> (g - 5)
            for offset in source_offsets(j):
                at = j + offset
                ok = jnp.logical_and(at >= 0, at < nodes)
                sources.append(tree[jnp.where(ok, (0, 8)[g - 5] + at, 12)])
        top.append(fold(couple(sources, uppers[g])))

    down = top[6]
    for g in range(6, 0, -1):
        mats = passing[g]
        odd = jnp.broadcast_to((device >> (g - 1)) & 1, BLOCK)
        mats = jnp.where(odd == 1, mats[R:].astype(F32), mats[:R].astype(F32)).astype(BF16)
        down = top[g - 1] + times_transposed(down, four_times(mats))

    packed = pack(down).astype(F32)
    packed = jnp.where(block_of(down) < 3, packed, 0.0).astype(BF16)
    for copy in late:
        copy.wait()
    at = block_of(down)
    stores = []
    for m in range(8):
        x = parts[m] + jnp.dot(packed, passes[m], preferred_element_type=F32)
        x = x.astype(BF16).astype(F32)
        rows = jnp.concatenate([jnp.where(at == k, x, 0.0) for k in range(4)], axis=0)
        far = jnp.dot(
            rows.astype(BF16), basis[4 * m : 4 * m + 4].reshape(LANES, LANES), preferred_element_type=F32
        )
        for k in range(4):
            out[4 * m + k] = near[4 * m + k] + far[R * k : R * (k + 1)]
        stores += fetch(((out.at[pl.ds(4 * m, 4)], out_hbm.at[pl.ds(4 * m, 4)]),), sems, 7 + m)
    for copy in stores:
        copy.wait()


def down_all(groups, mine, base_upper, basis, parts, passes, near):
    return pl.pallas_call(
        down_kernel,
        in_specs=[HBM] * 7,
        out_specs=HBM,
        out_shape=jax.ShapeDtypeStruct((SPAN, *BLOCK), F32),
        scratch_shapes=[
            pltpu.VMEM((GROUPS, TOP + EDGE, LANES), BF16),
            pltpu.VMEM((5 * 144, LANES), BF16),
            pltpu.VMEM(BLOCK, BF16),
            pltpu.VMEM((13, *BLOCK), BF16),
            pltpu.VMEM((5, 5, *BLOCK), BF16),
            pltpu.VMEM((SPAN, *BLOCK), BF16),
            pltpu.VMEM((8, *BLOCK), F32),
            pltpu.VMEM((8, LANES, LANES), BF16),
            pltpu.VMEM((SPAN, *BLOCK), F32),
            pltpu.VMEM((SPAN, *BLOCK), F32),
            pltpu.SemaphoreType.DMA((15,)),
        ],
        compiler_params=kernel_params(),
        name="down_all",
    )(groups, mine, base_upper, basis, parts, passes, near)


def swapped(x, first, devices):
    lower = range(first, devices - 1, 2)
    return lax.ppermute(x, "leaf", [(i, i + 1) for i in lower] + [(i + 1, i) for i in lower])


def on_device(
    devices,
    trial_vectors,
    leaf_basis,
    near_blocks,
    near_src,
    near_count,
    couple_src,
    couple_count,
    couple_leaf,
    transfer,
    couple_upper,
):
    transfer_rows = transfer.reshape(SPAN, 2, 8, LANES).transpose(0, 2, 1, 3).reshape(SPAN, 16, LANES)
    leaf_rows = couple_leaf.reshape(SPAN, 8, 8, LANES).transpose(0, 2, 1, 3).reshape(SPAN, 64, LANES)
    upper_slots = couple_upper.transpose(1, 0, 2)

    in_row = [list(range(g * GROUP, (g + 1) * GROUP)) for g in range(GROUPS)]
    across = [list(range(g, devices, GROUP)) for g in range(GROUP)]
    exchange = functools.partial(lax.all_to_all, axis_name="leaf", split_axis=0, concat_axis=0, tiled=True)

    trial_rows = trial_vectors.reshape(SPAN * R, LANES)
    send, own, transfer_mats = local_up(trial_rows, leaf_basis, transfer_rows, upper_slots)
    got = exchange(send, axis_index_groups=in_row)
    to_chip, to_next, upper_mats, base_upper = prepare(trial_rows, own, upper_slots)
    chip_halo = swapped(to_chip, 0, devices)
    next_halo = swapped(to_next, 1, devices)
    group_send, mine = group_up(got)
    groups = exchange(group_send, axis_index_groups=across)
    parts, passes, near = middle(
        couple_src.T, couple_count, near_src.T, near_count, trial_rows, own, chip_halo, next_halo,
        leaf_rows, transfer_mats, upper_mats, near_blocks, mine,
    )
    return down_all(groups, mine, base_upper, leaf_basis, parts, passes, near)


def solution(mesh):
    placed = (
        P("leaf", None, None),
        P("leaf", None, None),
        P("leaf", None, None, None),
        P("leaf", None),
        P("leaf"),
        P("leaf", None),
        P("leaf"),
        P("leaf", None, None),
        P("leaf", None, None),
        P("leaf", None, None),
    )
    return jax.shard_map(
        functools.partial(on_device, mesh.shape["leaf"]),
        mesh=mesh,
        in_specs=placed,
        out_specs=P("leaf", None, None),
        check_vma=False,
    )
```
